256 devices in a mesh: blk: 64 (over z, x, core), grp: 4 (over y).
Axes of the slice: x: 4, y: 4, z: 8, core: 2. Of those that a mesh axis runs over, the one named last changes fastest.
Arguments:
- flow: float32 [3072, 5, 4096], P(('blk', 'grp')), may hold values from -3 to 6, as said below
- adjoint: float32 [3072, 5, 4096], P(('blk', 'grp')), may hold values from -6 to 6
- cut_flag: int32 [3072, 4096], P(('blk', 'grp')), may hold values 0 or 1
- lateral_owner: int32 [3072, 4, 1], P(('blk', 'grp')), may hold values from 0 to 63; in each aligned block of 48 rows (0 to 47, 48 to 95, ..., all dimensions but the last counted through in order) at most 2 rows name the same one
- lateral_link: int32 [3072, 4], P(('blk', 'grp')), may hold values from 0 to 59
- vertical_link: int32 [3072, 2], P(('blk', 'grp')), may hold values from 0 to 59
Outputs:
- indicator: float32 [3072, 4096], P(('blk', 'grp'))
The draws below stay inside these ranges and needn't reach their ends.
Inputs may be any that keep to these rules, and one draw needn't show every extreme that they name: `flow`: density lies between 1 and 2, pressure between 1 and 2, every velocity component between -1.25 and 1.25. `lateral_owner`: among the faces 0 to 3 of the blocks of one device, at most 2 have their neighbour on any one blk index, and in every draw some device reaches 2.
All inputs are finite; a program needn't handle non-finite values. No bound on the sum of `cut_flag` on one device may be relied on, other than what follows from the above.
Results may differ from the reference program's by a relative error of at most 0.0003.
Values sent between devices are 32-bit elements; how exact they have to be, the bound alone decides.
No kernel may reach another device: no remote copies, remote signals or barrier semaphores. Data moves between devices by JAX's collectives and lax.ppermute only.
A program may use at most 128 MiB of HBM per device.

```python
import math
import jax
import jax.numpy as jnp
import numpy as np
from jax import lax

EDGE = 16
BLK_DEV = 12
CELLS = 4096
NB = 3072
CAP = 2
N_BLK = 64
N_GRP = 4


def draw_flow(key, part):
    keys = jax.random.split(key, 9)
    grid_shape = (NB, CELLS)
    density = jnp.exp(jax.random.uniform(keys[0], grid_shape, jnp.float32, 0.0, math.log(2.0)))
    pressure = jnp.exp(jax.random.uniform(keys[1], grid_shape, jnp.float32, 0.0, math.log(2.0)))
    velocity = jnp.clip(0.25 * jax.random.normal(keys[2], (3,) + grid_shape, jnp.float32), -0.5, 0.5)
    transonic = jax.random.uniform(keys[3], (NB, 1), jnp.float32) < 0.125
    direction = jax.random.randint(keys[4], (NB, 1), 0, 3)
    heading = jnp.where(jax.random.uniform(keys[5], (NB, 1), jnp.float32) < 0.5, -1.0, 1.0)
    magnitude = jax.random.uniform(keys[6], grid_shape, jnp.float32, 0.75, 1.25)
    fast_density = jax.random.uniform(keys[7], grid_shape, jnp.float32, 1.6, 2.0)
    fast_pressure = jax.random.uniform(keys[8], grid_shape, jnp.float32, 1.0, 1.2)
    density = jnp.where(transonic, fast_density, density)
    pressure = jnp.where(transonic, fast_pressure, pressure)
    component = jnp.arange(3, dtype=jnp.int32)[:, None, None]
    picked = (component == direction[None]) & transonic[None]
    velocity = jnp.where(picked, (heading * magnitude)[None], velocity)
    energy = pressure / 0.4 + 0.5 * density * jnp.sum(velocity * velocity, axis=0)
    return jnp.stack([density, density * velocity[0], density * velocity[1], density * velocity[2], energy], axis=1)


def plant(drawn, rng, low, top_value):
    extent = drawn.shape
    spot = [jax.random.randint(jax.random.fold_in(rng, axis), (), 0, extent[axis]) for axis in range(len(extent))]
    drawn = drawn.at[tuple(spot)].set(low)
    longest = extent.index(max(extent))
    spot[longest] = (spot[longest] + 1) % extent[longest]
    return drawn.at[tuple(spot)].set(top_value)


def level_of(rng, shape, cuts, low, high):
    gain = 1.0
    for axis_at, blocks in cuts:
        steps = jax.random.uniform(jax.random.fold_in(jax.random.fold_in(rng, 6), axis_at), (blocks,), jnp.float32, low / len(cuts), high / len(cuts))
        gain = gain * jnp.repeat(jnp.exp(steps), shape[axis_at] // blocks).reshape((-1,) + (1,) * (len(shape) - 1 - axis_at))
    return gain


def assign_block(key, own, number, rows, number_of, top, reach, slope):
    order = jax.random.permutation(key, number_of)
    heavy_load, common = shares(number_of, rows * top, reach, slope, True), shares(number_of, rows * top, reach, slope, False)
    places = jnp.arange(number_of)

    def named(tallies, offset_by):
        used = int((tallies > 0).sum())
        fixed = max(1, used // 4)
        moved = fixed + (places - fixed + offset_by * (used - fixed)) % max(1, number_of - fixed)
        return jnp.zeros((number_of,), jnp.int32).at[order[jnp.where(places < fixed, places, moved)]].set(jnp.asarray(tallies, jnp.int32))

    tallies = jnp.where(number % 4 == 0, named(heavy_load, number // 4), named(common, number - number // 4 - 1))
    mixed = jax.random.permutation(jax.random.fold_in(own, 3), number_of)
    giver, sink = mixed[0:number_of // 2 * 2:2], mixed[1:number_of // 2 * 2:2]
    slack = jnp.minimum(tallies[giver] - 1, reach - tallies[sink]) // 2
    slack = jnp.where((giver == order[0]) | (sink == order[0]) | (tallies[sink] == 0), 0, jnp.maximum(slack, 0))
    moved = jax.random.randint(jax.random.fold_in(own, 4), (number_of // 2,), 0, 1 << 20) % (slack + 1)
    tallies = tallies.at[giver].add(-moved).at[sink].add(moved)
    labels = jnp.searchsorted(jnp.cumsum(tallies), jnp.arange(rows * top), side="right").astype(jnp.int32)
    table = labels.reshape(top, rows).T
    table = table[jax.random.permutation(jax.random.fold_in(own, 1), rows)]
    offset_by = jax.random.randint(jax.random.fold_in(own, 2), (rows, 1), 0, top)
    return jnp.take_along_axis(table, (jnp.arange(top)[None, :] + offset_by) % top, axis=1)


def shares(count, total, limit, lean, full):
    weights = [(1 << 20) // math.isqrt(standing ** lean) + 1 for standing in range(1, count + 1)]
    largest = limit if full else min(limit, max(-(-total // count), total * weights[0] // sum(weights)))
    least = 1 if total - largest >= count - 1 else 0
    holding, rest = [largest] + [least] * (count - 1), total - largest - least * (count - 1)
    while rest > 0:
        movable = [i for i in range(1, count) if holding[i] < largest] or [i for i in range(1, count) if holding[i] < limit]
        whole, budget = sum([weights[i] for i in movable]), rest
        for i in movable:
            addition = min(limit - holding[i], max(1, budget * weights[i] // whole), rest)
            holding[i] = holding[i] + addition
            rest = rest - addition
    return np.array(holding)


def centred(rng, dims, scale, bound, shards=(), held_as=jnp.bfloat16):
    loudness = level_of(rng, dims, shards, -0.22, 0.18) if shards else 1.0
    values = jax.random.normal(rng, dims, jnp.float32) * scale * loudness
    return jnp.minimum(jnp.maximum(values, -bound), bound).astype(held_as)


def setup_inputs(seed: int = 0) -> dict:
    splits = jax.random.split(jax.random.key(seed), 7)
    flow = draw_flow(jax.random.fold_in(splits[6], 71), 0)
    adjoint = centred(splits[1], (NB, 5, CELLS), 1.0, 6.0, ((0, 256),), jnp.float32)
    cut_flag = plant((jax.random.randint(splits[2], (NB, CELLS), 0, 8) < 1).astype(jnp.int32), jax.random.fold_in(splits[2], 1), 0, 1)
    lateral_owner_keys = jax.random.split(jax.random.fold_in(splits[3], 1), NB * 4 // (4 * BLK_DEV))
    lateral_owner_turns = jax.random.permutation(jax.random.fold_in(splits[3], 3), NB * 4 // (4 * BLK_DEV))
    lateral_owner = jax.vmap(lambda own, number: assign_block(jax.random.fold_in(splits[3], 2), own, number, 4 * BLK_DEV, N_BLK, 1, CAP, 2))(lateral_owner_keys, lateral_owner_turns).reshape((NB, 4, 1))
    lateral_link = plant(jax.random.randint(splits[4], (NB, 4), 0, 5 * BLK_DEV), jax.random.fold_in(splits[4], 1), 0, (5 * BLK_DEV) - 1).astype(jnp.int32)
    vertical_link = plant(jax.random.randint(splits[5], (NB, 2), 0, 5 * BLK_DEV), jax.random.fold_in(splits[5], 1), 0, (5 * BLK_DEV) - 1).astype(jnp.int32)
    return {"flow": flow, "adjoint": adjoint, "cut_flag": cut_flag, "lateral_owner": lateral_owner, "lateral_link": lateral_link, "vertical_link": vertical_link}


HEAT_RATIO = 1.4
ENTROPY_FIX = 0.2
FREESTREAM = (1.0, 0.0, 0.0, 0.3, 1.0)

def primitive(conserved):
    density = conserved[:, 0]
    velocity = conserved[:, 1:4] / density[:, None]
    pressure = (HEAT_RATIO - 1.0) * (conserved[:, 4] - 0.5 * density * lax.optimization_barrier(jnp.sum(velocity * velocity, axis=1)))
    return jnp.concatenate([density[:, None], velocity, pressure[:, None]], axis=1)

def minmod(first_diff, second_diff):
    return jnp.where(first_diff * second_diff > 0.0, jnp.sign(first_diff) * jnp.minimum(jnp.abs(first_diff), jnp.abs(second_diff)), 0.0)

def harten(wave_rate, spread):
    return jnp.where(wave_rate < spread, (wave_rate * wave_rate + spread * spread) / (2.0 * spread), wave_rate)

def roe_flux(left_state, right_state, normal_axis):
    left_rho = left_state[0]
    right_rho = right_state[0]
    left_vel = left_state[1:4]
    right_vel = right_state[1:4]
    left_press = left_state[4]
    right_press = right_state[4]
    factor = HEAT_RATIO / (HEAT_RATIO - 1.0)
    left_enth = factor * left_press / left_rho + 0.5 * lax.optimization_barrier(jnp.sum(left_vel * left_vel, axis=0))
    right_enth = factor * right_press / right_rho + 0.5 * lax.optimization_barrier(jnp.sum(right_vel * right_vel, axis=0))
    left_root = jnp.sqrt(left_rho)
    right_root = jnp.sqrt(right_rho)
    weight_sum = left_root + right_root
    mean_vel = (left_root * left_vel + right_root * right_vel) / weight_sum
    mean_enth = (left_root * left_enth + right_root * right_enth) / weight_sum
    speed_sq = lax.optimization_barrier(jnp.sum(mean_vel * mean_vel, axis=0))
    sound_sq = (HEAT_RATIO - 1.0) * (mean_enth - 0.5 * speed_sq)
    sound_speed = jnp.sqrt(sound_sq)
    mean_rho = left_root * right_root
    normal = mean_vel[normal_axis]
    jump_vel = right_vel - left_vel
    jump_rho = right_rho - left_rho
    jump_press = right_press - left_press
    jump_normal = jump_vel[normal_axis]
    wave_slow = (jump_press - mean_rho * sound_speed * jump_normal) / (2.0 * sound_sq)
    wave_fast = (jump_press + mean_rho * sound_speed * jump_normal) / (2.0 * sound_sq)
    wave_entropy = jump_rho - jump_press / sound_sq
    spread = ENTROPY_FIX * sound_speed
    slow_part = harten(jnp.abs(normal - sound_speed), spread) * wave_slow
    fast_part = harten(jnp.abs(normal + sound_speed), spread) * wave_fast
    mid_part = jnp.abs(normal) * wave_entropy
    shear_part = jnp.abs(normal) * mean_rho
    unit_vector = [1.0 if axis_no == normal_axis else 0.0 for axis_no in range(3)]
    shear_jump = [jump_vel[axis_no] - jump_normal * unit_vector[axis_no] for axis_no in range(3)]
    diss_mass = slow_part + fast_part + mid_part
    diss_mom = [slow_part * (mean_vel[axis_no] - sound_speed * unit_vector[axis_no]) + fast_part * (mean_vel[axis_no] + sound_speed * unit_vector[axis_no]) + mid_part * mean_vel[axis_no] + shear_part * shear_jump[axis_no] for axis_no in range(3)]
    diss_energy = slow_part * (mean_enth - normal * sound_speed) + fast_part * (mean_enth + normal * sound_speed) + mid_part * 0.5 * speed_sq + shear_part * (mean_vel[0] * shear_jump[0] + mean_vel[1] * shear_jump[1] + mean_vel[2] * shear_jump[2])
    left_normal = left_vel[normal_axis]
    right_normal = right_vel[normal_axis]
    mass_flux = 0.5 * (left_rho * left_normal + right_rho * right_normal) - 0.5 * diss_mass
    momentum = [0.5 * (left_rho * left_normal * left_vel[axis_no] + right_rho * right_normal * right_vel[axis_no] + (left_press + right_press) * unit_vector[axis_no]) - 0.5 * diss_mom[axis_no] for axis_no in range(3)]
    energy = 0.5 * (left_rho * left_normal * left_enth + right_rho * right_normal * right_enth) - 0.5 * diss_energy
    return jnp.stack([mass_flux] + momentum + [energy], axis=0)

def wall_flux(pressure, normal_axis):
    nothing = jnp.zeros_like(pressure)
    parts = [pressure if axis_no == normal_axis else nothing for axis_no in range(3)]
    return jnp.stack([nothing] + parts + [nothing], axis=0)

def face_flux(left_state, right_state, left_solid, right_solid, normal_axis):
    roe_value = roe_flux(left_state, right_state, normal_axis)
    from_left = (right_solid > 0.5) & (left_solid < 0.5)
    from_right = (left_solid > 0.5) & (right_solid < 0.5)
    return jnp.where(from_left, wall_flux(left_state[4], normal_axis), jnp.where(from_right, wall_flux(right_state[4], normal_axis), roe_value))

def faces_of(coarse_cube):
    face_shape = (coarse_cube.shape[0], coarse_cube.shape[1], EDGE * EDGE)
    return jnp.stack([coarse_cube[:, :, 0].reshape(face_shape), coarse_cube[:, :, -1].reshape(face_shape), coarse_cube[:, :, :, 0].reshape(face_shape), coarse_cube[:, :, :, -1].reshape(face_shape), coarse_cube[:, :, :, :, 0].reshape(face_shape), coarse_cube[:, :, :, :, -1].reshape(face_shape)], axis=1)

def select_face(face_slab, level_code):
    channels = face_slab.shape[0]
    half_edge = EDGE // 2
    square = face_slab.reshape(channels, EDGE, EDGE)
    quarter_code = jnp.minimum(level_code, 3)
    anchor = jnp.zeros((), jnp.int32)
    first_start = (quarter_code // 2 * half_edge).astype(jnp.int32)
    second_start = (quarter_code % 2 * half_edge).astype(jnp.int32)
    quarter = lax.dynamic_slice(square, (anchor, first_start, second_start), (channels, half_edge, half_edge))
    widened = jnp.broadcast_to(quarter[:, :, None, :, None], (channels, half_edge, 2, half_edge, 2))
    return jnp.where(level_code == 4, face_slab, widened.reshape(channels, EDGE * EDGE))

def prolong(coarse_cube, ghosts):
    channels = coarse_cube.shape[0]
    edge_cells = coarse_cube.shape[1]
    slopes = []
    for axis_no in range(3):
        dim_no = axis_no + 1
        lower_side = jnp.concatenate([jnp.expand_dims(ghosts[2 * axis_no], dim_no), lax.slice_in_dim(coarse_cube, 0, edge_cells - 1, axis=dim_no)], axis=dim_no)
        upper_side = jnp.concatenate([lax.slice_in_dim(coarse_cube, 1, edge_cells, axis=dim_no), jnp.expand_dims(ghosts[2 * axis_no + 1], dim_no)], axis=dim_no)
        slopes.append(minmod(upper_side - coarse_cube, coarse_cube - lower_side))
    split_shape = (channels, edge_cells, 1, edge_cells, 1, edge_cells, 1)
    child_signs = jnp.array([-0.25, 0.25], jnp.float32)
    fine_field = coarse_cube.reshape(split_shape) + slopes[0].reshape(split_shape) * child_signs[:, None, None, None, None] + slopes[1].reshape(split_shape) * child_signs[:, None, None] + slopes[2].reshape(split_shape) * child_signs
    return fine_field.reshape(channels, 2 * edge_cells, 2 * edge_cells, 2 * edge_cells)

def residual(fine_field, fine_ghosts, solid_mask):
    size_fine = fine_field.shape[1]
    summed = jnp.zeros_like(fine_field)
    for axis_no in range(3):
        dim_no = axis_no + 1
        left_state = jnp.concatenate([jnp.expand_dims(fine_ghosts[2 * axis_no], dim_no), fine_field], axis=dim_no)
        right_state = jnp.concatenate([fine_field, jnp.expand_dims(fine_ghosts[2 * axis_no + 1], dim_no)], axis=dim_no)
        open_rim = jnp.expand_dims(jnp.zeros((size_fine, size_fine), jnp.float32), axis_no)
        left_solid = jnp.concatenate([open_rim, solid_mask], axis=axis_no)
        right_solid = jnp.concatenate([solid_mask, open_rim], axis=axis_no)
        flux_all = face_flux(left_state, right_state, left_solid, right_solid, axis_no)
        summed = summed + lax.slice_in_dim(flux_all, 1, size_fine + 1, axis=dim_no) - lax.slice_in_dim(flux_all, 0, size_fine, axis=dim_no)
    return jnp.where(solid_mask[None] > 0.5, 0.0, summed)

def block_indicator(operands):
    flow_prim, adjoint_block, ghosts, flags = operands
    coarse_flow = flow_prim.reshape(5, EDGE, EDGE, EDGE)
    coarse_adjoint = adjoint_block.reshape(5, EDGE, EDGE, EDGE)
    face_ghosts = ghosts.reshape(6, 10, EDGE, EDGE)
    fine_flow = prolong(coarse_flow, face_ghosts[:, :5])
    fine_adjoint = prolong(coarse_adjoint, face_ghosts[:, 5:])
    wide_ghosts = jnp.broadcast_to(face_ghosts[:, :5, :, None, :, None], (6, 5, EDGE, 2, EDGE, 2)).reshape(6, 5, 2 * EDGE, 2 * EDGE)
    solid_mask = jnp.broadcast_to(flags.astype(jnp.float32).reshape(EDGE, 1, EDGE, 1, EDGE, 1), (EDGE, 2, EDGE, 2, EDGE, 2)).reshape(2 * EDGE, 2 * EDGE, 2 * EDGE)
    fine_residual = residual(fine_flow, wide_ghosts, solid_mask)
    weighted = lax.optimization_barrier(jnp.sum(fine_adjoint * fine_residual, axis=0))
    coarse = weighted.reshape(EDGE, 2, EDGE, 2, EDGE, 2).sum(axis=(1, 3, 5))
    return jnp.abs(coarse).reshape(EDGE * EDGE * EDGE)

def reference(flow, adjoint, cut_flag, lateral_owner, lateral_link, vertical_link):
    number_blocks = flow.shape[0]
    primitives = primitive(flow)
    coarse_both = jnp.concatenate([primitives, adjoint], axis=1).reshape(number_blocks, 10, EDGE, EDGE, EDGE)
    face_all = faces_of(coarse_both)
    block_ids = jnp.arange(number_blocks, dtype=jnp.int32)
    device_ids = block_ids // BLK_DEV
    region = device_ids % N_GRP
    column = device_ids // N_GRP
    lateral_block = (lateral_owner[:, :, 0] * N_GRP + region[:, None]) * BLK_DEV + lateral_link // 5
    opposite = jnp.array([1, 0, 3, 2], jnp.int32)
    lateral_slab = face_all[lateral_block, opposite[None, :]]
    lateral_ghost = jax.vmap(jax.vmap(select_face))(lateral_slab, lateral_link % 5)
    lower_region = jnp.maximum(region - 1, 0)
    upper_region = jnp.minimum(region + 1, N_GRP - 1)
    lower_block = (column * N_GRP + lower_region) * BLK_DEV + vertical_link[:, 0] // 5
    upper_block = (column * N_GRP + upper_region) * BLK_DEV + vertical_link[:, 1] // 5
    lower_ghost = jax.vmap(select_face)(face_all[lower_block, 5], vertical_link[:, 0] % 5)
    upper_ghost = jax.vmap(select_face)(face_all[upper_block, 4], vertical_link[:, 1] % 5)
    state = jnp.array(FREESTREAM, jnp.float32)
    farfield_layer = jnp.concatenate([jnp.broadcast_to(state[:, None], (5, EDGE * EDGE)), jnp.zeros((5, EDGE * EDGE), jnp.float32)], axis=0)
    lower_ghost = jnp.where((region == 0)[:, None, None], farfield_layer, lower_ghost)
    upper_ghost = jnp.where((region == N_GRP - 1)[:, None, None], farfield_layer, upper_ghost)
    ghosts = jnp.concatenate([lateral_ghost, lower_ghost[:, None], upper_ghost[:, None]], axis=1)
    return lax.map(block_indicator, (primitives, adjoint, ghosts, cut_flag))
```

```python
import math

import jax
import jax.numpy as jnp
from jax import lax
from jax.experimental import pallas as pl
from jax.experimental.pallas import tpu as pltpu
from jax.sharding import PartitionSpec as P

EDGE = 16
NB = 12
PL = 2 * NB
ROWS = EDGE * PL
LANES = 128
PEERS = 64
FACES = 4 * PL
PXR = (EDGE + 2) * PL
MR = (EDGE + 1) * PL

VEL = math.sqrt(0.2)
PRESS = 0.2
WEIGHTS = (1.0 / VEL, 5.0, 5.0, 5.0, 2.5 / VEL)
FARFIELD = (1.0, 0.0, 0.0, 0.3 * VEL, PRESS)
KNEE = 0.4 / math.sqrt(5.0)
START = 1.2 / math.sqrt(5.0)
CURVE = 1.25 * math.sqrt(5.0)

VMEM_LIMIT = 56 * 2**20


def lane():
    return lax.broadcasted_iota(jnp.int32, (8, LANES), 1)


def even_row():
    return lax.broadcasted_iota(jnp.int32, (8, LANES), 0) % 2 == 0


def rolled(x, amount, axis=1):
    size = x.shape[axis]
    amount = amount % size
    return x if amount == 0 else pltpu.roll(x, amount, axis)


def rows8(start):
    if isinstance(start, int):
        return pl.ds(start, 8)
    return pl.ds(pl.multiple_of(start, 8), 8)


def compact_j(load, side):
    low = lane() // EDGE
    halves = []
    for ih in range(2):
        total = None
        for il in range(8):
            x = rolled(load(ih * 8 + il), 16 * il if side == 0 else 16 * il + 16)
            total = x if total is None else jnp.where(low == il, x, total)
        halves.append(total)
    if side == 0:
        return jnp.where(even_row(), halves[0], rolled(halves[1], 1, 0))
    return jnp.where(even_row(), rolled(halves[0], -1, 0), halves[1])


def compact_k(load, side):
    depth = lane() % EDGE
    total = None
    for i in range(EDGE):
        x = rolled(load(i), i if side == 0 else i - 15)
        total = x if total is None else jnp.where(depth == i, x, total)
    return total


def spread_j(low, high, i):
    ih, il = i // 8, i % 8
    a = low if ih == 0 else rolled(low, -1, 0)
    c = rolled(high, 1, 0) if ih == 0 else high
    return jnp.where(even_row(), rolled(a, -16 * il), rolled(c, 16 * (7 - il)))


def spread_k(low, high, i):
    return jnp.where(lane() % EDGE == 0, rolled(low, -i), rolled(high, 15 - i))


def column_of(packed, rows, width):
    at = lax.broadcasted_iota(jnp.int32, (rows, width), 0) // 2
    spot = lax.broadcasted_iota(jnp.int32, (rows, width), 1)
    return jnp.sum(jnp.where(at == spot, packed, 0.0), axis=1, keepdims=True)


def index_tables(own, vertical, index_ref):
    spots = lax.broadcasted_iota(jnp.int32, (PL, LANES), 1)
    half = lax.broadcasted_iota(jnp.int32, (PL, LANES), 0) % 2
    low, depth = spots // EDGE, spots % EDGE
    wide = (4 * half + low // 2) * EDGE + depth // 2

    def store(f, code, row_part, col_part, base, step):
        full = code == 4
        index_ref[pl.ds(f * PL, PL), :] = jnp.where(full, spots, wide + 8 * col_part)
        index_ref[pl.ds(144 + f * PL, PL), :] = base + step * jnp.where(full, half, row_part)

    at = lax.broadcasted_iota(jnp.int32, (PL, NB), 0) // 2
    spot = lax.broadcasted_iota(jnp.int32, (PL, NB), 1)
    entries = [own[f : f + 1, :].astype(jnp.int32) for f in range(4)]
    holders = [e >> 9 for e in entries]
    for f in range(4):
        value = column_of(own[f : f + 1, :], PL, NB).astype(jnp.int32)
        owner, code = value >> 9, value & 7
        rank = jnp.zeros((PL, 1), jnp.float32)
        for other in range(f + 1):
            same = holders[other] == owner
            if other == f:
                same = same & (spot < at)
            rank = rank + jnp.sum(jnp.where(same, 1.0, 0.0), axis=1, keepdims=True)
        rank = rank.astype(jnp.int32)
        store(f, code, code >> 1, code & 1, rank * 2 * PEERS + owner, PEERS)
    for side in range(2):
        value = column_of(vertical[side : side + 1, :], PL, NB).astype(jnp.int32)
        slot, code = value >> 3, value & 7
        store(4 + side, code, code & 1, code >> 1, slot * 2, 1)


def prep_kernel(
    flow_ref, adj_ref, flag_ref, own_ref, vertical_ref,
    prim_ref, adjl_ref, solid_ref, lat_ref, low_ref, high_ref, index_ref,
):
    def relaid(ref, c, out_ref):
        for t in range(2 * EDGE):
            i, jh = divmod(t, 2)
            part = ref[c, :, pl.ds(t * LANES, LANES)]
            out_ref[pl.ds(i * PL + jh + c * ROWS, NB, stride=2), :] = part.astype(jnp.float32)

    for c in range(5):
        relaid(flow_ref, c, prim_ref)
        relaid(adj_ref, c, adjl_ref)
    relaid(flag_ref, 0, solid_ref)
    index_tables(
        own_ref[...].astype(jnp.float32), vertical_ref[...].astype(jnp.float32), index_ref
    )

    def convert(n, _):
        at = [rows8(c * ROWS + n * 8) for c in range(5)]
        rho = prim_ref[at[0]]
        inv = 1.0 / rho
        vel = [prim_ref[at[c]] * inv for c in (1, 2, 3)]
        square = vel[0] * vel[0] + vel[1] * vel[1] + vel[2] * vel[2]
        prim_ref[at[4]] = (0.4 * PRESS) * (prim_ref[at[4]] - 0.5 * rho * square)
        for c in range(3):
            prim_ref[at[c + 1]] = vel[c] * VEL
        return 0

    lax.fori_loop(0, ROWS // 8, convert, 0)

    def layers(ref, first):
        def one(n, _):
            c, g = n // 3, n % 3

            def load(i):
                return ref[rows8(c * ROWS + i * PL + g * 8), :]

            out = (c + first) * FACES + g * 8
            lat_ref[rows8(out), :] = load(0)
            lat_ref[rows8(out + PL), :] = load(EDGE - 1)
            lat_ref[rows8(out + 2 * PL), :] = compact_j(load, 0)
            lat_ref[rows8(out + 3 * PL), :] = compact_j(load, 1)
            low_ref[rows8((c + first) * PL + g * 8), :] = compact_k(load, 0)
            high_ref[rows8((c + first) * PL + g * 8), :] = compact_k(load, 1)
            return 0

        lax.fori_loop(0, 15, one, 0)

    layers(prim_ref, 0)
    layers(adjl_ref, 5)


def reply_kernel(me_ref, asked_ref, lat_ref, first_ref, second_ref):
    before = lax.broadcasted_iota(jnp.int32, (NB, NB), 0) < lax.broadcasted_iota(
        jnp.int32, (NB, NB), 1
    )
    before = jnp.where(before, 1.0, 0.0)
    earlier = jnp.zeros((PEERS, 1), jnp.float32)
    entries = []
    for f in range(4):
        asked = asked_ref[:, f, :]
        match = (asked >> 9) == me_ref[0]
        hits = jnp.where(match, 1.0, 0.0)
        rank = jnp.dot(hits, before, preferred_element_type=jnp.float32) + earlier
        earlier = earlier + jnp.sum(hits, axis=1, keepdims=True)
        face = (asked >> 3) & 63
        target = (((face & 3) * PL) + ((face >> 2) * 2)).astype(jnp.float32) + 10.0
        entries.append((match, rank, target))
    column = lax.broadcasted_iota(jnp.int32, (PEERS, FACES), 1).astype(jnp.float32)
    picks = []
    for s in range(2):
        row = jnp.full((PEERS, 1), -10.0, jnp.float32)
        for match, rank, target in entries:
            mine = match & (rank > s - 0.5) & (rank < s + 0.5)
            row = row + jnp.sum(jnp.where(mine, target, 0.0), axis=1, keepdims=True)
        for h in range(2):
            picks.append(jnp.where(column == row + float(h), 1.0, 0.0))
    picks = jnp.concatenate(picks, axis=0)
    for c in range(10):
        out = jnp.dot(
            picks,
            lat_ref[pl.ds(c * FACES, FACES), :],
            precision=lax.Precision.HIGHEST,
            preferred_element_type=jnp.float32,
        )
        ref, at, stride = (first_ref, c * 4, 24) if c < 6 else (second_ref, (c - 6) * 4, 16)
        for q in range(4):
            ref[pl.ds(at + q, PEERS, stride=stride), :] = out[q * PEERS : (q + 1) * PEERS]


def one_hot(columns, width):
    parts = []
    for start in range(0, width, LANES):
        parts.append(
            jnp.where(
                columns == lax.broadcasted_iota(jnp.int32, columns.shape, 1) + start, 1.0, 0.0
            )
        )
    return parts[0] if len(parts) == 1 else jnp.concatenate(parts, axis=1)


def widened(x, index):
    parts = [
        jnp.take_along_axis(
            x[n : n + 8], index[n : n + 8], axis=1, mode="promise_in_bounds"
        )
        for n in range(0, x.shape[0], 8)
    ]
    return jnp.concatenate(parts, axis=0)


def ghost_planes(edge_ref, index_ref, received, around, far, g_ref):
    lateral = one_hot(index_ref[pl.ds(144, FACES), :], 4 * PEERS)
    vertical = [one_hot(index_ref[pl.ds(240 + s * PL, PL), :], LANES)[:, :PL] for s in range(2)]
    for c in range(5):
        x = jnp.concatenate([received(c, q) for q in range(4)], axis=0)
        y = jnp.dot(
            lateral, x, precision=lax.Precision.HIGHEST, preferred_element_type=jnp.float32
        )
        g_ref[pl.ds(c * 144, FACES), :] = widened(y, index_ref[pl.ds(0, FACES), :])
        for s in range(2):
            y = jnp.dot(
                vertical[s],
                around(s, c),
                precision=lax.Precision.HIGHEST,
                preferred_element_type=jnp.float32,
            )
            y = widened(y, index_ref[pl.ds(FACES + s * PL, PL), :])
            g_ref[pl.ds(c * 144 + FACES + s * PL, PL), :] = jnp.where(
                edge_ref[s] == 1, jnp.full_like(y, far[c]), y
            )


def spread_ghosts(g_ref, gj_ref, gk_ref):
    def one(n, _):
        c, g = n // 3, n % 3
        faces = [g_ref[rows8(c * 144 + f * PL + g * 8), :] for f in range(2, 6)]
        for i in range(EDGE):
            at = rows8(c * ROWS + i * PL + g * 8)
            gj_ref[at, :] = spread_j(faces[0], faces[1], i)
            gk_ref[at, :] = spread_k(faces[2], faces[3], i)
        return 0

    lax.fori_loop(0, 15, one, 0)


def minmod(a, c):
    return jnp.maximum(jnp.minimum(a, jnp.maximum(c, 0.0)), jnp.minimum(c, 0.0))


def masks():
    low, depth, even = lane() // EDGE, lane() % EDGE, even_row()
    return dict(
        k_last=depth == EDGE - 1,
        k_first=depth == 0,
        j_wrap=low == 7,
        j_back=low == 0,
        j_last=(low == 7) & ~even,
        j_first=(low == 0) & even,
    )


def next_k(x):
    return rolled(x, -1)


def last_k(x):
    return rolled(x, 1)


def next_j(x, m):
    r = rolled(x, -16)
    return jnp.where(m["j_wrap"], rolled(r, -1, 0), r)


def last_j(x, m):
    r = rolled(x, 16)
    return jnp.where(m["j_back"], rolled(r, 1, 0), r)


def slopes_of(below, x, above, gj, gk, m):
    x4 = 0.25 * x
    out = [minmod(0.25 * above - x4, x4 - 0.25 * below)]
    up = jnp.where(m["j_last"], gj, next_j(x, m))
    down = jnp.where(m["j_first"], gj, last_j(x, m))
    out.append(minmod(0.25 * up - x4, x4 - 0.25 * down))
    up = jnp.where(m["k_last"], gk, next_k(x))
    down = jnp.where(m["k_first"], gk, last_k(x))
    out.append(minmod(0.25 * up - x4, x4 - 0.25 * down))
    return out


def state(q):
    rho, u, v, w, p = q
    rs = lax.rsqrt(rho)
    enth = 7.0 * p * (rs * rs) + (u * u + v * v + w * w)
    return (rho, u, v, w, p, rho * rs, enth)


def four(base, first, second):
    out = []
    for a in (-1, 1):
        half = [x + s if a > 0 else x - s for x, s in zip(base, first)]
        for e in (-1, 1):
            out.append(state([x + s if e > 0 else x - s for x, s in zip(half, second)]))
    return out


def roe(left, right, axis):
    n = 1 + axis
    weight = right[5] * pl.reciprocal(left[5] + right[5], approx=True)
    jump = right[n] - left[n]
    mean = [None] * 4
    for c in (1, 2, 3):
        d = jump if c == n else right[c] - left[c]
        mean[c] = left[c] + weight * d
    enth = left[6] + weight * (right[6] - left[6])
    c2 = enth - (mean[1] * mean[1] + mean[2] * mean[2] + mean[3] * mean[3])
    rc = lax.rsqrt(c2)
    un = mean[n]
    ahead = un > 0.0
    sign = jnp.where(ahead, VEL, -VEL)
    b = jnp.maximum(START - jnp.abs(un) * rc, 0.0)
    s = jnp.minimum(b, KNEE)
    speed = 2.5 * b - s * (2.5 - (2.5 * CURVE) * s)
    wave = speed * ((right[4] - left[4]) * rc - sign * (left[5] * right[5] * jump))
    sc = sign * (c2 * rc)
    up = [jnp.where(ahead, left[c], right[c]) for c in (0, 1, 2, 3, 4, 6)]
    mass = up[0] * up[n]
    t = un * sc
    flux = [mass - wave]
    for c in (1, 2, 3):
        if c == n:
            flux.append((mass * up[c] + up[4]) - wave * (mean[c] - sc))
        else:
            flux.append(mass * up[c] - wave * mean[c])
    flux.append(mass * up[5] - wave * (enth - t - t))
    return flux


def face_sums(lefts, rights, axis):
    f = [roe(a, c, axis) for a, c in zip(lefts, rights)]
    plain, first, second = [], [], []
    for c in range(5):
        lo, hi = f[0][c] + f[1][c], f[2][c] + f[3][c]
        dlo, dhi = f[1][c] - f[0][c], f[3][c] - f[2][c]
        plain.append(lo + hi)
        first.append(hi - lo)
        second.append(dlo + dhi)
    return plain, first, second


def plain_sum(lefts, rights, axis):
    f = [roe(a, c, axis) for a, c in zip(lefts, rights)]
    return [(f[0][c] + f[1][c]) + (f[2][c] + f[3][c]) for c in range(5)]


def walled(sums, axis, solid_a, solid_b, wall_a, wall_b):
    from_a = (solid_b > 0.5) & (solid_a < 0.5)
    from_b = (solid_a > 0.5) & (solid_b < 0.5)
    any_wall = from_a | from_b
    out = []
    for part, pa, pb in zip(sums, wall_a, wall_b):
        new = []
        for c in range(5):
            if c == axis + 1:
                new.append(jnp.where(from_a, pa, jnp.where(from_b, pb, part[c])))
            else:
                new.append(jnp.where(any_wall, 0.0, part[c]))
        out.append(new)
    return out


def wall_sums(p, normal, first, second):
    return (4.0 * (p + normal), 4.0 * first, 4.0 * second)


TANGENTS = ((1, 2), (0, 2), (0, 1))


def flux_kernel(
    edge_ref, index_ref, prim_ref, solid_ref, got_ref, low_ref, high_ref, out_ref,
    g_ref, px_ref, s_ref, gj_ref, gk_ref, cb_ref, cf_ref, ej_ref, ek_ref, pv_ref,
):
    ghost_planes(
        edge_ref,
        index_ref,
        lambda c, q: got_ref[pl.ds(c * 4 + q, PEERS, stride=24), :],
        lambda s, c: (low_ref, high_ref)[s][pl.ds(c * PL, PL), :],
        FARFIELD,
        g_ref,
    )
    for c in range(5):
        px_ref[pl.ds(c * PXR, PL), :] = g_ref[pl.ds(c * 144, PL), :]
        px_ref[pl.ds(c * PXR + PL, ROWS), :] = prim_ref[pl.ds(c * ROWS, ROWS), :]
        px_ref[pl.ds(c * PXR + PL + ROWS, PL), :] = g_ref[pl.ds(c * 144 + PL, PL), :]
    spread_ghosts(g_ref, gj_ref, gk_ref)
    m = masks()

    def slopes(n, _):
        for c in range(5):
            at = c * PXR + PL + n * 8
            out = slopes_of(
                px_ref[rows8(at - PL), :],
                px_ref[rows8(at), :],
                px_ref[rows8(at + PL), :],
                gj_ref[rows8(c * ROWS + n * 8), :],
                gk_ref[rows8(c * ROWS + n * 8), :],
                m,
            )
            for d in range(3):
                s_ref[rows8((d * 5 + c) * ROWS + n * 8), :] = out[d]
        return 0

    lax.fori_loop(0, ROWS // 8, slopes, 0)

    def pack(n, _):
        c, g = n // 3, n % 3

        def value(i):
            return px_ref[rows8(c * PXR + PL + i * PL + g * 8), :]

        def slope(d, i):
            return s_ref[rows8((d * 5 + c) * ROWS + i * PL + g * 8), :]

        for way, compact in ((0, compact_j), (1, compact_k)):
            d = way + 1
            for side in range(2):
                parts = [
                    lambda i: value(i) - slope(d, i) if side == 0 else value(i) + slope(d, i)
                ] + [lambda i, t=t: slope(t, i) for t in TANGENTS[d]]
                for q in range(3):
                    cb_ref[rows8((((way * 2 + side) * 3 + q) * 5 + c) * PL + g * 8), :] = compact(
                        parts[q], side
                    )
        return 0

    lax.fori_loop(0, 15, pack, 0)

    def rim(g, _):
        for way in range(2):
            for side in range(2):
                at = (way * 2 + side) * 15
                quantities = [
                    [cb_ref[rows8((at + q * 5 + c) * PL + g * 8), :] for c in range(5)]
                    for q in range(3)
                ]
                own = four(*quantities)
                beyond = state(
                    [g_ref[rows8(c * 144 + (2 + way * 2 + side) * PL + g * 8), :] for c in range(5)]
                )
                outer = [beyond] * 4
                sums = face_sums(*((outer, own) if side == 0 else (own, outer)), way + 1)
                for q in range(3):
                    for c in range(5):
                        cf_ref[rows8((at + q * 5 + c) * PL + g * 8), :] = sums[q][c]
        return 0

    lax.fori_loop(0, 3, rim, 0)

    def unpack(n, _):
        q, g = n // 3, n % 3
        j0, j1, k0, k1 = (cf_ref[rows8((f * 15 + q) * PL + g * 8), :] for f in range(4))
        for i in range(EDGE):
            at = rows8(q * ROWS + i * PL + g * 8)
            ej_ref[at, :] = spread_j(j0, j1, i)
            ek_ref[at, :] = spread_k(k0, k1, i)
        return 0

    lax.fori_loop(0, 45, unpack, 0)

    def put_back(sums, row):
        for c in range(5):
            for moment, part in ((0, 0), (1, 0), (2, 1), (3, 2)):
                at = rows8((moment * 5 + c) * MR + row)
                out_ref[at, :] = out_ref[at, :] + sums[part][c]

    def column(g, _):
        g8 = g * 8
        below = state([g_ref[rows8(c * 144 + g8), :] for c in range(5)])
        for n in range(4):
            for q in range(7):
                pv_ref[pl.ds((n * 7 + q) * 8, 8), :] = below[q]
        for q in range(20):
            out_ref[rows8(q * MR + g8), :] = jnp.zeros((8, LANES), jnp.float32)

        def plane(i, _):
            row = i * PL + g8
            x = [px_ref[rows8(c * PXR + PL + row), :] for c in range(5)]
            s = [[s_ref[rows8((d * 5 + c) * ROWS + row), :] for c in range(5)] for d in range(3)]
            solid = solid_ref[rows8(row), :]
            child = [
                four([a + b if up else a - b for a, b in zip(x, s[0])], s[1], s[2])
                for up in (False, True)
            ]
            lower = [
                child[0],
                [child[0][0], child[0][1], child[1][0], child[1][1]],
                [child[0][0], child[0][2], child[1][0], child[1][2]],
            ]
            upper = [
                child[1],
                [child[0][2], child[0][3], child[1][2], child[1][3]],
                [child[0][1], child[0][3], child[1][1], child[1][3]],
            ]
            moments = [[None] * 5 for _ in range(4)]

            def add(k, c, value, sign):
                old = moments[k][c]
                if old is None:
                    moments[k][c] = value if sign > 0 else -value
                else:
                    moments[k][c] = old + value if sign > 0 else old - value

            for d in range(3):
                inner = plain_sum(lower[d], upper[d], d)
                for c in range(5):
                    add(d + 1, c, inner[c] + inner[c], -1)

            before = [
                tuple(pv_ref[pl.ds((n * 7 + q) * 8, 8), :] for q in range(7)) for n in range(4)
            ]
            prior = jnp.maximum(row - PL, g8)
            wall_a = wall_sums(
                px_ref[rows8(4 * PXR + PL + prior), :],
                *(s_ref[rows8((d * 5 + 4) * ROWS + prior), :] for d in range(3)),
            )
            wall_b = wall_sums(x[4], -s[0][4], s[1][4], s[2][4])
            sums = face_sums(before, child[0], 0)
            sums = walled(sums, 0, solid_ref[rows8(prior), :], solid, wall_a, wall_b)
            put_back(sums, row)
            for c in range(5):
                add(0, c, sums[0][c], -1)
                add(1, c, sums[0][c], 1)
                add(2, c, sums[1][c], -1)
                add(3, c, sums[2][c], -1)
            for n in range(4):
                for q in range(7):
                    pv_ref[pl.ds((n * 7 + q) * 8, 8), :] = child[1][n][q]

            for d in (1, 2):
                if d == 1:
                    ahead, back = (lambda y: next_j(y, m)), (lambda y: last_j(y, m))
                    first, last, rim_ref = m["j_first"], m["j_last"], ej_ref
                else:
                    ahead, back = next_k, last_k
                    first, last, rim_ref = m["k_first"], m["k_last"], ek_ref
                beyond = [tuple(ahead(y) for y in st) for st in lower[d]]
                sums = face_sums(upper[d], beyond, d)
                t0, t1 = TANGENTS[d]
                wall_a = wall_sums(x[4], s[d][4], s[t0][4], s[t1][4])
                wall_b = [
                    ahead(y) for y in wall_sums(x[4], -s[d][4], s[t0][4], s[t1][4])
                ]
                sums = walled(sums, d, solid, ahead(solid), wall_a, wall_b)
                for c in range(5):
                    edge = [rim_ref[rows8((q * 5 + c) * ROWS + row), :] for q in range(3)]
                    high = [jnp.where(last, edge[q], sums[q][c]) for q in range(3)]
                    low = [jnp.where(first, edge[q], back(sums[q][c])) for q in range(3)]
                    add(0, c, high[0], 1)
                    add(0, c, low[0], -1)
                    add(d + 1, c, high[0], 1)
                    add(d + 1, c, low[0], 1)
                    add(t0 + 1, c, high[1], 1)
                    add(t0 + 1, c, low[1], -1)
                    add(t1 + 1, c, high[2], 1)
                    add(t1 + 1, c, low[2], -1)
            for k in range(4):
                for c in range(5):
                    out_ref[rows8((k * 5 + c) * MR + PL + row), :] = moments[k][c]
            return 0

        lax.fori_loop(0, EDGE, plane, 0)
        before = [tuple(pv_ref[pl.ds((n * 7 + q) * 8, 8), :] for q in range(7)) for n in range(4)]
        above = state([g_ref[rows8(c * 144 + PL + g8), :] for c in range(5)])
        put_back(face_sums(before, [above] * 4, 0), EDGE * PL + g8)
        return 0

    lax.fori_loop(0, 3, column, 0)


def adjoint_kernel(
    edge_ref, index_ref, adj_ref, solid_ref, got0_ref, got_ref, low_ref, high_ref, mom_ref, out_ref,
    g_ref, px_ref, gj_ref, gk_ref, acc_ref,
):
    def received(c, q):
        if c == 0:
            return got0_ref[pl.ds(20 + q, PEERS, stride=24), :]
        return got_ref[pl.ds((c - 1) * 4 + q, PEERS, stride=16), :]

    ghost_planes(
        edge_ref,
        index_ref,
        received,
        lambda s, c: (low_ref, high_ref)[s][pl.ds((c + 5) * PL, PL), :],
        (0.0,) * 5,
        g_ref,
    )
    for c in range(5):
        px_ref[pl.ds(c * PXR, PL), :] = g_ref[pl.ds(c * 144, PL), :]
        px_ref[pl.ds(c * PXR + PL, ROWS), :] = adj_ref[pl.ds(c * ROWS, ROWS), :]
        px_ref[pl.ds(c * PXR + PL + ROWS, PL), :] = g_ref[pl.ds(c * 144 + PL, PL), :]
    spread_ghosts(g_ref, gj_ref, gk_ref)
    m = masks()

    def weigh(n, _):
        total = None
        for c in range(5):
            at = c * PXR + PL + n * 8
            x = px_ref[rows8(at), :]
            s = slopes_of(
                px_ref[rows8(at - PL), :],
                x,
                px_ref[rows8(at + PL), :],
                gj_ref[rows8(c * ROWS + n * 8), :],
                gk_ref[rows8(c * ROWS + n * 8), :],
                m,
            )
            y = [mom_ref[rows8((k * 5 + c) * MR + PL + n * 8), :] for k in range(4)]
            part = WEIGHTS[c] * (x * y[0] + s[0] * y[1] + s[1] * y[2] + s[2] * y[3])
            total = part if total is None else total + part
        acc_ref[rows8(n * 8), :] = jnp.where(
            solid_ref[rows8(n * 8), :] > 0.5, 0.0, jnp.abs(total)
        )
        return 0

    lax.fori_loop(0, ROWS // 8, weigh, 0)
    for t in range(2 * EDGE):
        i, jh = divmod(t, 2)
        out_ref[:, pl.ds(t * LANES, LANES)] = acc_ref[pl.ds(i * PL + jh, NB, stride=2), :]


def shape(*dims):
    return jax.ShapeDtypeStruct(dims, jnp.float32)


def scratch(*rows):
    return [pltpu.VMEM((r, LANES), jnp.float32) for r in rows]


SMEM = pl.BlockSpec(memory_space=pltpu.SMEM)
VMEM = pl.BlockSpec(memory_space=pltpu.VMEM)
PARAMS = pltpu.CompilerParams(vmem_limit_bytes=VMEM_LIMIT)


def prep(flow, adjoint, cut_flag, own, vertical):
    return pl.pallas_call(
        prep_kernel,
        out_shape=[
            shape(5 * ROWS, LANES),
            shape(5 * ROWS, LANES),
            shape(ROWS, LANES),
            shape(10 * FACES, LANES),
            shape(10 * PL, LANES),
            shape(10 * PL, LANES),
            jax.ShapeDtypeStruct((288, LANES), jnp.int32),
        ],
        in_specs=[VMEM] * 5,
        out_specs=[VMEM] * 7,
        compiler_params=PARAMS,
    )(flow.transpose(1, 0, 2), adjoint.transpose(1, 0, 2), cut_flag[None], own, vertical)


def reply(me, asked, layers):
    return pl.pallas_call(
        reply_kernel,
        out_shape=[shape(24 * PEERS, LANES), shape(16 * PEERS, LANES)],
        in_specs=[SMEM, VMEM, VMEM],
        out_specs=[VMEM] * 2,
        compiler_params=PARAMS,
    )(me, asked, layers)


def fluxes(edge, index, prim, solid, got, low, high):
    return pl.pallas_call(
        flux_kernel,
        out_shape=shape(20 * MR, LANES),
        in_specs=[SMEM] + [VMEM] * 6,
        out_specs=VMEM,
        scratch_shapes=scratch(
            5 * 144, 5 * PXR, 15 * ROWS, 5 * ROWS, 5 * ROWS, 60 * PL, 60 * PL, 15 * ROWS, 15 * ROWS, 224
        ),
        compiler_params=PARAMS,
    )(edge, index, prim, solid, got, low, high)


def weights(edge, index, adj, solid, got0, got, low, high, moments):
    return pl.pallas_call(
        adjoint_kernel,
        out_shape=shape(NB, EDGE * EDGE * EDGE),
        in_specs=[SMEM] + [VMEM] * 8,
        out_specs=VMEM,
        scratch_shapes=scratch(5 * 144, 5 * PXR, 5 * ROWS, 5 * ROWS, ROWS),
        compiler_params=PARAMS,
    )(edge, index, adj, solid, got0, got, low, high, moments)


def packed_requests(lateral_owner, lateral_link, vertical_link):
    link = lateral_link.T
    far = lax.broadcasted_iota(jnp.int32, link.shape, 0) ^ 1
    own = (lateral_owner[:, :, 0].T * 64 + link // 5 * 4 + far) * 8 + link % 5
    return own, vertical_link.T // 5 * 8 + vertical_link.T % 5


def exchange(block, axis):
    chunks = block.reshape(PEERS, -1, LANES)
    out = lax.all_to_all(chunks, axis, split_axis=0, concat_axis=0, tiled=True)
    return out.reshape(-1, LANES)


def local(flow, adjoint, cut_flag, lateral_owner, lateral_link, vertical_link):
    own, vertical = packed_requests(lateral_owner, lateral_link, vertical_link)
    asked = lax.all_gather(own, "blk")
    prim, adj, solid, layers, low_face, high_face, index = prep(
        flow, adjoint, cut_flag, own, vertical
    )
    regions = lax.axis_size("grp")
    region = lax.axis_index("grp")
    low = lax.ppermute(high_face, "grp", [(r, r + 1) for r in range(regions - 1)])
    high = lax.ppermute(low_face, "grp", [(r + 1, r) for r in range(regions - 1)])
    me = lax.axis_index("blk").astype(jnp.int32).reshape(1)
    first, second = reply(me, asked, layers)
    got0 = exchange(first, "blk")
    second, got0 = lax.optimization_barrier((second, got0))
    got = exchange(second, "blk")
    edge = jnp.stack([region == 0, region == regions - 1]).astype(jnp.int32)
    moments = fluxes(edge, index, prim, solid, got0, low, high)
    return weights(edge, index, adj, solid, got0, got, low, high, moments)


def solution(mesh):
    in_specs = (
        P(("blk", "grp"), None, None),
        P(("blk", "grp"), None, None),
        P(("blk", "grp"), None),
        P(("blk", "grp"), None, None),
        P(("blk", "grp"), None),
        P(("blk", "grp"), None),
    )
    out_specs = P(("blk", "grp"), None)
    return jax.shard_map(local, mesh=mesh, in_specs=in_specs, out_specs=out_specs, check_vma=False)
```

```python
import math

import jax
import jax.numpy as jnp
from jax import lax
from jax.experimental import pallas as pl
from jax.experimental.pallas import tpu as pltpu
from jax.sharding import PartitionSpec as P

EDGE = 16
NB = 12
PL = 2 * NB
ROWS = EDGE * PL
LANES = 128
PEERS = 64
FACES = 4 * PL
PXR = (EDGE + 2) * PL
MR = (EDGE + 1) * PL

VEL = math.sqrt(0.2)
PRESS = 0.2
WEIGHTS = (1.0 / VEL, 5.0, 5.0, 5.0, 2.5 / VEL)
FARFIELD = (1.0, 0.0, 0.0, 0.3 * VEL, PRESS)
KNEE = 0.4 / math.sqrt(5.0)
START = 1.2 / math.sqrt(5.0)
CURVE = 1.25 * math.sqrt(5.0)

VMEM_LIMIT = 56 * 2**20


def lane():
    return lax.broadcasted_iota(jnp.int32, (8, LANES), 1)


def even_row():
    return lax.broadcasted_iota(jnp.int32, (8, LANES), 0) % 2 == 0


def rolled(x, amount, axis=1):
    size = x.shape[axis]
    amount = amount % size
    return x if amount == 0 else pltpu.roll(x, amount, axis)


def rows8(start):
    if isinstance(start, int):
        return pl.ds(start, 8)
    return pl.ds(pl.multiple_of(start, 8), 8)


def compact_j(load, side):
    low = lane() // EDGE
    halves = []
    for ih in range(2):
        total = None
        for il in range(8):
            x = rolled(load(ih * 8 + il), 16 * il if side == 0 else 16 * il + 16)
            total = x if total is None else jnp.where(low == il, x, total)
        halves.append(total)
    if side == 0:
        return jnp.where(even_row(), halves[0], rolled(halves[1], 1, 0))
    return jnp.where(even_row(), rolled(halves[0], -1, 0), halves[1])


def compact_k(load, side):
    depth = lane() % EDGE
    total = None
    for i in range(EDGE):
        x = rolled(load(i), i if side == 0 else i - 15)
        total = x if total is None else jnp.where(depth == i, x, total)
    return total


def spread_j(low, high, i):
    ih, il = i // 8, i % 8
    a = low if ih == 0 else rolled(low, -1, 0)
    c = rolled(high, 1, 0) if ih == 0 else high
    return jnp.where(even_row(), rolled(a, -16 * il), rolled(c, 16 * (7 - il)))


def spread_k(low, high, i):
    return jnp.where(lane() % EDGE == 0, rolled(low, -i), rolled(high, 15 - i))


def column_of(packed, rows, width):
    at = lax.broadcasted_iota(jnp.int32, (rows, width), 0) // 2
    spot = lax.broadcasted_iota(jnp.int32, (rows, width), 1)
    return jnp.sum(jnp.where(at == spot, packed, 0.0), axis=1, keepdims=True)


def index_tables(own, vertical, index_ref):
    spots = lax.broadcasted_iota(jnp.int32, (PL, LANES), 1)
    half = lax.broadcasted_iota(jnp.int32, (PL, LANES), 0) % 2
    low, depth = spots // EDGE, spots % EDGE
    wide = (4 * half + low // 2) * EDGE + depth // 2

    def store(f, code, row_part, col_part, base, step):
        full = code == 4
        index_ref[pl.ds(f * PL, PL), :] = jnp.where(full, spots, wide + 8 * col_part)
        index_ref[pl.ds(144 + f * PL, PL), :] = base + step * jnp.where(full, half, row_part)

    at = lax.broadcasted_iota(jnp.int32, (PL, NB), 0) // 2
    spot = lax.broadcasted_iota(jnp.int32, (PL, NB), 1)
    entries = [own[f : f + 1, :].astype(jnp.int32) for f in range(4)]
    holders = [e >> 9 for e in entries]
    for f in range(4):
        value = column_of(own[f : f + 1, :], PL, NB).astype(jnp.int32)
        owner, code = value >> 9, value & 7
        rank = jnp.zeros((PL, 1), jnp.float32)
        for other in range(f + 1):
            same = holders[other] == owner
            if other == f:
                same = same & (spot < at)
            rank = rank + jnp.sum(jnp.where(same, 1.0, 0.0), axis=1, keepdims=True)
        rank = rank.astype(jnp.int32)
        store(f, code, code >> 1, code & 1, rank * 2 * PEERS + owner, PEERS)
    for side in range(2):
        value = column_of(vertical[side : side + 1, :], PL, NB).astype(jnp.int32)
        slot, code = value >> 3, value & 7
        store(4 + side, code, code & 1, code >> 1, slot * 2, 1)


def prep_kernel(
    flow_ref, adj_ref, flag_ref, own_ref, vertical_ref,
    prim_ref, adjl_ref, solid_ref, lat_ref, low_ref, high_ref, index_ref,
):
    def relaid(ref, c, out_ref):
        for t in range(2 * EDGE):
            i, jh = divmod(t, 2)
            part = ref[c, :, pl.ds(t * LANES, LANES)]
            out_ref[pl.ds(i * PL + jh + c * ROWS, NB, stride=2), :] = part.astype(jnp.float32)

    for c in range(5):
        relaid(flow_ref, c, prim_ref)
        relaid(adj_ref, c, adjl_ref)
    relaid(flag_ref, 0, solid_ref)
    index_tables(
        own_ref[...].astype(jnp.float32), vertical_ref[...].astype(jnp.float32), index_ref
    )

    def convert(n, _):
        at = [rows8(c * ROWS + n * 8) for c in range(5)]
        rho = prim_ref[at[0]]
        inv = 1.0 / rho
        vel = [prim_ref[at[c]] * inv for c in (1, 2, 3)]
        square = vel[0] * vel[0] + vel[1] * vel[1] + vel[2] * vel[2]
        prim_ref[at[4]] = (0.4 * PRESS) * (prim_ref[at[4]] - 0.5 * rho * square)
        for c in range(3):
            prim_ref[at[c + 1]] = vel[c] * VEL
        return 0

    lax.fori_loop(0, ROWS // 8, convert, 0)

    def layers(ref, first):
        def one(n, _):
            c, g = n // 3, n % 3

            def load(i):
                return ref[rows8(c * ROWS + i * PL + g * 8), :]

            out = (c + first) * FACES + g * 8
            lat_ref[rows8(out), :] = load(0)
            lat_ref[rows8(out + PL), :] = load(EDGE - 1)
            lat_ref[rows8(out + 2 * PL), :] = compact_j(load, 0)
            lat_ref[rows8(out + 3 * PL), :] = compact_j(load, 1)
            low_ref[rows8((c + first) * PL + g * 8), :] = compact_k(load, 0)
            high_ref[rows8((c + first) * PL + g * 8), :] = compact_k(load, 1)
            return 0

        lax.fori_loop(0, 15, one, 0)

    layers(prim_ref, 0)
    layers(adjl_ref, 5)


def reply_kernel(me_ref, asked_ref, lat_ref, first_ref, second_ref):
    before = lax.broadcasted_iota(jnp.int32, (NB, NB), 0) < lax.broadcasted_iota(
        jnp.int32, (NB, NB), 1
    )
    before = jnp.where(before, 1.0, 0.0)
    earlier = jnp.zeros((PEERS, 1), jnp.float32)
    entries = []
    for f in range(4):
        asked = asked_ref[:, f, :]
        match = (asked >> 9) == me_ref[0]
        hits = jnp.where(match, 1.0, 0.0)
        rank = jnp.dot(hits, before, preferred_element_type=jnp.float32) + earlier
        earlier = earlier + jnp.sum(hits, axis=1, keepdims=True)
        face = (asked >> 3) & 63
        target = (((face & 3) * PL) + ((face >> 2) * 2)).astype(jnp.float32) + 10.0
        entries.append((match, rank, target))
    column = lax.broadcasted_iota(jnp.int32, (PEERS, FACES), 1).astype(jnp.float32)
    picks = []
    for s in range(2):
        row = jnp.full((PEERS, 1), -10.0, jnp.float32)
        for match, rank, target in entries:
            mine = match & (rank > s - 0.5) & (rank < s + 0.5)
            row = row + jnp.sum(jnp.where(mine, target, 0.0), axis=1, keepdims=True)
        for h in range(2):
            picks.append(jnp.where(column == row + float(h), 1.0, 0.0))
    picks = jnp.concatenate(picks, axis=0)
    for c in range(10):
        out = jnp.dot(
            picks,
            lat_ref[pl.ds(c * FACES, FACES), :],
            precision=lax.Precision.HIGHEST,
            preferred_element_type=jnp.float32,
        )
        ref, at, stride = (first_ref, c * 4, 24) if c < 6 else (second_ref, (c - 6) * 4, 16)
        for q in range(4):
            ref[pl.ds(at + q, PEERS, stride=stride), :] = out[q * PEERS : (q + 1) * PEERS]


def one_hot(columns, width):
    parts = []
    for start in range(0, width, LANES):
        parts.append(
            jnp.where(
                columns == lax.broadcasted_iota(jnp.int32, columns.shape, 1) + start, 1.0, 0.0
            )
        )
    return parts[0] if len(parts) == 1 else jnp.concatenate(parts, axis=1)


def widened(x, index):
    parts = [
        jnp.take_along_axis(
            x[n : n + 8], index[n : n + 8], axis=1, mode="promise_in_bounds"
        )
        for n in range(0, x.shape[0], 8)
    ]
    return jnp.concatenate(parts, axis=0)


def ghost_planes(edge_ref, index_ref, received, around, far, g_ref):
    lateral = one_hot(index_ref[pl.ds(144, FACES), :], 4 * PEERS)
    vertical = [one_hot(index_ref[pl.ds(240 + s * PL, PL), :], LANES)[:, :PL] for s in range(2)]
    for c in range(5):
        x = jnp.concatenate([received(c, q) for q in range(4)], axis=0)
        y = jnp.dot(
            lateral, x, precision=lax.Precision.HIGHEST, preferred_element_type=jnp.float32
        )
        g_ref[pl.ds(c * 144, FACES), :] = widened(y, index_ref[pl.ds(0, FACES), :])
        for s in range(2):
            y = jnp.dot(
                vertical[s],
                around(s, c),
                precision=lax.Precision.HIGHEST,
                preferred_element_type=jnp.float32,
            )
            y = widened(y, index_ref[pl.ds(FACES + s * PL, PL), :])
            g_ref[pl.ds(c * 144 + FACES + s * PL, PL), :] = jnp.where(
                edge_ref[s] == 1, jnp.full_like(y, far[c]), y
            )


def spread_ghosts(g_ref, gj_ref, gk_ref):
    def one(n, _):
        c, g = n // 3, n % 3
        faces = [g_ref[rows8(c * 144 + f * PL + g * 8), :] for f in range(2, 6)]
        for i in range(EDGE):
            at = rows8(c * ROWS + i * PL + g * 8)
            gj_ref[at, :] = spread_j(faces[0], faces[1], i)
            gk_ref[at, :] = spread_k(faces[2], faces[3], i)
        return 0

    lax.fori_loop(0, 15, one, 0)


def minmod(a, c):
    return jnp.maximum(jnp.minimum(a, jnp.maximum(c, 0.0)), jnp.minimum(c, 0.0))


def masks():
    low, depth, even = lane() // EDGE, lane() % EDGE, even_row()
    return dict(
        k_last=depth == EDGE - 1,
        k_first=depth == 0,
        j_wrap=low == 7,
        j_back=low == 0,
        j_last=(low == 7) & ~even,
        j_first=(low == 0) & even,
    )


def next_k(x):
    return rolled(x, -1)


def last_k(x):
    return rolled(x, 1)


def next_j(x, m):
    r = rolled(x, -16)
    return jnp.where(m["j_wrap"], rolled(r, -1, 0), r)


def last_j(x, m):
    r = rolled(x, 16)
    return jnp.where(m["j_back"], rolled(r, 1, 0), r)


def slopes_of(below, x, above, gj, gk, m):
    x4 = 0.25 * x
    out = [minmod(0.25 * above - x4, x4 - 0.25 * below)]
    up = jnp.where(m["j_last"], gj, next_j(x, m))
    down = jnp.where(m["j_first"], gj, last_j(x, m))
    out.append(minmod(0.25 * up - x4, x4 - 0.25 * down))
    up = jnp.where(m["k_last"], gk, next_k(x))
    down = jnp.where(m["k_first"], gk, last_k(x))
    out.append(minmod(0.25 * up - x4, x4 - 0.25 * down))
    return out


def state(q):
    rho, u, v, w, p = q
    rs = lax.rsqrt(rho)
    enth = 7.0 * p * (rs * rs) + (u * u + v * v + w * w)
    return (rho, u, v, w, p, rho * rs, enth)


def four(base, first, second):
    out = []
    for a in (-1, 1):
        half = [x + s if a > 0 else x - s for x, s in zip(base, first)]
        for e in (-1, 1):
            out.append(state([x + s if e > 0 else x - s for x, s in zip(half, second)]))
    return out


def roe(left, right, axis):
    n = 1 + axis
    weight = right[5] * pl.reciprocal(left[5] + right[5], approx=True)
    jump = right[n] - left[n]
    mean = [None] * 4
    for c in (1, 2, 3):
        d = jump if c == n else right[c] - left[c]
        mean[c] = left[c] + weight * d
    enth = left[6] + weight * (right[6] - left[6])
    c2 = enth - (mean[1] * mean[1] + mean[2] * mean[2] + mean[3] * mean[3])
    rc = lax.rsqrt(c2)
    un = mean[n]
    ahead = un > 0.0
    sign = jnp.where(ahead, VEL, -VEL)
    b = jnp.maximum(START - jnp.abs(un) * rc, 0.0)
    s = jnp.minimum(b, KNEE)
    speed = 2.5 * b - s * (2.5 - (2.5 * CURVE) * s)
    wave = speed * ((right[4] - left[4]) * rc - sign * (left[5] * right[5] * jump))
    sc = sign * (c2 * rc)
    up = [jnp.where(ahead, left[c], right[c]) for c in (0, 1, 2, 3, 4, 6)]
    mass = up[0] * up[n]
    t = un * sc
    flux = [mass - wave]
    for c in (1, 2, 3):
        if c == n:
            flux.append((mass * up[c] + up[4]) - wave * (mean[c] - sc))
        else:
            flux.append(mass * up[c] - wave * mean[c])
    flux.append(mass * up[5] - wave * (enth - t - t))
    return flux


def face_sums(lefts, rights, axis):
    f = [roe(a, c, axis) for a, c in zip(lefts, rights)]
    plain, first, second = [], [], []
    for c in range(5):
        lo, hi = f[0][c] + f[1][c], f[2][c] + f[3][c]
        dlo, dhi = f[1][c] - f[0][c], f[3][c] - f[2][c]
        plain.append(lo + hi)
        first.append(hi - lo)
        second.append(dlo + dhi)
    return plain, first, second


def plain_sum(lefts, rights, axis):
    f = [roe(a, c, axis) for a, c in zip(lefts, rights)]
    return [(f[0][c] + f[1][c]) + (f[2][c] + f[3][c]) for c in range(5)]


def walled(sums, axis, solid_a, solid_b, wall_a, wall_b):
    from_a = (solid_b > 0.5) & (solid_a < 0.5)
    from_b = (solid_a > 0.5) & (solid_b < 0.5)
    any_wall = from_a | from_b
    out = []
    for part, pa, pb in zip(sums, wall_a, wall_b):
        new = []
        for c in range(5):
            if c == axis + 1:
                new.append(jnp.where(from_a, pa, jnp.where(from_b, pb, part[c])))
            else:
                new.append(jnp.where(any_wall, 0.0, part[c]))
        out.append(new)
    return out


def wall_sums(p, normal, first, second):
    return (4.0 * (p + normal), 4.0 * first, 4.0 * second)


TANGENTS = ((1, 2), (0, 2), (0, 1))


def flux_kernel(
    edge_ref, index_ref, prim_ref, solid_ref, got_ref, low_ref, high_ref, out_ref,
    g_ref, px_ref, s_ref, gj_ref, gk_ref, cb_ref, cf_ref, ej_ref, ek_ref, pv_ref,
):
    ghost_planes(
        edge_ref,
        index_ref,
        lambda c, q: got_ref[pl.ds(c * 4 + q, PEERS, stride=24), :],
        lambda s, c: (low_ref, high_ref)[s][pl.ds(c * PL, PL), :],
        FARFIELD,
        g_ref,
    )
    for c in range(5):
        px_ref[pl.ds(c * PXR, PL), :] = g_ref[pl.ds(c * 144, PL), :]
        px_ref[pl.ds(c * PXR + PL, ROWS), :] = prim_ref[pl.ds(c * ROWS, ROWS), :]
        px_ref[pl.ds(c * PXR + PL + ROWS, PL), :] = g_ref[pl.ds(c * 144 + PL, PL), :]
    spread_ghosts(g_ref, gj_ref, gk_ref)
    m = masks()

    def slopes(n, _):
        for c in range(5):
            at = c * PXR + PL + n * 8
            out = slopes_of(
                px_ref[rows8(at - PL), :],
                px_ref[rows8(at), :],
                px_ref[rows8(at + PL), :],
                gj_ref[rows8(c * ROWS + n * 8), :],
                gk_ref[rows8(c * ROWS + n * 8), :],
                m,
            )
            for d in range(3):
                s_ref[rows8((d * 5 + c) * ROWS + n * 8), :] = out[d]
        return 0

    lax.fori_loop(0, ROWS // 8, slopes, 0)

    def pack(n, _):
        c, g = n // 3, n % 3

        def value(i):
            return px_ref[rows8(c * PXR + PL + i * PL + g * 8), :]

        def slope(d, i):
            return s_ref[rows8((d * 5 + c) * ROWS + i * PL + g * 8), :]

        for way, compact in ((0, compact_j), (1, compact_k)):
            d = way + 1
            for side in range(2):
                parts = [
                    lambda i: value(i) - slope(d, i) if side == 0 else value(i) + slope(d, i)
                ] + [lambda i, t=t: slope(t, i) for t in TANGENTS[d]]
                for q in range(3):
                    cb_ref[rows8((((way * 2 + side) * 3 + q) * 5 + c) * PL + g * 8), :] = compact(
                        parts[q], side
                    )
        return 0

    lax.fori_loop(0, 15, pack, 0)

    def rim(g, _):
        for way in range(2):
            for side in range(2):
                at = (way * 2 + side) * 15
                quantities = [
                    [cb_ref[rows8((at + q * 5 + c) * PL + g * 8), :] for c in range(5)]
                    for q in range(3)
                ]
                own = four(*quantities)
                beyond = state(
                    [g_ref[rows8(c * 144 + (2 + way * 2 + side) * PL + g * 8), :] for c in range(5)]
                )
                outer = [beyond] * 4
                sums = face_sums(*((outer, own) if side == 0 else (own, outer)), way + 1)
                for q in range(3):
                    for c in range(5):
                        cf_ref[rows8((at + q * 5 + c) * PL + g * 8), :] = sums[q][c]
        return 0

    lax.fori_loop(0, 3, rim, 0)

    def unpack(n, _):
        q, g = n // 3, n % 3
        j0, j1, k0, k1 = (cf_ref[rows8((f * 15 + q) * PL + g * 8), :] for f in range(4))
        for i in range(EDGE):
            at = rows8(q * ROWS + i * PL + g * 8)
            ej_ref[at, :] = spread_j(j0, j1, i)
            ek_ref[at, :] = spread_k(k0, k1, i)
        return 0

    lax.fori_loop(0, 45, unpack, 0)

    def put_back(sums, row):
        for c in range(5):
            for moment, part in ((0, 0), (1, 0), (2, 1), (3, 2)):
                at = rows8((moment * 5 + c) * MR + row)
                out_ref[at, :] = out_ref[at, :] + sums[part][c]

    def column(g, _):
        g8 = g * 8
        below = state([g_ref[rows8(c * 144 + g8), :] for c in range(5)])
        for n in range(4):
            for q in range(7):
                pv_ref[pl.ds((n * 7 + q) * 8, 8), :] = below[q]
        for q in range(20):
            out_ref[rows8(q * MR + g8), :] = jnp.zeros((8, LANES), jnp.float32)

        def plane(i, _):
            row = i * PL + g8
            x = [px_ref[rows8(c * PXR + PL + row), :] for c in range(5)]
            s = [[s_ref[rows8((d * 5 + c) * ROWS + row), :] for c in range(5)] for d in range(3)]
            solid = solid_ref[rows8(row), :]
            child = [
                four([a + b if up else a - b for a, b in zip(x, s[0])], s[1], s[2])
                for up in (False, True)
            ]
            lower = [
                child[0],
                [child[0][0], child[0][1], child[1][0], child[1][1]],
                [child[0][0], child[0][2], child[1][0], child[1][2]],
            ]
            upper = [
                child[1],
                [child[0][2], child[0][3], child[1][2], child[1][3]],
                [child[0][1], child[0][3], child[1][1], child[1][3]],
            ]
            moments = [[None] * 5 for _ in range(4)]

            def add(k, c, value, sign):
                old = moments[k][c]
                if old is None:
                    moments[k][c] = value if sign > 0 else -value
                else:
                    moments[k][c] = old + value if sign > 0 else old - value

            for d in range(3):
                inner = plain_sum(lower[d], upper[d], d)
                for c in range(5):
                    add(d + 1, c, inner[c] + inner[c], -1)

            before = [
                tuple(pv_ref[pl.ds((n * 7 + q) * 8, 8), :] for q in range(7)) for n in range(4)
            ]
            prior = jnp.maximum(row - PL, g8)
            wall_a = wall_sums(
                px_ref[rows8(4 * PXR + PL + prior), :],
                *(s_ref[rows8((d * 5 + 4) * ROWS + prior), :] for d in range(3)),
            )
            wall_b = wall_sums(x[4], -s[0][4], s[1][4], s[2][4])
            sums = face_sums(before, child[0], 0)
            sums = walled(sums, 0, solid_ref[rows8(prior), :], solid, wall_a, wall_b)
            put_back(sums, row)
            for c in range(5):
                add(0, c, sums[0][c], -1)
                add(1, c, sums[0][c], 1)
                add(2, c, sums[1][c], -1)
                add(3, c, sums[2][c], -1)
            for n in range(4):
                for q in range(7):
                    pv_ref[pl.ds((n * 7 + q) * 8, 8), :] = child[1][n][q]

            for d in (1, 2):
                if d == 1:
                    ahead, back = (lambda y: next_j(y, m)), (lambda y: last_j(y, m))
                    first, last, rim_ref = m["j_first"], m["j_last"], ej_ref
                else:
                    ahead, back = next_k, last_k
                    first, last, rim_ref = m["k_first"], m["k_last"], ek_ref
                beyond = [tuple(ahead(y) for y in st) for st in lower[d]]
                sums = face_sums(upper[d], beyond, d)
                t0, t1 = TANGENTS[d]
                wall_a = wall_sums(x[4], s[d][4], s[t0][4], s[t1][4])
                wall_b = [
                    ahead(y) for y in wall_sums(x[4], -s[d][4], s[t0][4], s[t1][4])
                ]
                sums = walled(sums, d, solid, ahead(solid), wall_a, wall_b)
                for c in range(5):
                    edge = [rim_ref[rows8((q * 5 + c) * ROWS + row), :] for q in range(3)]
                    high = [jnp.where(last, edge[q], sums[q][c]) for q in range(3)]
                    low = [jnp.where(first, edge[q], back(sums[q][c])) for q in range(3)]
                    add(0, c, high[0], 1)
                    add(0, c, low[0], -1)
                    add(d + 1, c, high[0], 1)
                    add(d + 1, c, low[0], 1)
                    add(t0 + 1, c, high[1], 1)
                    add(t0 + 1, c, low[1], -1)
                    add(t1 + 1, c, high[2], 1)
                    add(t1 + 1, c, low[2], -1)
            for k in range(4):
                for c in range(5):
                    out_ref[rows8((k * 5 + c) * MR + PL + row), :] = moments[k][c]
            return 0

        lax.fori_loop(0, EDGE, plane, 0)
        before = [tuple(pv_ref[pl.ds((n * 7 + q) * 8, 8), :] for q in range(7)) for n in range(4)]
        above = state([g_ref[rows8(c * 144 + PL + g8), :] for c in range(5)])
        put_back(face_sums(before, [above] * 4, 0), EDGE * PL + g8)
        return 0

    lax.fori_loop(0, 3, column, 0)


def adjoint_kernel(
    edge_ref, index_ref, adj_ref, solid_ref, got0_ref, got_ref, low_ref, high_ref, mom_ref, out_ref,
    g_ref, px_ref, gj_ref, gk_ref, acc_ref,
):
    def received(c, q):
        if c == 0:
            return got0_ref[pl.ds(20 + q, PEERS, stride=24), :]
        return got_ref[pl.ds((c - 1) * 4 + q, PEERS, stride=16), :]

    ghost_planes(
        edge_ref,
        index_ref,
        received,
        lambda s, c: (low_ref, high_ref)[s][pl.ds((c + 5) * PL, PL), :],
        (0.0,) * 5,
        g_ref,
    )
    for c in range(5):
        px_ref[pl.ds(c * PXR, PL), :] = g_ref[pl.ds(c * 144, PL), :]
        px_ref[pl.ds(c * PXR + PL, ROWS), :] = adj_ref[pl.ds(c * ROWS, ROWS), :]
        px_ref[pl.ds(c * PXR + PL + ROWS, PL), :] = g_ref[pl.ds(c * 144 + PL, PL), :]
    spread_ghosts(g_ref, gj_ref, gk_ref)
    m = masks()

    def weigh(n, _):
        total = None
        for c in range(5):
            at = c * PXR + PL + n * 8
            x = px_ref[rows8(at), :]
            s = slopes_of(
                px_ref[rows8(at - PL), :],
                x,
                px_ref[rows8(at + PL), :],
                gj_ref[rows8(c * ROWS + n * 8), :],
                gk_ref[rows8(c * ROWS + n * 8), :],
                m,
            )
            y = [mom_ref[rows8((k * 5 + c) * MR + PL + n * 8), :] for k in range(4)]
            part = WEIGHTS[c] * (x * y[0] + s[0] * y[1] + s[1] * y[2] + s[2] * y[3])
            total = part if total is None else total + part
        acc_ref[rows8(n * 8), :] = jnp.where(
            solid_ref[rows8(n * 8), :] > 0.5, 0.0, jnp.abs(total)
        )
        return 0

    lax.fori_loop(0, ROWS // 8, weigh, 0)
    for t in range(2 * EDGE):
        i, jh = divmod(t, 2)
        out_ref[:, pl.ds(t * LANES, LANES)] = acc_ref[pl.ds(i * PL + jh, NB, stride=2), :]


def shape(*dims):
    return jax.ShapeDtypeStruct(dims, jnp.float32)


def scratch(*rows):
    return [pltpu.VMEM((r, LANES), jnp.float32) for r in rows]


SMEM = pl.BlockSpec(memory_space=pltpu.SMEM)
VMEM = pl.BlockSpec(memory_space=pltpu.VMEM)
PARAMS = pltpu.CompilerParams(vmem_limit_bytes=VMEM_LIMIT)


def prep(flow, adjoint, cut_flag, own, vertical):
    return pl.pallas_call(
        prep_kernel,
        out_shape=[
            shape(5 * ROWS, LANES),
            shape(5 * ROWS, LANES),
            shape(ROWS, LANES),
            shape(10 * FACES, LANES),
            shape(10 * PL, LANES),
            shape(10 * PL, LANES),
            jax.ShapeDtypeStruct((288, LANES), jnp.int32),
        ],
        in_specs=[VMEM] * 5,
        out_specs=[VMEM] * 7,
        compiler_params=PARAMS,
    )(flow.transpose(1, 0, 2), adjoint.transpose(1, 0, 2), cut_flag[None], own, vertical)


def reply(me, asked, layers):
    return pl.pallas_call(
        reply_kernel,
        out_shape=[shape(24 * PEERS, LANES), shape(16 * PEERS, LANES)],
        in_specs=[SMEM, VMEM, VMEM],
        out_specs=[VMEM] * 2,
        compiler_params=PARAMS,
    )(me, asked, layers)


def fluxes(edge, index, prim, solid, got, low, high):
    return pl.pallas_call(
        flux_kernel,
        out_shape=shape(20 * MR, LANES),
        in_specs=[SMEM] + [VMEM] * 6,
        out_specs=VMEM,
        scratch_shapes=scratch(
            5 * 144, 5 * PXR, 15 * ROWS, 5 * ROWS, 5 * ROWS, 60 * PL, 60 * PL, 15 * ROWS, 15 * ROWS, 224
        ),
        compiler_params=PARAMS,
    )(edge, index, prim, solid, got, low, high)


def weights(edge, index, adj, solid, got0, got, low, high, moments):
    return pl.pallas_call(
        adjoint_kernel,
        out_shape=shape(NB, EDGE * EDGE * EDGE),
        in_specs=[SMEM] + [VMEM] * 8,
        out_specs=VMEM,
        scratch_shapes=scratch(5 * 144, 5 * PXR, 5 * ROWS, 5 * ROWS, ROWS),
        compiler_params=PARAMS,
    )(edge, index, adj, solid, got0, got, low, high, moments)


def packed_requests(lateral_owner, lateral_link, vertical_link):
    link = lateral_link.T
    far = lax.broadcasted_iota(jnp.int32, link.shape, 0) ^ 1
    own = (lateral_owner[:, :, 0].T * 64 + link // 5 * 4 + far) * 8 + link % 5
    return own, vertical_link.T // 5 * 8 + vertical_link.T % 5


def exchange(block, axis):
    chunks = block.reshape(PEERS, -1, LANES)
    out = lax.all_to_all(chunks, axis, split_axis=0, concat_axis=0, tiled=True)
    return out.reshape(-1, LANES)


def local(flow, adjoint, cut_flag, lateral_owner, lateral_link, vertical_link):
    own, vertical = packed_requests(lateral_owner, lateral_link, vertical_link)
    asked = lax.all_to_all(
        jnp.broadcast_to(own, (PEERS,) + own.shape), "blk", split_axis=0, concat_axis=0, tiled=True
    )
    prim, adj, solid, layers, low_face, high_face, index = prep(
        flow, adjoint, cut_flag, own, vertical
    )
    regions = lax.axis_size("grp")
    region = lax.axis_index("grp")
    low = lax.ppermute(high_face, "grp", [(r, r + 1) for r in range(regions - 1)])
    high = lax.ppermute(low_face, "grp", [(r + 1, r) for r in range(regions - 1)])
    me = lax.axis_index("blk").astype(jnp.int32).reshape(1)
    first, second = reply(me, asked, layers)
    first, second, low, high = lax.optimization_barrier((first, second, low, high))
    got0 = exchange(first, "blk")
    second, got0 = lax.optimization_barrier((second, got0))
    got = exchange(second, "blk")
    edge = jnp.stack([region == 0, region == regions - 1]).astype(jnp.int32)
    moments = fluxes(edge, index, prim, solid, got0, low, high)
    return weights(edge, index, adj, solid, got0, got, low, high, moments)


def solution(mesh):
    in_specs = (
        P(("blk", "grp"), None, None),
        P(("blk", "grp"), None, None),
        P(("blk", "grp"), None),
        P(("blk", "grp"), None, None),
        P(("blk", "grp"), None),
        P(("blk", "grp"), None),
    )
    out_specs = P(("blk", "grp"), None)
    return jax.shard_map(local, mesh=mesh, in_specs=in_specs, out_specs=out_specs, check_vma=False)
```

```python
import math

import jax
import jax.numpy as jnp
from jax import lax
from jax.experimental import pallas as pl
from jax.experimental.pallas import tpu as pltpu
from jax.sharding import PartitionSpec as P

EDGE = 16
NB = 12
PL = 2 * NB
ROWS = EDGE * PL
LANES = 128
PEERS = 64
FACES = 4 * PL
PXR = (EDGE + 2) * PL
MR = (EDGE + 1) * PL

VEL = math.sqrt(0.2)
PRESS = 0.2
WEIGHTS = (1.0 / VEL, 5.0, 5.0, 5.0, 2.5 / VEL)
FARFIELD = (1.0, 0.0, 0.0, 0.3 * VEL, PRESS)
KNEE = 0.4 / math.sqrt(5.0)
START = 1.2 / math.sqrt(5.0)
CURVE = 1.25 * math.sqrt(5.0)

VMEM_LIMIT = 56 * 2**20


def lane():
    return lax.broadcasted_iota(jnp.int32, (8, LANES), 1)


def even_row():
    return lax.broadcasted_iota(jnp.int32, (8, LANES), 0) % 2 == 0


def rolled(x, amount, axis=1):
    size = x.shape[axis]
    amount = amount % size
    return x if amount == 0 else pltpu.roll(x, amount, axis)


def rows8(start):
    if isinstance(start, int):
        return pl.ds(start, 8)
    return pl.ds(pl.multiple_of(start, 8), 8)


def compact_j(load, side):
    low = lane() // EDGE
    halves = []
    for ih in range(2):
        total = None
        for il in range(8):
            x = rolled(load(ih * 8 + il), 16 * il if side == 0 else 16 * il + 16)
            total = x if total is None else jnp.where(low == il, x, total)
        halves.append(total)
    if side == 0:
        return jnp.where(even_row(), halves[0], rolled(halves[1], 1, 0))
    return jnp.where(even_row(), rolled(halves[0], -1, 0), halves[1])


def compact_k(load, side):
    depth = lane() % EDGE
    total = None
    for i in range(EDGE):
        x = rolled(load(i), i if side == 0 else i - 15)
        total = x if total is None else jnp.where(depth == i, x, total)
    return total


def compact_depths(load, count):
    low = lane() // EDGE
    spots = list(range(count)) + [7 - n for n in range(count)]
    halves = []
    for ih in range(2):
        totals = [None] * len(spots)
        for il in range(8):
            x = rolled(load(ih * 8 + il), 16 * il)
            for n, spot in enumerate(spots):
                t = totals[n]
                totals[n] = x if t is None else jnp.where(low == (spot + il) % 8, x, t)
        halves.append([rolled(t, -16 * spot) for t, spot in zip(totals, spots)])
    even = even_row()
    near = [jnp.where(even, a, rolled(c, 1, 0)) for a, c in zip(halves[0][:count], halves[1][:count])]
    far = [jnp.where(even, rolled(a, -1, 0), c) for a, c in zip(halves[0][count:], halves[1][count:])]
    return near, far


def spread_j(low, high, i):
    ih, il = i // 8, i % 8
    a = low if ih == 0 else rolled(low, -1, 0)
    c = rolled(high, 1, 0) if ih == 0 else high
    return jnp.where(even_row(), rolled(a, -16 * il), rolled(c, 16 * (7 - il)))


def spread_k(low, high, i):
    return jnp.where(lane() % EDGE == 0, rolled(low, -i), rolled(high, 15 - i))


def column_of(packed, rows, width):
    at = lax.broadcasted_iota(jnp.int32, (rows, width), 0) // 2
    spot = lax.broadcasted_iota(jnp.int32, (rows, width), 1)
    return jnp.sum(jnp.where(at == spot, packed, 0.0), axis=1, keepdims=True)


def index_tables(own, vertical, index_ref):
    spots = lax.broadcasted_iota(jnp.int32, (PL, LANES), 1)
    half = lax.broadcasted_iota(jnp.int32, (PL, LANES), 0) % 2
    low, depth = spots // EDGE, spots % EDGE
    wide = (4 * half + low // 2) * EDGE + depth // 2

    def store(f, code, row_part, col_part, base, step):
        full = code == 4
        index_ref[pl.ds(f * PL, PL), :] = jnp.where(full, spots, wide + 8 * col_part)
        index_ref[pl.ds(144 + f * PL, PL), :] = base + step * jnp.where(full, half, row_part)

    at = lax.broadcasted_iota(jnp.int32, (PL, NB), 0) // 2
    spot = lax.broadcasted_iota(jnp.int32, (PL, NB), 1)
    entries = [own[f : f + 1, :].astype(jnp.int32) for f in range(4)]
    holders = [e >> 9 for e in entries]
    for f in range(4):
        value = column_of(own[f : f + 1, :], PL, NB).astype(jnp.int32)
        owner, code = value >> 9, value & 7
        rank = jnp.zeros((PL, 1), jnp.float32)
        for other in range(f + 1):
            same = holders[other] == owner
            if other == f:
                same = same & (spot < at)
            rank = rank + jnp.sum(jnp.where(same, 1.0, 0.0), axis=1, keepdims=True)
        rank = rank.astype(jnp.int32)
        store(f, code, code >> 1, code & 1, rank * 2 * PEERS + owner, PEERS)
    for side in range(2):
        value = column_of(vertical[side : side + 1, :], PL, NB).astype(jnp.int32)
        slot, code = value >> 3, value & 7
        store(4 + side, code, code & 1, code >> 1, slot * 2, 1)


def prep_kernel(
    flow_ref, adj_ref, flag_ref, own_ref, vertical_ref,
    prim_ref, adjl_ref, solid_ref, lat_ref, low_ref, high_ref, index_ref,
):
    def relaid(ref, c, out_ref):
        for t in range(2 * EDGE):
            i, jh = divmod(t, 2)
            part = ref[c, :, pl.ds(t * LANES, LANES)]
            out_ref[pl.ds(i * PL + jh + c * ROWS, NB, stride=2), :] = part.astype(jnp.float32)

    for c in range(5):
        relaid(flow_ref, c, prim_ref)
        relaid(adj_ref, c, adjl_ref)
    relaid(flag_ref, 0, solid_ref)
    index_tables(
        own_ref[...].astype(jnp.float32), vertical_ref[...].astype(jnp.float32), index_ref
    )

    def convert(n, _):
        at = [rows8(c * ROWS + n * 8) for c in range(5)]
        rho = prim_ref[at[0]]
        inv = 1.0 / rho
        vel = [prim_ref[at[c]] * inv for c in (1, 2, 3)]
        square = vel[0] * vel[0] + vel[1] * vel[1] + vel[2] * vel[2]
        prim_ref[at[4]] = (0.4 * PRESS) * (prim_ref[at[4]] - 0.5 * rho * square)
        for c in range(3):
            prim_ref[at[c + 1]] = vel[c] * VEL
        return 0

    lax.fori_loop(0, ROWS // 8, convert, 0)

    def layers(ref, first):
        def one(n, _):
            c, g = n // 3, n % 3

            def load(i):
                return ref[rows8(c * ROWS + i * PL + g * 8), :]

            out = (c + first) * FACES + g * 8
            lat_ref[rows8(out), :] = load(0)
            lat_ref[rows8(out + PL), :] = load(EDGE - 1)
            lat_ref[rows8(out + 2 * PL), :] = compact_j(load, 0)
            lat_ref[rows8(out + 3 * PL), :] = compact_j(load, 1)
            low_ref[rows8((c + first) * PL + g * 8), :] = compact_k(load, 0)
            high_ref[rows8((c + first) * PL + g * 8), :] = compact_k(load, 1)
            return 0

        lax.fori_loop(0, 15, one, 0)

    layers(prim_ref, 0)
    layers(adjl_ref, 5)


def reply_kernel(me_ref, asked_ref, lat_ref, out_ref):
    before = lax.broadcasted_iota(jnp.int32, (NB, NB), 0) < lax.broadcasted_iota(
        jnp.int32, (NB, NB), 1
    )
    before = jnp.where(before, 1.0, 0.0)
    earlier = jnp.zeros((PEERS, 1), jnp.float32)
    entries = []
    for f in range(4):
        asked = asked_ref[:, f, :]
        match = (asked >> 9) == me_ref[0]
        hits = jnp.where(match, 1.0, 0.0)
        rank = jnp.dot(hits, before, preferred_element_type=jnp.float32) + earlier
        earlier = earlier + jnp.sum(hits, axis=1, keepdims=True)
        face = (asked >> 3) & 63
        target = (((face & 3) * PL) + ((face >> 2) * 2)).astype(jnp.float32) + 10.0
        entries.append((match, rank, target))
    column = lax.broadcasted_iota(jnp.int32, (PEERS, FACES), 1).astype(jnp.float32)
    picks = []
    for s in range(2):
        row = jnp.full((PEERS, 1), -10.0, jnp.float32)
        for match, rank, target in entries:
            mine = match & (rank > s - 0.5) & (rank < s + 0.5)
            row = row + jnp.sum(jnp.where(mine, target, 0.0), axis=1, keepdims=True)
        for h in range(2):
            picks.append(jnp.where(column == row + float(h), 1.0, 0.0))
    picks = jnp.concatenate(picks, axis=0)
    for c in range(10):
        out = jnp.dot(
            picks,
            lat_ref[pl.ds(c * FACES, FACES), :],
            precision=lax.Precision.HIGHEST,
            preferred_element_type=jnp.float32,
        )
        for q in range(4):
            out_ref[pl.ds(c * 4 + q, PEERS, stride=40), :] = out[q * PEERS : (q + 1) * PEERS]


def one_hot(columns, width):
    parts = []
    for start in range(0, width, LANES):
        parts.append(
            jnp.where(
                columns == lax.broadcasted_iota(jnp.int32, columns.shape, 1) + start, 1.0, 0.0
            )
        )
    return parts[0] if len(parts) == 1 else jnp.concatenate(parts, axis=1)


def widened(x, index):
    parts = [
        jnp.take_along_axis(
            x[n : n + 8], index[n : n + 8], axis=1, mode="promise_in_bounds"
        )
        for n in range(0, x.shape[0], 8)
    ]
    return jnp.concatenate(parts, axis=0)


def fetched(columns, parts):
    y = jnp.dot(
        columns,
        jnp.concatenate(parts, axis=1),
        precision=lax.Precision.HIGHEST,
        preferred_element_type=jnp.float32,
    )
    return [y[:, n * LANES : (n + 1) * LANES] for n in range(len(parts))]


def minmod(a, c):
    return jnp.maximum(jnp.minimum(a, jnp.maximum(c, 0.0)), jnp.minimum(c, 0.0))


def masks():
    low, depth, even = lane() // EDGE, lane() % EDGE, even_row()
    return dict(
        k_last=depth == EDGE - 1,
        k_first=depth == 0,
        j_wrap=low == 7,
        j_back=low == 0,
        j_last=(low == 7) & ~even,
        j_first=(low == 0) & even,
        j_penult=(low == 6) & ~even,
    )


def next_k(x):
    return rolled(x, -1)


def last_k(x):
    return rolled(x, 1)


def next_j(x, m):
    r = rolled(x, -16)
    return jnp.where(m["j_wrap"], rolled(r, -1, 0), r)


def last_j(x, m):
    r = rolled(x, 16)
    return jnp.where(m["j_back"], rolled(r, 1, 0), r)


def slopes_of(below, x, above, gt, gk, m):
    x4 = 0.25 * x
    out = [minmod(0.25 * above - x4, x4 - 0.25 * below)]
    gt = x if gt is None else gt
    up = jnp.where(m["j_last"], gt, next_j(x, m))
    down = jnp.where(m["j_first"], gt, last_j(x, m))
    out.append(minmod(0.25 * up - x4, x4 - 0.25 * down))
    up = jnp.where(m["k_last"], gk, next_k(x))
    down = jnp.where(m["k_first"], gk, last_k(x))
    out.append(minmod(0.25 * up - x4, x4 - 0.25 * down))
    return out


def state(q):
    rho, u, v, w, p = q
    rs = lax.rsqrt(rho)
    enth = 7.0 * p * (rs * rs) + (u * u + v * v + w * w)
    return (rho, u, v, w, p, rho * rs, enth)


def four(base, first, second):
    out = []
    for a in (-1, 1):
        half = [x + s if a > 0 else x - s for x, s in zip(base, first)]
        for e in (-1, 1):
            out.append(state([x + s if e > 0 else x - s for x, s in zip(half, second)]))
    return out


def roe(left, right, axis):
    n = 1 + axis
    weight = right[5] * pl.reciprocal(left[5] + right[5], approx=True)
    jump = right[n] - left[n]
    mean = [None] * 4
    for c in (1, 2, 3):
        d = jump if c == n else right[c] - left[c]
        mean[c] = left[c] + weight * d
    enth = left[6] + weight * (right[6] - left[6])
    c2 = enth - (mean[1] * mean[1] + mean[2] * mean[2] + mean[3] * mean[3])
    rc = lax.rsqrt(c2)
    un = mean[n]
    ahead = un > 0.0
    sign = jnp.where(ahead, VEL, -VEL)
    b = jnp.maximum(START - jnp.abs(un) * rc, 0.0)
    s = jnp.minimum(b, KNEE)
    speed = 2.5 * b - s * (2.5 - (2.5 * CURVE) * s)
    wave = speed * ((right[4] - left[4]) * rc - sign * (left[5] * right[5] * jump))
    sc = sign * (c2 * rc)
    up = [jnp.where(ahead, left[c], right[c]) for c in (0, 1, 2, 3, 4, 6)]
    mass = up[0] * up[n]
    t = un * sc
    flux = [mass - wave]
    for c in (1, 2, 3):
        if c == n:
            flux.append((mass * up[c] + up[4]) - wave * (mean[c] - sc))
        else:
            flux.append(mass * up[c] - wave * mean[c])
    flux.append(mass * up[5] - wave * (enth - t - t))
    return flux


def face_sums(lefts, rights, axis):
    f = [roe(a, c, axis) for a, c in zip(lefts, rights)]
    plain, first, second = [], [], []
    for c in range(5):
        lo, hi = f[0][c] + f[1][c], f[2][c] + f[3][c]
        dlo, dhi = f[1][c] - f[0][c], f[3][c] - f[2][c]
        plain.append(lo + hi)
        first.append(hi - lo)
        second.append(dlo + dhi)
    return plain, first, second


def plain_sum(lefts, rights, axis):
    f = [roe(a, c, axis) for a, c in zip(lefts, rights)]
    return [(f[0][c] + f[1][c]) + (f[2][c] + f[3][c]) for c in range(5)]


def walled(sums, axis, solid_a, solid_b, wall_a, wall_b, gone=None):
    from_a = (solid_b > 0.5) & (solid_a < 0.5)
    from_b = (solid_a > 0.5) & (solid_b < 0.5)
    dead = from_a | from_b
    if gone is not None:
        dead = dead | gone
    out = []
    for part, pa, pb in zip(sums, wall_a, wall_b):
        new = []
        for c in range(5):
            if c == axis + 1:
                value = jnp.where(from_a, pa, jnp.where(from_b, pb, part[c]))
                new.append(value if gone is None else jnp.where(gone, 0.0, value))
            else:
                new.append(jnp.where(dead, 0.0, part[c]))
        out.append(new)
    return out


def wall_sums(p, normal, first, second):
    return (4.0 * (p + normal), 4.0 * first, 4.0 * second)


TANGENTS = ((1, 2), (0, 2), (0, 1))


class Moments:
    def __init__(self):
        self.value = [[None] * 5 for _ in range(4)]

    def add(self, k, part, sign):
        for c in range(5):
            old = self.value[k][c]
            if old is None:
                self.value[k][c] = part[c] if sign > 0 else -part[c]
            else:
                self.value[k][c] = old + part[c] if sign > 0 else old - part[c]

    def below(self, d, sums):
        self.add(0, sums[0], -1)
        self.add(d + 1, sums[0], 1)
        for t, part in zip(TANGENTS[d], sums[1:]):
            self.add(t + 1, part, -1)

    def above(self, d, sums):
        self.add(0, sums[0], 1)
        self.add(d + 1, sums[0], 1)
        for t, part in zip(TANGENTS[d], sums[1:]):
            self.add(t + 1, part, 1)

    def weighed(self, adj, slopes):
        total = None
        for c in range(5):
            part = adj[c] * self.value[0][c]
            for d in range(3):
                part = part + slopes[d][c] * self.value[d + 1][c]
            total = WEIGHTS[c] * part if total is None else total + WEIGHTS[c] * part
        return total


def weighed_sums(sums, normal, first, second):
    total = None
    for c in range(5):
        part = WEIGHTS[c] * (normal[c] * sums[0][c] + first[c] * sums[1][c] + second[c] * sums[2][c])
        total = part if total is None else total + part
    return total


def children(x, s):
    child = [
        four([a + b if up else a - b for a, b in zip(x, s[0])], s[1], s[2]) for up in (False, True)
    ]
    lower = [
        child[0],
        [child[0][0], child[0][1], child[1][0], child[1][1]],
        [child[0][0], child[0][2], child[1][0], child[1][2]],
    ]
    upper = [
        child[1],
        [child[0][2], child[0][3], child[1][2], child[1][3]],
        [child[0][1], child[0][3], child[1][1], child[1][3]],
    ]
    return lower, upper


def within(moments, lower, upper, axes):
    for d in range(3):
        inner = plain_sum(lower[d], upper[d], axes[d])
        moments.add(d + 1, [y + y for y in inner], -1)


def along(moments, d, axis, lower, upper, x, s, solid, ahead, back, gone):
    sums = face_sums(upper[d], [tuple(ahead(y) for y in st) for st in lower[d]], axis)
    t0, t1 = TANGENTS[d]
    wall_a = wall_sums(x[4], s[d][4], s[t0][4], s[t1][4])
    wall_b = [ahead(y) for y in wall_sums(x[4], -s[d][4], s[t0][4], s[t1][4])]
    sums = walled(sums, axis, solid, ahead(solid), wall_a, wall_b, gone)
    moments.above(d, sums)
    moments.below(d, [[back(y) for y in part] for part in sums])


def ends(moments, d, axis, x, s, ghost, first, last):
    n = axis + 1
    flip = jnp.where(first, -1.0, 1.0)
    base = [a + flip * b for a, b in zip(x, s[d])]
    t0, t1 = TANGENTS[d]
    f0, f1, g = list(s[t0]), list(s[t1]), list(ghost)
    for part in (base, f0, f1, g):
        part[n] = flip * part[n]
    sums = face_sums(four(base, f0, f1), [state(g)] * 4, axis)
    shown = first | last
    sums = [
        [jnp.where(shown, flip * y if c == n else y, 0.0) for c, y in enumerate(part)] for part in sums
    ]
    moments.add(0, sums[0], 1)
    moments.add(d + 1, [flip * y for y in sums[0]], 1)
    moments.add(t0 + 1, sums[1], 1)
    moments.add(t1 + 1, sums[2], 1)


def inner_kernel(
    edge_ref, index_ref, prim_ref, adj_ref, solid_ref, low_ref, high_ref,
    acc_ref, px_ref, pg_ref, ps_ref,
    v_ref, gk_ref, pv_ref, aw_ref,
):
    for side in range(2):
        ref = (low_ref, high_ref)[side]
        columns = one_hot(index_ref[pl.ds(240 + side * PL, PL), :], LANES)[:, :PL]
        parts = fetched(columns, [ref[pl.ds(c * PL, PL), :] for c in range(10)])
        for c in range(10):
            y = widened(parts[c], index_ref[pl.ds(FACES + side * PL, PL), :])
            far = FARFIELD[c] if c < 5 else 0.0
            v_ref[pl.ds((side * 10 + c) * PL, PL), :] = jnp.where(
                edge_ref[side] == 1, jnp.full_like(y, far), y
            )

    def spread(n, _):
        c, g = n // 3, n % 3
        low, high = (v_ref[rows8((side * 10 + c) * PL + g * 8), :] for side in range(2))
        for i in range(EDGE):
            gk_ref[rows8(c * ROWS + i * PL + g * 8), :] = spread_k(low, high, i)
        return 0

    lax.fori_loop(0, 30, spread, 0)

    def packed(load, out_ref, depth, first, step, g):
        planes = [[load(n) for n in range(depth)], [load(EDGE - 1 - n) for n in range(depth)]]
        for n, sides in enumerate((planes, compact_depths(load, depth))):
            for side in range(2):
                for at in range(depth):
                    row = (((n * 2 + side) * depth + at) * step + first) * PL + g * 8
                    out_ref[rows8(row), :] = sides[side][at]

    def pack(n, _):
        c, g = n // 3, n % 3

        def load_of(ref, first):
            return lambda i: ref[rows8((c + first) * ROWS + i * PL + g * 8), :]

        packed(load_of(prim_ref, 0), px_ref, 3, c, 10, g)
        packed(load_of(adj_ref, 0), px_ref, 3, c + 5, 10, g)
        packed(load_of(gk_ref, 0), pg_ref, 2, c, 10, g)
        packed(load_of(gk_ref, 5), pg_ref, 2, c + 5, 10, g)
        return 0

    lax.fori_loop(0, 15, pack, 0)
    for g in range(3):
        packed(lambda i: solid_ref[pl.ds(i * PL + g * 8, 8), :], ps_ref, 2, 0, 1, g)

    m = masks()
    inside = ~(m["j_first"] | m["j_last"])
    gone_j = m["j_first"] | m["j_last"] | m["j_penult"]
    for i in (0, EDGE - 1):
        acc_ref[pl.ds(i * PL, PL), :] = jnp.zeros((PL, LANES), jnp.float32)

    def column(g, _):
        g8 = g * 8
        start = state([jnp.full((8, LANES), y, jnp.float32) for y in (1.0, 0.0, 0.0, 0.0, 0.2)])
        for n in range(4):
            for q in range(7):
                pv_ref[pl.ds((n * 7 + q) * 8, 8), :] = start[q]
        aw_ref[...] = jnp.zeros_like(aw_ref)

        def plane(i, _):
            row = i * PL + g8

            def around(ref, c, first):
                at = c * ROWS + row
                return slopes_of(
                    ref[rows8(at - PL), :],
                    ref[rows8(at), :],
                    ref[rows8(at + PL), :],
                    None,
                    gk_ref[rows8((c + first) * ROWS + row), :],
                    m,
                )

            x = [prim_ref[rows8(c * ROWS + row), :] for c in range(5)]
            s = list(zip(*[around(prim_ref, c, 0) for c in range(5)]))
            ghost = [gk_ref[rows8(c * ROWS + row), :] for c in range(5)]
            solid = solid_ref[rows8(row), :]
            lower, upper = children(x, s)
            moments = Moments()
            within(moments, lower, upper, (0, 1, 2))

            before = [
                tuple(pv_ref[pl.ds((n * 7 + q) * 8, 8), :] for q in range(7)) for n in range(4)
            ]
            prior = row - PL
            wall_a = [pv_ref[pl.ds((28 + q) * 8, 8), :] for q in range(3)]
            wall_b = wall_sums(x[4], -s[0][4], s[1][4], s[2][4])
            sums = face_sums(before, lower[0], 0)
            sums = walled(sums, 0, solid_ref[rows8(prior), :], solid, wall_a, wall_b)
            used = jnp.where(i > 1, 1.0, 0.0)
            sums = [[used * y for y in part] for part in sums]
            moments.below(0, sums)
            old = [[aw_ref[pl.ds((q * 5 + c) * 8, 8), :] for c in range(5)] for q in range(3)]
            acc_ref[rows8(prior), :] = acc_ref[rows8(prior), :] + jnp.where(
                inside, weighed_sums(sums, *old), 0.0
            )
            for n in range(4):
                for q in range(7):
                    pv_ref[pl.ds((n * 7 + q) * 8, 8), :] = upper[0][n][q]
            for q, y in enumerate(wall_sums(x[4], s[0][4], s[1][4], s[2][4])):
                pv_ref[pl.ds((28 + q) * 8, 8), :] = y

            along(
                moments, 1, 1, lower, upper, x, s, solid,
                lambda y: next_j(y, m), lambda y: last_j(y, m), gone_j,
            )
            along(moments, 2, 2, lower, upper, x, s, solid, next_k, last_k, m["k_last"])
            ends(moments, 2, 2, x, s, ghost, m["k_first"], m["k_last"])

            a = [adj_ref[rows8(c * ROWS + row), :] for c in range(5)]
            t = list(zip(*[around(adj_ref, c, 5) for c in range(5)]))
            acc_ref[rows8(row), :] = jnp.where(inside, moments.weighed(a, t), 0.0)
            for c in range(5):
                aw_ref[pl.ds(c * 8, 8), :] = a[c] + t[0][c]
                aw_ref[pl.ds((5 + c) * 8, 8), :] = t[1][c]
                aw_ref[pl.ds((10 + c) * 8, 8), :] = t[2][c]
            return 0

        for q in range(3):
            pv_ref[pl.ds((28 + q) * 8, 8), :] = jnp.zeros((8, LANES), jnp.float32)
        lax.fori_loop(1, EDGE - 1, plane, 0)
        return 0

    lax.fori_loop(0, 3, column, 0)


def rim_kernel(
    index_ref, got_ref, px_ref, pg_ref, ps_ref, solid_ref, acc_ref, out_ref,
    gl_ref, tg_ref, pm_ref, total_ref,
):
    columns = one_hot(index_ref[pl.ds(144, FACES), :], 4 * PEERS)
    parts = fetched(
        columns,
        [
            jnp.concatenate(
                [got_ref[pl.ds(c * 4 + q, PEERS, stride=40), :] for q in range(4)], axis=0
            )
            for c in range(10)
        ],
    )
    for c in range(10):
        y = widened(parts[c], index_ref[pl.ds(0, FACES), :])
        for f in range(4):
            gl_ref[pl.ds((f * 10 + c) * PL, PL), :] = y[f * PL : (f + 1) * PL]

    def side_ghosts(n, _):
        c, g = n // 3, n % 3
        low, high = (gl_ref[rows8((f * 10 + c) * PL + g * 8), :] for f in (2, 3))
        for at, i in enumerate((0, 1, EDGE - 1, EDGE - 2)):
            tg_ref[rows8((at * 10 + c) * PL + g * 8), :] = spread_j(low, high, i)
        return 0

    lax.fori_loop(0, 30, side_ghosts, 0)
    m = masks()

    def boundary(n):
        axes = (n, 1 - n, 2)

        def one(at, _):
            side, g8 = at // 3, at % 3 * 8
            flip = jnp.where(side == 0, 1.0, -1.0)

            def load(ref, first):
                out = []
                for c in range(10):
                    y = ref[rows8((first + c) * PL + g8), :]
                    out.append(flip * y if c % 5 == n + 1 else y)
                return out

            place = n * 2 + side
            x = [load(px_ref, (place * 3 + depth) * 10) for depth in range(3)]
            outer = load(gl_ref, place * 10)
            gk = [load(pg_ref, (place * 2 + depth) * 10) for depth in range(2)]
            if n == 0:
                gt = [load(tg_ref, (side * 2 + depth) * 10) for depth in range(2)]
            else:
                gt = [[None] * 10] * 2
            solid = [ps_ref[rows8((place * 2 + depth) * PL + g8), :] for depth in range(2)]
            s0 = list(
                zip(*[slopes_of(outer[c], x[0][c], x[1][c], gt[0][c], gk[0][c], m) for c in range(10)])
            )
            s1 = list(
                zip(*[slopes_of(x[0][c], x[1][c], x[2][c], gt[1][c], gk[1][c], m) for c in range(10)])
            )
            flow, adj = x[0][:5], x[0][5:]
            s, t = [y[:5] for y in s0], [y[5:] for y in s0]
            lower, upper = children(flow, s)
            moments = Moments()
            within(moments, lower, upper, axes)
            moments.below(0, face_sums([state(outer[:5])] * 4, lower[0], n))

            flow1, adj1 = x[1][:5], x[1][5:]
            f1, t1 = [y[:5] for y in s1], [y[5:] for y in s1]
            sums = face_sums(
                upper[0], four([a - b for a, b in zip(flow1, f1[0])], f1[1], f1[2]), n
            )
            sums = walled(
                sums,
                n,
                solid[0],
                solid[1],
                wall_sums(flow[4], s[0][4], s[1][4], s[2][4]),
                wall_sums(flow1[4], -f1[0][4], f1[1][4], f1[2][4]),
            )
            moments.above(0, sums)
            next_total = -weighed_sums(
                sums, [a - b for a, b in zip(adj1, t1[0])], t1[1], t1[2]
            )

            gone = m["j_last"]
            if n == 1:
                gone = gone | m["j_first"] | m["j_penult"]
            along(
                moments, 1, axes[1], lower, upper, flow, s, solid[0],
                lambda y: next_j(y, m), lambda y: last_j(y, m), gone,
            )
            if n == 0:
                ends(moments, 1, axes[1], flow, s, gt[0][:5], m["j_first"], m["j_last"])
            along(moments, 2, 2, lower, upper, flow, s, solid[0], next_k, last_k, m["k_last"])
            ends(moments, 2, 2, flow, s, gk[0][:5], m["k_first"], m["k_last"])
            total = moments.weighed(adj, t)
            if n == 1:
                kept = ~(m["j_first"] | m["j_last"])
                total = jnp.where(kept, total, 0.0)
                next_total = jnp.where(kept, next_total, 0.0)
            pm_ref[rows8(place * 2 * PL + g8), :] = total
            pm_ref[rows8((place * 2 + 1) * PL + g8), :] = next_total
            return 0

        lax.fori_loop(0, 6, one, 0)

    boundary(0)
    boundary(1)

    low, even = lane() // EDGE, even_row()
    for g in range(3):
        planes = [[pm_ref[pl.ds((p * 2 + d) * PL + g * 8, 8), :] for d in range(2)] for p in range(4)]
        near = [planes[2], [rolled(y, -1, 0) for y in planes[2]]]
        far = [[rolled(y, 1, 0) for y in planes[3]], planes[3]]
        for i in range(EDGE):
            ih, il = i // 8, i % 8
            a, c = near[ih], far[ih]
            extra = jnp.where(
                even,
                jnp.where(
                    low == 0,
                    rolled(a[0], -16 * il),
                    jnp.where(low == 1, rolled(a[1], 16 - 16 * il), 0.0),
                ),
                jnp.where(
                    low == 7,
                    rolled(c[0], 112 - 16 * il),
                    jnp.where(low == 6, rolled(c[1], 96 - 16 * il), 0.0),
                ),
            )
            at = pl.ds(i * PL + g * 8, 8)
            total = acc_ref[at, :] + extra
            if i < 2:
                total = total + planes[0][i]
            elif i > EDGE - 3:
                total = total + planes[1][EDGE - 1 - i]
            total_ref[at, :] = jnp.where(solid_ref[at, :] > 0.5, 0.0, jnp.abs(total))
    for t in range(2 * EDGE):
        i, jh = divmod(t, 2)
        out_ref[:, pl.ds(t * LANES, LANES)] = total_ref[pl.ds(i * PL + jh, NB, stride=2), :]


def shape(*dims):
    return jax.ShapeDtypeStruct(dims, jnp.float32)


def scratch(*rows):
    return [pltpu.VMEM((r, LANES), jnp.float32) for r in rows]


SMEM = pl.BlockSpec(memory_space=pltpu.SMEM)
VMEM = pl.BlockSpec(memory_space=pltpu.VMEM)
PARAMS = pltpu.CompilerParams(vmem_limit_bytes=VMEM_LIMIT)


def prep(flow, adjoint, cut_flag, own, vertical):
    return pl.pallas_call(
        prep_kernel,
        out_shape=[
            shape(5 * ROWS, LANES),
            shape(5 * ROWS, LANES),
            shape(ROWS, LANES),
            shape(10 * FACES, LANES),
            shape(10 * PL, LANES),
            shape(10 * PL, LANES),
            jax.ShapeDtypeStruct((288, LANES), jnp.int32),
        ],
        in_specs=[VMEM] * 5,
        out_specs=[VMEM] * 7,
        cost_estimate=pl.CostEstimate(flops=10**8, bytes_accessed=3 * 10**7, transcendentals=0),
        compiler_params=PARAMS,
    )(flow.transpose(1, 0, 2), adjoint.transpose(1, 0, 2), cut_flag[None], own, vertical)


def reply(me, asked, layers):
    return pl.pallas_call(
        reply_kernel,
        out_shape=shape(40 * PEERS, LANES),
        in_specs=[SMEM, VMEM, VMEM],
        out_specs=VMEM,
        compiler_params=PARAMS,
    )(me, asked, layers)


def inner(edge, index, prim, adj, solid, low, high):
    return pl.pallas_call(
        inner_kernel,
        out_shape=[
            shape(ROWS, LANES), shape(120 * PL, LANES), shape(80 * PL, LANES), shape(8 * PL, LANES)
        ],
        in_specs=[SMEM] + [VMEM] * 6,
        out_specs=[VMEM] * 4,
        scratch_shapes=scratch(20 * PL, 10 * ROWS, 31 * 8, 15 * 8),
        compiler_params=PARAMS,
    )(edge, index, prim, adj, solid, low, high)


def rim(index, got, planes, ghosts, walls, solid, acc):
    return pl.pallas_call(
        rim_kernel,
        out_shape=shape(NB, EDGE * EDGE * EDGE),
        in_specs=[VMEM] * 7,
        out_specs=VMEM,
        scratch_shapes=scratch(40 * PL, 40 * PL, 8 * PL, ROWS),
        compiler_params=PARAMS,
    )(index, got, planes, ghosts, walls, solid, acc)


def packed_requests(lateral_owner, lateral_link, vertical_link):
    link = lateral_link.T
    far = lax.broadcasted_iota(jnp.int32, link.shape, 0) ^ 1
    own = (lateral_owner[:, :, 0].T * 64 + link // 5 * 4 + far) * 8 + link % 5
    return own, vertical_link.T // 5 * 8 + vertical_link.T % 5


def exchange(block, axis):
    chunks = block.reshape(PEERS, -1, LANES)
    out = lax.all_to_all(chunks, axis, split_axis=0, concat_axis=0, tiled=True)
    return out.reshape(-1, LANES)


def local(flow, adjoint, cut_flag, lateral_owner, lateral_link, vertical_link):
    own, vertical = packed_requests(lateral_owner, lateral_link, vertical_link)
    asked = lax.all_to_all(
        jnp.broadcast_to(own, (PEERS,) + own.shape), "blk", split_axis=0, concat_axis=0, tiled=True
    )
    prim, adj, solid, layers, low_face, high_face, index = prep(
        flow, adjoint, cut_flag, own, vertical
    )
    asked, low_face, high_face = lax.optimization_barrier((asked, low_face, high_face))
    regions = lax.axis_size("grp")
    region = lax.axis_index("grp")
    low = lax.ppermute(high_face, "grp", [(r, r + 1) for r in range(regions - 1)])
    high = lax.ppermute(low_face, "grp", [(r + 1, r) for r in range(regions - 1)])
    me = lax.axis_index("blk").astype(jnp.int32).reshape(1)
    replies = reply(me, asked, layers)
    replies, low, high = lax.optimization_barrier((replies, low, high))
    got = exchange(replies, "blk")
    edge = jnp.stack([region == 0, region == regions - 1]).astype(jnp.int32)
    acc, planes, ghosts, walls = inner(edge, index, prim, adj, solid, low, high)
    return rim(index, got, planes, ghosts, walls, solid, acc)


def solution(mesh):
    in_specs = (
        P(("blk", "grp"), None, None),
        P(("blk", "grp"), None, None),
        P(("blk", "grp"), None),
        P(("blk", "grp"), None, None),
        P(("blk", "grp"), None),
        P(("blk", "grp"), None),
    )
    out_specs = P(("blk", "grp"), None)
    return jax.shard_map(local, mesh=mesh, in_specs=in_specs, out_specs=out_specs, check_vma=False)
```

```python
import math

import jax
import jax.numpy as jnp
from jax import lax
from jax.experimental import pallas as pl
from jax.experimental.pallas import tpu as pltpu
from jax.sharding import PartitionSpec as P

EDGE = 16
NB = 12
PL = 2 * NB
ROWS = EDGE * PL
LANES = 128
PEERS = 64
FACES = 4 * PL
PXR = (EDGE + 2) * PL
MR = (EDGE + 1) * PL

VEL = math.sqrt(0.2)
PRESS = 0.2
WEIGHTS = (1.0 / VEL, 5.0, 5.0, 5.0, 2.5 / VEL)
FARFIELD = (1.0, 0.0, 0.0, 0.3 * VEL, PRESS)
KNEE = 0.4 / math.sqrt(5.0)
START = 1.2 / math.sqrt(5.0)
CURVE = 1.25 * math.sqrt(5.0)

VMEM_LIMIT = 24 * 2**20


def lane():
    return lax.broadcasted_iota(jnp.int32, (8, LANES), 1)


def even_row():
    return lax.broadcasted_iota(jnp.int32, (8, LANES), 0) % 2 == 0


def rolled(x, amount, axis=1):
    size = x.shape[axis]
    amount = amount % size
    return x if amount == 0 else pltpu.roll(x, amount, axis)


def rows8(start):
    if isinstance(start, int):
        return pl.ds(start, 8)
    return pl.ds(pl.multiple_of(start, 8), 8)


def compact_k(load):
    depth = lane() % EDGE
    low = high = None
    for i in range(EDGE):
        x = rolled(load(i), i)
        low = x if low is None else jnp.where(depth == i, x, low)
        high = x if high is None else jnp.where(depth == (i + 15) % EDGE, x, high)
    return low, rolled(high, -15)


def compact_depths(load, count):
    low = lane() // EDGE
    spots = list(range(count)) + [7 - n for n in range(count)]
    halves = []
    for ih in range(2):
        totals = [None] * len(spots)
        for il in range(8):
            x = rolled(load(ih * 8 + il), 16 * il)
            for n, spot in enumerate(spots):
                t = totals[n]
                totals[n] = x if t is None else jnp.where(low == (spot + il) % 8, x, t)
        halves.append(totals)
    even = even_row()
    near = [jnp.where(even, a, rolled(c, 1, 0)) for a, c in zip(halves[0][:count], halves[1][:count])]
    far = [jnp.where(even, rolled(a, -1, 0), c) for a, c in zip(halves[0][count:], halves[1][count:])]
    out = [rolled(t, -16 * spot) for t, spot in zip(near + far, spots)]
    return out[:count], out[count:]


def spread_j(low, high, i):
    ih, il = i // 8, i % 8
    a = low if ih == 0 else rolled(low, -1, 0)
    c = rolled(high, 1, 0) if ih == 0 else high
    return jnp.where(even_row(), rolled(a, -16 * il), rolled(c, 16 * (7 - il)))


def spread_k(low, high, i):
    return jnp.where(lane() % EDGE == 0, rolled(low, -i), rolled(high, 15 - i))


def column_of(packed, rows, width):
    at = lax.broadcasted_iota(jnp.int32, (rows, width), 0) // 2
    spot = lax.broadcasted_iota(jnp.int32, (rows, width), 1)
    return jnp.sum(jnp.where(at == spot, packed, 0.0), axis=1, keepdims=True)


def index_tables(own, vertical, index_ref):
    spots = lax.broadcasted_iota(jnp.int32, (PL, LANES), 1)
    half = lax.broadcasted_iota(jnp.int32, (PL, LANES), 0) % 2
    low, depth = spots // EDGE, spots % EDGE
    wide = (4 * half + low // 2) * EDGE + depth // 2

    def store(f, code, row_part, col_part, base, step):
        full = code == 4
        index_ref[pl.ds(f * PL, PL), :] = jnp.where(full, spots, wide + 8 * col_part)
        index_ref[pl.ds(144 + f * PL, PL), :] = base + step * jnp.where(full, half, row_part)

    at = lax.broadcasted_iota(jnp.int32, (PL, NB), 0) // 2
    spot = lax.broadcasted_iota(jnp.int32, (PL, NB), 1)
    entries = [own[f : f + 1, :].astype(jnp.int32) for f in range(4)]
    holders = [e >> 9 for e in entries]
    for f in range(4):
        value = column_of(own[f : f + 1, :], PL, NB).astype(jnp.int32)
        owner, code = value >> 9, value & 7
        rank = jnp.zeros((PL, 1), jnp.float32)
        for other in range(f + 1):
            same = holders[other] == owner
            if other == f:
                same = same & (spot < at)
            rank = rank + jnp.sum(jnp.where(same, 1.0, 0.0), axis=1, keepdims=True)
        rank = rank.astype(jnp.int32)
        store(f, code, code >> 1, code & 1, rank * 2 * PEERS + owner, PEERS)
    for side in range(2):
        value = column_of(vertical[side : side + 1, :], PL, NB).astype(jnp.int32)
        slot = (value.astype(jnp.float32) * 0.2 + 0.05).astype(jnp.int32)
        code = value - 5 * slot
        store(4 + side, code, code & 1, code >> 1, slot * 2, 1)


def prep_kernel(
    flow_ref, adj_ref, flag_ref, own_ref, vertical_ref,
    prim_ref, adjl_ref, solid_ref, lat_ref, low_ref, high_ref, index_ref,
):
    def relaid(ref, c, out_ref):
        for t in range(2 * EDGE):
            i, jh = divmod(t, 2)
            part = ref[c, :, pl.ds(t * LANES, LANES)]
            out_ref[pl.ds(i * PL + jh + c * ROWS, NB, stride=2), :] = part.astype(jnp.float32)

    for c in range(5):
        relaid(flow_ref, c, prim_ref)
        relaid(adj_ref, c, adjl_ref)
    relaid(flag_ref, 0, solid_ref)
    index_tables(
        own_ref[0].astype(jnp.float32), vertical_ref[...].astype(jnp.float32), index_ref
    )

    def convert(n, _):
        at = [pl.ds(pl.multiple_of(c * ROWS + n * 64, 64), 64) for c in range(5)]
        rho = prim_ref[at[0]]
        inv = 1.0 / rho
        vel = [prim_ref[at[c]] * inv for c in (1, 2, 3)]
        square = vel[0] * vel[0] + vel[1] * vel[1] + vel[2] * vel[2]
        prim_ref[at[4]] = (0.4 * PRESS) * (prim_ref[at[4]] - 0.5 * rho * square)
        for c in range(3):
            prim_ref[at[c + 1]] = vel[c] * VEL
        return 0

    lax.fori_loop(0, ROWS // 64, convert, 0)

    def layers(ref, first):
        def one(c, _):
            for g in range(3):

                def load(i):
                    return ref[rows8(c * ROWS + i * PL + g * 8), :]

                out = (c + first) * FACES + g * 8
                lat_ref[rows8(out), :] = load(0)
                lat_ref[rows8(out + PL), :] = load(EDGE - 1)
                near, far = compact_depths(load, 1)
                lat_ref[rows8(out + 2 * PL), :] = near[0]
                lat_ref[rows8(out + 3 * PL), :] = far[0]
                low, high = compact_k(load)
                low_ref[rows8((c + first) * PL + g * 8), :] = low
                high_ref[rows8((c + first) * PL + g * 8), :] = high
            return 0

        lax.fori_loop(0, 5, one, 0)

    layers(prim_ref, 0)
    layers(adjl_ref, 5)


def reply_kernel(me_ref, asked_ref, lat_ref, out_ref):
    before = lax.broadcasted_iota(jnp.int32, (NB, NB), 0) < lax.broadcasted_iota(
        jnp.int32, (NB, NB), 1
    )
    before = jnp.where(before, 1.0, 0.0)
    earlier = jnp.zeros((PEERS, 1), jnp.float32)
    entries = []
    for f in range(4):
        asked = asked_ref[:, f, :]
        match = (asked >> 9) == me_ref[0]
        hits = jnp.where(match, 1.0, 0.0)
        rank = jnp.dot(hits, before, preferred_element_type=jnp.float32) + earlier
        earlier = earlier + jnp.sum(hits, axis=1, keepdims=True)
        face = (asked >> 3) & 63
        target = (((face & 3) * PL) + ((face >> 2) * 2)).astype(jnp.float32) + 10.0
        entries.append((match, rank, target))
    column = lax.broadcasted_iota(jnp.int32, (PEERS, FACES), 1).astype(jnp.float32)
    picks = []
    for s in range(2):
        row = jnp.full((PEERS, 1), -10.0, jnp.float32)
        for match, rank, target in entries:
            mine = match & (rank > s - 0.5) & (rank < s + 0.5)
            row = row + jnp.sum(jnp.where(mine, target, 0.0), axis=1, keepdims=True)
        for h in range(2):
            picks.append(jnp.where(column == row + float(h), 1.0, 0.0))
    picks = jnp.concatenate(picks, axis=0)
    for c in range(10):
        out = jnp.dot(
            picks,
            lat_ref[pl.ds(c * FACES, FACES), :],
            precision=lax.Precision.HIGHEST,
            preferred_element_type=jnp.float32,
        )
        for q in range(4):
            out_ref[pl.ds(c * 4 + q, PEERS, stride=40), :] = out[q * PEERS : (q + 1) * PEERS]


def one_hot(columns, width):
    parts = []
    for start in range(0, width, LANES):
        parts.append(
            jnp.where(
                columns == lax.broadcasted_iota(jnp.int32, columns.shape, 1) + start, 1.0, 0.0
            )
        )
    return parts[0] if len(parts) == 1 else jnp.concatenate(parts, axis=1)


def widened(x, index):
    parts = [
        jnp.take_along_axis(
            x[n : n + 8], index[n : n + 8], axis=1, mode="promise_in_bounds"
        )
        for n in range(0, x.shape[0], 8)
    ]
    return jnp.concatenate(parts, axis=0)


def fetched(columns, parts):
    y = jnp.dot(
        columns,
        jnp.concatenate(parts, axis=1),
        precision=lax.Precision.HIGHEST,
        preferred_element_type=jnp.float32,
    )
    return [y[:, n * LANES : (n + 1) * LANES] for n in range(len(parts))]


def minmod(a, c):
    return jnp.maximum(jnp.minimum(a, jnp.maximum(c, 0.0)), jnp.minimum(c, 0.0))


def masks():
    low, depth, even = lane() // EDGE, lane() % EDGE, even_row()
    return dict(
        k_last=depth == EDGE - 1,
        k_first=depth == 0,
        j_wrap=low == 7,
        j_back=low == 0,
        j_last=(low == 7) & ~even,
        j_first=(low == 0) & even,
        j_penult=(low == 6) & ~even,
    )


def next_k(x):
    return rolled(x, -1)


def last_k(x):
    return rolled(x, 1)


def next_j(x, m):
    r = rolled(x, -16)
    return jnp.where(m["j_wrap"], rolled(r, -1, 0), r)


def last_j(x, m):
    r = rolled(x, 16)
    return jnp.where(m["j_back"], rolled(r, 1, 0), r)


def slopes_of(below, x, above, gt, gk, m):
    out = [0.25 * minmod(above - x, x - below)]
    gt = x if gt is None else gt
    up = jnp.where(m["j_last"], gt, next_j(x, m))
    down = jnp.where(m["j_first"], gt, last_j(x, m))
    out.append(0.25 * minmod(up - x, x - down))
    up = jnp.where(m["k_last"], gk, next_k(x))
    down = jnp.where(m["k_first"], gk, last_k(x))
    out.append(0.25 * minmod(up - x, x - down))
    return out


def state(q):
    rho, u, v, w, p = q
    rs = lax.rsqrt(rho)
    enth = 7.0 * p * (rs * rs) + (u * u + v * v + w * w)
    return (rho, u, v, w, p, rho * rs, enth)


def four(base, first, second):
    out = []
    for a in (-1, 1):
        half = [x + s if a > 0 else x - s for x, s in zip(base, first)]
        for e in (-1, 1):
            out.append(state([x + s if e > 0 else x - s for x, s in zip(half, second)]))
    return out


def roe(left, right, axis):
    n = 1 + axis
    weight = right[5] * pl.reciprocal(left[5] + right[5], approx=True)
    jump = right[n] - left[n]
    mean = [None] * 4
    for c in (1, 2, 3):
        d = jump if c == n else right[c] - left[c]
        mean[c] = left[c] + weight * d
    enth = left[6] + weight * (right[6] - left[6])
    c2 = enth - (mean[1] * mean[1] + mean[2] * mean[2] + mean[3] * mean[3])
    rc = lax.rsqrt(c2)
    un = mean[n]
    ahead = un > 0.0
    sign = jnp.where(ahead, VEL, -VEL)
    b = jnp.maximum(START - jnp.abs(un) * rc, 0.0)
    s = jnp.minimum(b, KNEE)
    speed = 2.5 * b - s * (2.5 - (2.5 * CURVE) * s)
    wave = speed * ((right[4] - left[4]) * rc - sign * (left[5] * right[5] * jump))
    sc = sign * (c2 * rc)
    up = [jnp.where(ahead, left[c], right[c]) for c in (0, 1, 2, 3, 4, 6)]
    mass = up[0] * up[n]
    t = un * sc
    flux = [mass - wave]
    for c in (1, 2, 3):
        if c == n:
            flux.append((mass * up[c] + up[4]) - wave * (mean[c] - sc))
        else:
            flux.append(mass * up[c] - wave * mean[c])
    flux.append(mass * up[5] - wave * (enth - t - t))
    return flux


def face_sums(lefts, rights, axis):
    f = [roe(a, c, axis) for a, c in zip(lefts, rights)]
    plain, first, second = [], [], []
    for c in range(5):
        lo, hi = f[0][c] + f[1][c], f[2][c] + f[3][c]
        dlo, dhi = f[1][c] - f[0][c], f[3][c] - f[2][c]
        plain.append(lo + hi)
        first.append(hi - lo)
        second.append(dlo + dhi)
    return plain, first, second


def plain_sum(lefts, rights, axis):
    f = [roe(a, c, axis) for a, c in zip(lefts, rights)]
    return [(f[0][c] + f[1][c]) + (f[2][c] + f[3][c]) for c in range(5)]


def walled(sums, axis, solid_a, solid_b, wall_a, wall_b, gone=None):
    from_a = (solid_b > 0.5) & (solid_a < 0.5)
    from_b = (solid_a > 0.5) & (solid_b < 0.5)
    dead = from_a | from_b
    if gone is not None:
        dead = dead | gone
    out = []
    for part, pa, pb in zip(sums, wall_a, wall_b):
        new = []
        for c in range(5):
            if c == axis + 1:
                value = jnp.where(from_a, pa, jnp.where(from_b, pb, part[c]))
                new.append(value if gone is None else jnp.where(gone, 0.0, value))
            else:
                new.append(jnp.where(dead, 0.0, part[c]))
        out.append(new)
    return out


def wall_sums(p, normal, first, second):
    return (4.0 * (p + normal), 4.0 * first, 4.0 * second)


TANGENTS = ((1, 2), (0, 2), (0, 1))


class Moments:
    def __init__(self):
        self.value = [[None] * 5 for _ in range(4)]

    def add(self, k, part, sign):
        for c in range(5):
            old = self.value[k][c]
            if old is None:
                self.value[k][c] = part[c] if sign > 0 else -part[c]
            else:
                self.value[k][c] = old + part[c] if sign > 0 else old - part[c]

    def below(self, d, sums):
        self.add(0, sums[0], -1)
        self.add(d + 1, sums[0], 1)
        for t, part in zip(TANGENTS[d], sums[1:]):
            self.add(t + 1, part, -1)

    def above(self, d, sums):
        self.add(0, sums[0], 1)
        self.add(d + 1, sums[0], 1)
        for t, part in zip(TANGENTS[d], sums[1:]):
            self.add(t + 1, part, 1)

    def weighed(self, adj, slopes):
        total = None
        for c in range(5):
            part = adj[c] * self.value[0][c]
            for d in range(3):
                part = part + slopes[d][c] * self.value[d + 1][c]
            total = WEIGHTS[c] * part if total is None else total + WEIGHTS[c] * part
        return total


def weighed_sums(sums, normal, first, second):
    total = None
    for c in range(5):
        part = WEIGHTS[c] * (normal[c] * sums[0][c] + first[c] * sums[1][c] + second[c] * sums[2][c])
        total = part if total is None else total + part
    return total


def children(x, s):
    child = [
        four([a + b if up else a - b for a, b in zip(x, s[0])], s[1], s[2]) for up in (False, True)
    ]
    lower = [
        child[0],
        [child[0][0], child[0][1], child[1][0], child[1][1]],
        [child[0][0], child[0][2], child[1][0], child[1][2]],
    ]
    upper = [
        child[1],
        [child[0][2], child[0][3], child[1][2], child[1][3]],
        [child[0][1], child[0][3], child[1][1], child[1][3]],
    ]
    return lower, upper


def within(moments, lower, upper, axes):
    for d in range(3):
        inner = plain_sum(lower[d], upper[d], axes[d])
        moments.add(d + 1, [y + y for y in inner], -1)


def along(moments, d, axis, lower, upper, x, s, solid, ahead, back, gone):
    sums = face_sums(upper[d], [tuple(ahead(y) for y in st) for st in lower[d]], axis)
    t0, t1 = TANGENTS[d]
    wall_a = wall_sums(x[4], s[d][4], s[t0][4], s[t1][4])
    wall_b = [ahead(y) for y in wall_sums(x[4], -s[d][4], s[t0][4], s[t1][4])]
    sums = walled(sums, axis, solid, ahead(solid), wall_a, wall_b, gone)
    moments.above(d, sums)
    moments.below(d, [[back(y) for y in part] for part in sums])


def ends(moments, d, axis, x, s, ghost, first, last):
    n = axis + 1
    flip = jnp.where(first, -1.0, 1.0)
    base = [a + flip * b for a, b in zip(x, s[d])]
    t0, t1 = TANGENTS[d]
    f0, f1, g = list(s[t0]), list(s[t1]), list(ghost)
    for part in (base, f0, f1, g):
        part[n] = flip * part[n]
    sums = face_sums(four(base, f0, f1), [state(g)] * 4, axis)
    shown = first | last
    sums = [
        [jnp.where(shown, flip * y if c == n else y, 0.0) for c, y in enumerate(part)] for part in sums
    ]
    moments.add(0, sums[0], 1)
    moments.add(d + 1, [flip * y for y in sums[0]], 1)
    moments.add(t0 + 1, sums[1], 1)
    moments.add(t1 + 1, sums[2], 1)


def inner_kernel(
    edge_ref, index_ref, prim_ref, adj_ref, solid_ref, low_ref, high_ref,
    acc_ref, px_ref, pg_ref, ps_ref,
    v_ref, gk_ref, pv_ref, aw_ref,
):
    for side in range(2):
        ref = (low_ref, high_ref)[side]
        columns = one_hot(index_ref[pl.ds(240 + side * PL, PL), :], LANES)[:, :PL]
        parts = fetched(columns, [ref[pl.ds(c * PL, PL), :] for c in range(10)])
        for c in range(10):
            y = widened(parts[c], index_ref[pl.ds(FACES + side * PL, PL), :])
            far = FARFIELD[c] if c < 5 else 0.0
            v_ref[pl.ds((side * 10 + c) * PL, PL), :] = jnp.where(
                edge_ref[side] == 1, jnp.full_like(y, far), y
            )

    def spread(c, _):
        for g in range(3):
            low, high = (v_ref[rows8((side * 10 + c) * PL + g * 8), :] for side in range(2))
            for i in range(EDGE):
                gk_ref[rows8(c * ROWS + i * PL + g * 8), :] = spread_k(low, high, i)
        return 0

    lax.fori_loop(0, 10, spread, 0)

    def packed(load, out_ref, depth, first, step, g):
        planes = [[load(n) for n in range(depth)], [load(EDGE - 1 - n) for n in range(depth)]]
        for n, sides in enumerate((planes, compact_depths(load, depth))):
            for side in range(2):
                for at in range(depth):
                    row = (((n * 2 + side) * depth + at) * step + first) * PL + g * 8
                    out_ref[rows8(row), :] = sides[side][at]

    def pack(c, _):
        for g in range(3):

            def load_of(ref, first):
                return lambda i: ref[rows8((c + first) * ROWS + i * PL + g * 8), :]

            packed(load_of(prim_ref, 0), px_ref, 3, c, 10, g)
            packed(load_of(adj_ref, 0), px_ref, 3, c + 5, 10, g)
            packed(load_of(gk_ref, 0), pg_ref, 2, c, 10, g)
            packed(load_of(gk_ref, 5), pg_ref, 2, c + 5, 10, g)
        return 0

    lax.fori_loop(0, 5, pack, 0)
    for g in range(3):
        packed(lambda i: solid_ref[pl.ds(i * PL + g * 8, 8), :], ps_ref, 2, 0, 1, g)

    m = masks()
    inside = ~(m["j_first"] | m["j_last"])
    gone_j = m["j_first"] | m["j_last"] | m["j_penult"]
    for i in (0, EDGE - 1):
        acc_ref[pl.ds(i * PL, PL), :] = jnp.zeros((PL, LANES), jnp.float32)

    def column(g, _):
        g8 = g * 8
        start = state([jnp.full((8, LANES), y, jnp.float32) for y in (1.0, 0.0, 0.0, 0.0, 0.2)])
        for n in range(4):
            for q in range(7):
                pv_ref[pl.ds((n * 7 + q) * 8, 8), :] = start[q]
        aw_ref[...] = jnp.zeros_like(aw_ref)

        def plane(i, _):
            row = i * PL + g8

            def around(ref, c, first):
                at = c * ROWS + row
                return slopes_of(
                    ref[rows8(at - PL), :],
                    ref[rows8(at), :],
                    ref[rows8(at + PL), :],
                    None,
                    gk_ref[rows8((c + first) * ROWS + row), :],
                    m,
                )

            x = [prim_ref[rows8(c * ROWS + row), :] for c in range(5)]
            s = list(zip(*[around(prim_ref, c, 0) for c in range(5)]))
            ghost = [gk_ref[rows8(c * ROWS + row), :] for c in range(5)]
            solid = solid_ref[rows8(row), :]
            lower, upper = children(x, s)
            moments = Moments()
            within(moments, lower, upper, (0, 1, 2))

            before = [
                tuple(pv_ref[pl.ds((n * 7 + q) * 8, 8), :] for q in range(7)) for n in range(4)
            ]
            prior = row - PL
            wall_a = [pv_ref[pl.ds((28 + q) * 8, 8), :] for q in range(3)]
            wall_b = wall_sums(x[4], -s[0][4], s[1][4], s[2][4])
            sums = face_sums(before, lower[0], 0)
            sums = walled(sums, 0, solid_ref[rows8(prior), :], solid, wall_a, wall_b)
            used = jnp.where(i > 1, 1.0, 0.0)
            sums = [[used * y for y in part] for part in sums]
            moments.below(0, sums)
            old = [[aw_ref[pl.ds((q * 5 + c) * 8, 8), :] for c in range(5)] for q in range(3)]
            acc_ref[rows8(prior), :] = acc_ref[rows8(prior), :] + jnp.where(
                inside, weighed_sums(sums, *old), 0.0
            )
            for n in range(4):
                for q in range(7):
                    pv_ref[pl.ds((n * 7 + q) * 8, 8), :] = upper[0][n][q]
            for q, y in enumerate(wall_sums(x[4], s[0][4], s[1][4], s[2][4])):
                pv_ref[pl.ds((28 + q) * 8, 8), :] = y

            along(
                moments, 1, 1, lower, upper, x, s, solid,
                lambda y: next_j(y, m), lambda y: last_j(y, m), gone_j,
            )
            along(moments, 2, 2, lower, upper, x, s, solid, next_k, last_k, m["k_last"])
            ends(moments, 2, 2, x, s, ghost, m["k_first"], m["k_last"])

            a = [adj_ref[rows8(c * ROWS + row), :] for c in range(5)]
            t = list(zip(*[around(adj_ref, c, 5) for c in range(5)]))
            acc_ref[rows8(row), :] = jnp.where(inside, moments.weighed(a, t), 0.0)
            for c in range(5):
                aw_ref[pl.ds(c * 8, 8), :] = a[c] + t[0][c]
                aw_ref[pl.ds((5 + c) * 8, 8), :] = t[1][c]
                aw_ref[pl.ds((10 + c) * 8, 8), :] = t[2][c]
            return 0

        for q in range(3):
            pv_ref[pl.ds((28 + q) * 8, 8), :] = jnp.zeros((8, LANES), jnp.float32)
        lax.fori_loop(1, EDGE - 1, plane, 0, unroll=2)
        return 0

    lax.fori_loop(0, 3, column, 0)


def rim_kernel(
    index_ref, got_ref, px_ref, pg_ref, ps_ref, solid_ref, acc_ref, out_ref,
    gl_ref, tg_ref, pm_ref, total_ref,
):
    columns = one_hot(index_ref[pl.ds(144, FACES), :], 4 * PEERS)
    parts = fetched(
        columns,
        [
            jnp.concatenate(
                [got_ref[pl.ds(c * 4 + q, PEERS, stride=40), :] for q in range(4)], axis=0
            )
            for c in range(10)
        ],
    )
    for c in range(10):
        y = widened(parts[c], index_ref[pl.ds(0, FACES), :])
        for f in range(4):
            gl_ref[pl.ds((f * 10 + c) * PL, PL), :] = y[f * PL : (f + 1) * PL]

    for c in range(10):
        for g in range(3):
            low, high = (gl_ref[rows8((f * 10 + c) * PL + g * 8), :] for f in (2, 3))
            for at, i in enumerate((0, 1, EDGE - 1, EDGE - 2)):
                tg_ref[rows8((at * 10 + c) * PL + g * 8), :] = spread_j(low, high, i)
    m = masks()

    def boundary(n):
        axes = (n, 1 - n, 2)

        def one(at, _):
            side, g8 = at // 3, at % 3 * 8
            flip = jnp.where(side == 0, 1.0, -1.0)

            def load(ref, first):
                out = []
                for c in range(10):
                    y = ref[rows8((first + c) * PL + g8), :]
                    out.append(flip * y if c % 5 == n + 1 else y)
                return out

            place = n * 2 + side
            x = [load(px_ref, (place * 3 + depth) * 10) for depth in range(3)]
            outer = load(gl_ref, place * 10)
            gk = [load(pg_ref, (place * 2 + depth) * 10) for depth in range(2)]
            if n == 0:
                gt = [load(tg_ref, (side * 2 + depth) * 10) for depth in range(2)]
            else:
                gt = [[None] * 10] * 2
            solid = [ps_ref[rows8((place * 2 + depth) * PL + g8), :] for depth in range(2)]
            s0 = list(
                zip(*[slopes_of(outer[c], x[0][c], x[1][c], gt[0][c], gk[0][c], m) for c in range(10)])
            )
            s1 = list(
                zip(*[slopes_of(x[0][c], x[1][c], x[2][c], gt[1][c], gk[1][c], m) for c in range(10)])
            )
            flow, adj = x[0][:5], x[0][5:]
            s, t = [y[:5] for y in s0], [y[5:] for y in s0]
            lower, upper = children(flow, s)
            moments = Moments()
            within(moments, lower, upper, axes)
            moments.below(0, face_sums([state(outer[:5])] * 4, lower[0], n))

            flow1, adj1 = x[1][:5], x[1][5:]
            f1, t1 = [y[:5] for y in s1], [y[5:] for y in s1]
            sums = face_sums(
                upper[0], four([a - b for a, b in zip(flow1, f1[0])], f1[1], f1[2]), n
            )
            sums = walled(
                sums,
                n,
                solid[0],
                solid[1],
                wall_sums(flow[4], s[0][4], s[1][4], s[2][4]),
                wall_sums(flow1[4], -f1[0][4], f1[1][4], f1[2][4]),
            )
            moments.above(0, sums)
            next_total = -weighed_sums(
                sums, [a - b for a, b in zip(adj1, t1[0])], t1[1], t1[2]
            )

            gone = m["j_last"]
            if n == 1:
                gone = gone | m["j_first"] | m["j_penult"]
            along(
                moments, 1, axes[1], lower, upper, flow, s, solid[0],
                lambda y: next_j(y, m), lambda y: last_j(y, m), gone,
            )
            if n == 0:
                ends(moments, 1, axes[1], flow, s, gt[0][:5], m["j_first"], m["j_last"])
            along(moments, 2, 2, lower, upper, flow, s, solid[0], next_k, last_k, m["k_last"])
            ends(moments, 2, 2, flow, s, gk[0][:5], m["k_first"], m["k_last"])
            total = moments.weighed(adj, t)
            if n == 1:
                kept = ~(m["j_first"] | m["j_last"])
                total = jnp.where(kept, total, 0.0)
                next_total = jnp.where(kept, next_total, 0.0)
            pm_ref[rows8(place * 2 * PL + g8), :] = total
            pm_ref[rows8((place * 2 + 1) * PL + g8), :] = next_total
            return 0

        lax.fori_loop(0, 6, one, 0)

    boundary(0)
    boundary(1)

    low, even = lane() // EDGE, even_row()
    for g in range(3):
        planes = [[pm_ref[pl.ds((p * 2 + d) * PL + g * 8, 8), :] for d in range(2)] for p in range(4)]
        near = [planes[2], [rolled(y, -1, 0) for y in planes[2]]]
        far = [[rolled(y, 1, 0) for y in planes[3]], planes[3]]
        for i in range(EDGE):
            ih, il = i // 8, i % 8
            a, c = near[ih], far[ih]
            extra = jnp.where(
                even,
                jnp.where(
                    low == 0,
                    rolled(a[0], -16 * il),
                    jnp.where(low == 1, rolled(a[1], 16 - 16 * il), 0.0),
                ),
                jnp.where(
                    low == 7,
                    rolled(c[0], 112 - 16 * il),
                    jnp.where(low == 6, rolled(c[1], 96 - 16 * il), 0.0),
                ),
            )
            at = pl.ds(i * PL + g * 8, 8)
            total = acc_ref[at, :] + extra
            if i < 2:
                total = total + planes[0][i]
            elif i > EDGE - 3:
                total = total + planes[1][EDGE - 1 - i]
            total_ref[at, :] = jnp.where(solid_ref[at, :] > 0.5, 0.0, jnp.abs(total))
    for t in range(2 * EDGE):
        i, jh = divmod(t, 2)
        out_ref[:, pl.ds(t * LANES, LANES)] = total_ref[pl.ds(i * PL + jh, NB, stride=2), :]


def shape(*dims):
    return jax.ShapeDtypeStruct(dims, jnp.float32)


def scratch(*rows):
    return [pltpu.VMEM((r, LANES), jnp.float32) for r in rows]


SMEM = pl.BlockSpec(memory_space=pltpu.SMEM)
VMEM = pl.BlockSpec(memory_space=pltpu.VMEM)
PARAMS = pltpu.CompilerParams(vmem_limit_bytes=VMEM_LIMIT)


def prep(flow, adjoint, cut_flag, own, vertical):
    return pl.pallas_call(
        prep_kernel,
        out_shape=[
            pltpu.VMEM((5 * ROWS, LANES), jnp.float32),
            pltpu.VMEM((5 * ROWS, LANES), jnp.float32),
            pltpu.VMEM((ROWS, LANES), jnp.float32),
            shape(10 * FACES, LANES),
            shape(10 * PL, LANES),
            shape(10 * PL, LANES),
            jax.ShapeDtypeStruct((288, LANES), jnp.int32),
        ],
        in_specs=[VMEM] * 5,
        out_specs=[VMEM] * 7,
        cost_estimate=pl.CostEstimate(flops=10**8, bytes_accessed=3 * 10**7, transcendentals=0),
        compiler_params=PARAMS,
    )(flow.transpose(1, 0, 2), adjoint.transpose(1, 0, 2), cut_flag[None], own, vertical)


def reply(me, asked, layers):
    return pl.pallas_call(
        reply_kernel,
        out_shape=shape(40 * PEERS, LANES),
        in_specs=[SMEM, VMEM, VMEM],
        out_specs=VMEM,
        compiler_params=PARAMS,
    )(me, asked, layers)


def inner(edge, index, prim, adj, solid, low, high):
    return pl.pallas_call(
        inner_kernel,
        out_shape=[pltpu.VMEM((n, LANES), jnp.float32) for n in (ROWS, 120 * PL, 80 * PL, 8 * PL)],
        in_specs=[SMEM] + [VMEM] * 6,
        out_specs=[VMEM] * 4,
        scratch_shapes=scratch(20 * PL, 10 * ROWS, 31 * 8, 15 * 8),
        compiler_params=PARAMS,
    )(edge, index, prim, adj, solid, low, high)


def rim(index, got, planes, ghosts, walls, solid, acc):
    return pl.pallas_call(
        rim_kernel,
        out_shape=shape(NB, EDGE * EDGE * EDGE),
        in_specs=[VMEM] * 7,
        out_specs=VMEM,
        scratch_shapes=scratch(40 * PL, 40 * PL, 8 * PL, ROWS),
        compiler_params=PARAMS,
    )(index, got, planes, ghosts, walls, solid, acc)


def ask_kernel(owner_ref, link_ref, out_ref):
    link = link_ref[...]
    slot = (link.astype(jnp.float32) * 0.2 + 0.05).astype(jnp.int32)
    far = lax.broadcasted_iota(jnp.int32, link.shape, 0) ^ 1
    own = (owner_ref[...] * 64 + slot * 4 + far) * 8 + (link - 5 * slot)
    out_ref[...] = jnp.broadcast_to(own[None], out_ref.shape)


def ask(lateral_owner, lateral_link):
    return pl.pallas_call(
        ask_kernel,
        out_shape=jax.ShapeDtypeStruct((PEERS, 4, NB), jnp.int32),
        in_specs=[VMEM] * 2,
        out_specs=VMEM,
        compiler_params=PARAMS,
    )(lateral_owner[:, :, 0].T, lateral_link.T)


def exchange(block, axis):
    chunks = block.reshape(PEERS, -1, LANES)
    out = lax.all_to_all(chunks, axis, split_axis=0, concat_axis=0, tiled=True)
    return out.reshape(-1, LANES)


def local(flow, adjoint, cut_flag, lateral_owner, lateral_link, vertical_link):
    own = ask(lateral_owner, lateral_link)
    asked = lax.all_to_all(own, "blk", split_axis=0, concat_axis=0, tiled=True)
    prim, adj, solid, layers, low_face, high_face, index = prep(
        flow, adjoint, cut_flag, own, vertical_link.T
    )
    asked, low_face, high_face = lax.optimization_barrier((asked, low_face, high_face))
    regions = lax.axis_size("grp")
    region = lax.axis_index("grp")
    low = lax.ppermute(high_face, "grp", [(r, r + 1) for r in range(regions - 1)])
    high = lax.ppermute(low_face, "grp", [(r + 1, r) for r in range(regions - 1)])
    me = lax.axis_index("blk").astype(jnp.int32).reshape(1)
    replies = reply(me, asked, layers)
    got = exchange(replies, "blk")
    edge = jnp.stack([region == 0, region == regions - 1]).astype(jnp.int32)
    acc, planes, ghosts, walls = inner(edge, index, prim, adj, solid, low, high)
    return rim(index, got, planes, ghosts, walls, solid, acc)


def solution(mesh):
    in_specs = (
        P(("blk", "grp"), None, None),
        P(("blk", "grp"), None, None),
        P(("blk", "grp"), None),
        P(("blk", "grp"), None, None),
        P(("blk", "grp"), None),
        P(("blk", "grp"), None),
    )
    out_specs = P(("blk", "grp"), None)
    return jax.shard_map(local, mesh=mesh, in_specs=in_specs, out_specs=out_specs, check_vma=False)
```

```python
import math

import jax
import jax.numpy as jnp
from jax import lax
from jax.experimental import pallas as pl
from jax.experimental.pallas import tpu as pltpu
from jax.sharding import PartitionSpec as P

EDGE = 16
NB = 12
PL = 2 * NB
ROWS = EDGE * PL
LANES = 128
PEERS = 64
FACES = 4 * PL
PXR = (EDGE + 2) * PL
MR = (EDGE + 1) * PL

VEL = math.sqrt(0.2)
PRESS = 0.2
WEIGHTS = (1.0 / VEL, 5.0, 5.0, 5.0, 2.5 / VEL)
FARFIELD = (1.0, 0.0, 0.0, 0.3 * VEL, PRESS)
KNEE = 0.4 / math.sqrt(5.0)
START = 1.2 / math.sqrt(5.0)
CURVE = 1.25 * math.sqrt(5.0)

VMEM_LIMIT = 56 * 2**20


def lane():
    return lax.broadcasted_iota(jnp.int32, (8, LANES), 1)


def even_row():
    return lax.broadcasted_iota(jnp.int32, (8, LANES), 0) % 2 == 0


def rolled(x, amount, axis=1):
    size = x.shape[axis]
    amount = amount % size
    return x if amount == 0 else pltpu.roll(x, amount, axis)


def rows8(start):
    if isinstance(start, int):
        return pl.ds(start, 8)
    return pl.ds(pl.multiple_of(start, 8), 8)


def compact_k(load):
    depth = lane() % EDGE
    low = high = None
    for i in range(EDGE):
        x = rolled(load(i), i)
        low = x if low is None else jnp.where(depth == i, x, low)
        high = x if high is None else jnp.where(depth == (i + 15) % EDGE, x, high)
    return low, rolled(high, -15)


def compact_depths(load, count):
    low = lane() // EDGE
    spots = list(range(count)) + [7 - n for n in range(count)]
    halves = []
    for ih in range(2):
        totals = [None] * len(spots)
        for il in range(8):
            x = rolled(load(ih * 8 + il), 16 * il)
            for n, spot in enumerate(spots):
                t = totals[n]
                totals[n] = x if t is None else jnp.where(low == (spot + il) % 8, x, t)
        halves.append(totals)
    even = even_row()
    near = [jnp.where(even, a, rolled(c, 1, 0)) for a, c in zip(halves[0][:count], halves[1][:count])]
    far = [jnp.where(even, rolled(a, -1, 0), c) for a, c in zip(halves[0][count:], halves[1][count:])]
    out = [rolled(t, -16 * spot) for t, spot in zip(near + far, spots)]
    return out[:count], out[count:]


def spread_j(low, high, i):
    ih, il = i // 8, i % 8
    a = low if ih == 0 else rolled(low, -1, 0)
    c = rolled(high, 1, 0) if ih == 0 else high
    return jnp.where(even_row(), rolled(a, -16 * il), rolled(c, 16 * (7 - il)))


def spread_k(low, high, i):
    return jnp.where(lane() % EDGE == 0, rolled(low, -i), rolled(high, 15 - i))


def column_of(packed, rows, width):
    at = lax.broadcasted_iota(jnp.int32, (rows, width), 0) // 2
    spot = lax.broadcasted_iota(jnp.int32, (rows, width), 1)
    return jnp.sum(jnp.where(at == spot, packed, 0.0), axis=1, keepdims=True)


def index_tables(own, vertical, index_ref):
    spots = lax.broadcasted_iota(jnp.int32, (PL, LANES), 1)
    half = lax.broadcasted_iota(jnp.int32, (PL, LANES), 0) % 2
    low, depth = spots // EDGE, spots % EDGE
    wide = (4 * half + low // 2) * EDGE + depth // 2

    def store(f, code, row_part, col_part, base, step):
        full = code == 4
        index_ref[pl.ds(f * PL, PL), :] = jnp.where(full, spots, wide + 8 * col_part)
        index_ref[pl.ds(144 + f * PL, PL), :] = base + step * jnp.where(full, half, row_part)

    at = lax.broadcasted_iota(jnp.int32, (PL, NB), 0) // 2
    spot = lax.broadcasted_iota(jnp.int32, (PL, NB), 1)
    entries = [own[f : f + 1, :].astype(jnp.int32) for f in range(4)]
    holders = [e >> 9 for e in entries]
    for f in range(4):
        value = column_of(own[f : f + 1, :], PL, NB).astype(jnp.int32)
        owner, code = value >> 9, value & 7
        rank = jnp.zeros((PL, 1), jnp.float32)
        for other in range(f + 1):
            same = holders[other] == owner
            if other == f:
                same = same & (spot < at)
            rank = rank + jnp.sum(jnp.where(same, 1.0, 0.0), axis=1, keepdims=True)
        rank = rank.astype(jnp.int32)
        store(f, code, code >> 1, code & 1, rank * 2 * PEERS + owner, PEERS)
    for side in range(2):
        value = column_of(vertical[side : side + 1, :], PL, NB).astype(jnp.int32)
        slot = (value.astype(jnp.float32) * 0.2 + 0.05).astype(jnp.int32)
        code = value - 5 * slot
        store(4 + side, code, code & 1, code >> 1, slot * 2, 1)


def prep_kernel(
    flow_ref, adj_ref, flag_ref, own_ref, vertical_ref,
    prim_ref, adjl_ref, solid_ref, lat_ref, low_ref, high_ref, index_ref,
):
    def relaid(ref, c, out_ref):
        for t in range(2 * EDGE):
            i, jh = divmod(t, 2)
            part = ref[c, :, pl.ds(t * LANES, LANES)]
            out_ref[pl.ds(i * PL + jh + c * ROWS, NB, stride=2), :] = part.astype(jnp.float32)

    for c in range(5):
        relaid(flow_ref, c, prim_ref)
        relaid(adj_ref, c, adjl_ref)
    relaid(flag_ref, 0, solid_ref)
    index_tables(
        own_ref[...].astype(jnp.float32), vertical_ref[...].astype(jnp.float32), index_ref
    )

    def convert(n, _):
        at = [pl.ds(pl.multiple_of(c * ROWS + n * 64, 64), 64) for c in range(5)]
        rho = prim_ref[at[0]]
        inv = 1.0 / rho
        vel = [prim_ref[at[c]] * inv for c in (1, 2, 3)]
        square = vel[0] * vel[0] + vel[1] * vel[1] + vel[2] * vel[2]
        prim_ref[at[4]] = (0.4 * PRESS) * (prim_ref[at[4]] - 0.5 * rho * square)
        for c in range(3):
            prim_ref[at[c + 1]] = vel[c] * VEL
        return 0

    lax.fori_loop(0, ROWS // 64, convert, 0)

    def layers(ref, first):
        def one(c, _):
            for g in range(3):

                def load(i):
                    return ref[rows8(c * ROWS + i * PL + g * 8), :]

                out = (c + first) * FACES + g * 8
                lat_ref[rows8(out), :] = load(0)
                lat_ref[rows8(out + PL), :] = load(EDGE - 1)
                near, far = compact_depths(load, 1)
                lat_ref[rows8(out + 2 * PL), :] = near[0]
                lat_ref[rows8(out + 3 * PL), :] = far[0]
                low, high = compact_k(load)
                low_ref[rows8((c + first) * PL + g * 8), :] = low
                high_ref[rows8((c + first) * PL + g * 8), :] = high
            return 0

        lax.fori_loop(0, 5, one, 0)

    layers(prim_ref, 0)
    layers(adjl_ref, 5)


def reply_kernel(me_ref, asked_ref, lat_ref, out_ref):
    before = lax.broadcasted_iota(jnp.int32, (LANES, LANES), 0) < lax.broadcasted_iota(
        jnp.int32, (LANES, LANES), 1
    )
    asked = asked_ref[...]
    match = (asked >> 9) == me_ref[0]
    rank = jnp.dot(
        jnp.where(match, 1.0, 0.0),
        jnp.where(before, 1.0, 0.0),
        preferred_element_type=jnp.float32,
    )
    face = (asked >> 3) & 63
    target = (((face & 3) * PL) + ((face >> 2) * 2)).astype(jnp.float32) + 10.0
    column = lax.broadcasted_iota(jnp.int32, (PEERS, FACES), 1).astype(jnp.float32)
    picks = []
    for s in range(2):
        mine = match & (rank > s - 0.5) & (rank < s + 0.5)
        row = jnp.sum(jnp.where(mine, target, 0.0), axis=1, keepdims=True) - 10.0
        for h in range(2):
            picks.append(jnp.where(column == row + float(h), 1.0, 0.0))
    picks = jnp.concatenate(picks, axis=0)
    for c in range(10):
        out = jnp.dot(
            picks,
            lat_ref[pl.ds(c * FACES, FACES), :],
            precision=lax.Precision.HIGHEST,
            preferred_element_type=jnp.float32,
        )
        for q in range(4):
            out_ref[pl.ds(c * 4 + q, PEERS, stride=40), :] = out[q * PEERS : (q + 1) * PEERS]


def one_hot(columns, width):
    parts = []
    for start in range(0, width, LANES):
        parts.append(
            jnp.where(
                columns == lax.broadcasted_iota(jnp.int32, columns.shape, 1) + start, 1.0, 0.0
            )
        )
    return parts[0] if len(parts) == 1 else jnp.concatenate(parts, axis=1)


def widened(x, index):
    parts = [
        jnp.take_along_axis(
            x[n : n + 8], index[n : n + 8], axis=1, mode="promise_in_bounds"
        )
        for n in range(0, x.shape[0], 8)
    ]
    return jnp.concatenate(parts, axis=0)


def fetched(columns, parts):
    y = jnp.dot(
        columns,
        jnp.concatenate(parts, axis=1),
        precision=lax.Precision.HIGHEST,
        preferred_element_type=jnp.float32,
    )
    return [y[:, n * LANES : (n + 1) * LANES] for n in range(len(parts))]


def minmod(a, c):
    return jnp.maximum(jnp.minimum(a, jnp.maximum(c, 0.0)), jnp.minimum(c, 0.0))


def masks():
    low, depth, even = lane() // EDGE, lane() % EDGE, even_row()
    return dict(
        k_last=depth == EDGE - 1,
        k_first=depth == 0,
        j_wrap=low == 7,
        j_back=low == 0,
        j_last=(low == 7) & ~even,
        j_first=(low == 0) & even,
        j_penult=(low == 6) & ~even,
    )


def next_k(x):
    return rolled(x, -1)


def last_k(x):
    return rolled(x, 1)


def next_j(x, m):
    r = rolled(x, -16)
    return jnp.where(m["j_wrap"], rolled(r, -1, 0), r)


def last_j(x, m):
    r = rolled(x, 16)
    return jnp.where(m["j_back"], rolled(r, 1, 0), r)


def slopes_of(below, x, above, gt, gk, m):
    out = [0.25 * minmod(above - x, x - below)]
    gt = x if gt is None else gt
    up = jnp.where(m["j_last"], gt, next_j(x, m))
    down = jnp.where(m["j_first"], gt, last_j(x, m))
    out.append(0.25 * minmod(up - x, x - down))
    up = jnp.where(m["k_last"], gk, next_k(x))
    down = jnp.where(m["k_first"], gk, last_k(x))
    out.append(0.25 * minmod(up - x, x - down))
    return out


def state(q):
    rho, u, v, w, p = q
    rs = lax.rsqrt(rho)
    enth = 7.0 * p * (rs * rs) + (u * u + v * v + w * w)
    return (rho, u, v, w, p, rho * rs, enth)


def four(base, first, second):
    out = []
    for a in (-1, 1):
        half = [x + s if a > 0 else x - s for x, s in zip(base, first)]
        for e in (-1, 1):
            out.append(state([x + s if e > 0 else x - s for x, s in zip(half, second)]))
    return out


def roe(left, right, axis):
    n = 1 + axis
    weight = right[5] * pl.reciprocal(left[5] + right[5], approx=True)
    jump = right[n] - left[n]
    mean = [None] * 4
    for c in (1, 2, 3):
        d = jump if c == n else right[c] - left[c]
        mean[c] = left[c] + weight * d
    enth = left[6] + weight * (right[6] - left[6])
    c2 = enth - (mean[1] * mean[1] + mean[2] * mean[2] + mean[3] * mean[3])
    rc = lax.rsqrt(c2)
    un = mean[n]
    ahead = un > 0.0
    sign = jnp.where(ahead, VEL, -VEL)
    b = jnp.maximum(START - jnp.abs(un) * rc, 0.0)
    s = jnp.minimum(b, KNEE)
    speed = 2.5 * b - s * (2.5 - (2.5 * CURVE) * s)
    wave = speed * ((right[4] - left[4]) * rc - sign * (left[5] * right[5] * jump))
    sc = sign * (c2 * rc)
    up = [jnp.where(ahead, left[c], right[c]) for c in (0, 1, 2, 3, 4, 6)]
    mass = up[0] * up[n]
    t = un * sc
    flux = [mass - wave]
    for c in (1, 2, 3):
        if c == n:
            flux.append((mass * up[c] + up[4]) - wave * (mean[c] - sc))
        else:
            flux.append(mass * up[c] - wave * mean[c])
    flux.append(mass * up[5] - wave * (enth - t - t))
    return flux


def face_sums(lefts, rights, axis):
    f = [roe(a, c, axis) for a, c in zip(lefts, rights)]
    plain, first, second = [], [], []
    for c in range(5):
        lo, hi = f[0][c] + f[1][c], f[2][c] + f[3][c]
        dlo, dhi = f[1][c] - f[0][c], f[3][c] - f[2][c]
        plain.append(lo + hi)
        first.append(hi - lo)
        second.append(dlo + dhi)
    return plain, first, second


def plain_sum(lefts, rights, axis):
    f = [roe(a, c, axis) for a, c in zip(lefts, rights)]
    return [(f[0][c] + f[1][c]) + (f[2][c] + f[3][c]) for c in range(5)]


def walled(sums, axis, solid_a, solid_b, wall_a, wall_b, gone=None):
    from_a = (solid_b > 0.5) & (solid_a < 0.5)
    from_b = (solid_a > 0.5) & (solid_b < 0.5)
    dead = from_a | from_b
    if gone is not None:
        dead = dead | gone
    out = []
    for part, pa, pb in zip(sums, wall_a, wall_b):
        new = []
        for c in range(5):
            if c == axis + 1:
                value = jnp.where(from_a, pa, jnp.where(from_b, pb, part[c]))
                new.append(value if gone is None else jnp.where(gone, 0.0, value))
            else:
                new.append(jnp.where(dead, 0.0, part[c]))
        out.append(new)
    return out


def wall_sums(p, normal, first, second):
    return (4.0 * (p + normal), 4.0 * first, 4.0 * second)


TANGENTS = ((1, 2), (0, 2), (0, 1))


class Moments:
    def __init__(self):
        self.value = [[None] * 5 for _ in range(4)]

    def add(self, k, part, sign):
        for c in range(5):
            old = self.value[k][c]
            if old is None:
                self.value[k][c] = part[c] if sign > 0 else -part[c]
            else:
                self.value[k][c] = old + part[c] if sign > 0 else old - part[c]

    def below(self, d, sums):
        self.add(0, sums[0], -1)
        self.add(d + 1, sums[0], 1)
        for t, part in zip(TANGENTS[d], sums[1:]):
            self.add(t + 1, part, -1)

    def above(self, d, sums):
        self.add(0, sums[0], 1)
        self.add(d + 1, sums[0], 1)
        for t, part in zip(TANGENTS[d], sums[1:]):
            self.add(t + 1, part, 1)

    def weighed(self, adj, slopes):
        total = None
        for c in range(5):
            part = adj[c] * self.value[0][c]
            for d in range(3):
                part = part + slopes[d][c] * self.value[d + 1][c]
            total = WEIGHTS[c] * part if total is None else total + WEIGHTS[c] * part
        return total


def weighed_sums(sums, normal, first, second):
    total = None
    for c in range(5):
        part = WEIGHTS[c] * (normal[c] * sums[0][c] + first[c] * sums[1][c] + second[c] * sums[2][c])
        total = part if total is None else total + part
    return total


def children(x, s):
    child = [
        four([a + b if up else a - b for a, b in zip(x, s[0])], s[1], s[2]) for up in (False, True)
    ]
    lower = [
        child[0],
        [child[0][0], child[0][1], child[1][0], child[1][1]],
        [child[0][0], child[0][2], child[1][0], child[1][2]],
    ]
    upper = [
        child[1],
        [child[0][2], child[0][3], child[1][2], child[1][3]],
        [child[0][1], child[0][3], child[1][1], child[1][3]],
    ]
    return lower, upper


def within(moments, lower, upper, axes):
    for d in range(3):
        inner = plain_sum(lower[d], upper[d], axes[d])
        moments.add(d + 1, [y + y for y in inner], -1)


def along(moments, d, axis, lower, upper, x, s, solid, ahead, back, gone):
    sums = face_sums(upper[d], [tuple(ahead(y) for y in st) for st in lower[d]], axis)
    t0, t1 = TANGENTS[d]
    wall_a = wall_sums(x[4], s[d][4], s[t0][4], s[t1][4])
    wall_b = [ahead(y) for y in wall_sums(x[4], -s[d][4], s[t0][4], s[t1][4])]
    sums = walled(sums, axis, solid, ahead(solid), wall_a, wall_b, gone)
    moments.above(d, sums)
    moments.below(d, [[back(y) for y in part] for part in sums])


def ends(moments, d, axis, x, s, ghost, first, last):
    n = axis + 1
    flip = jnp.where(first, -1.0, 1.0)
    base = [a + flip * b for a, b in zip(x, s[d])]
    t0, t1 = TANGENTS[d]
    f0, f1, g = list(s[t0]), list(s[t1]), list(ghost)
    for part in (base, f0, f1, g):
        part[n] = flip * part[n]
    sums = face_sums(four(base, f0, f1), [state(g)] * 4, axis)
    shown = first | last
    sums = [
        [jnp.where(shown, flip * y if c == n else y, 0.0) for c, y in enumerate(part)] for part in sums
    ]
    moments.add(0, sums[0], 1)
    moments.add(d + 1, [flip * y for y in sums[0]], 1)
    moments.add(t0 + 1, sums[1], 1)
    moments.add(t1 + 1, sums[2], 1)


def inner_kernel(
    edge_ref, index_ref, prim_ref, adj_ref, solid_ref, low_ref, high_ref,
    acc_ref, px_ref, pg_ref, ps_ref,
    v_ref, gk_ref, pv_ref, aw_ref,
):
    for side in range(2):
        ref = (low_ref, high_ref)[side]
        columns = one_hot(index_ref[pl.ds(240 + side * PL, PL), :], LANES)[:, :PL]
        parts = fetched(columns, [ref[pl.ds(c * PL, PL), :] for c in range(10)])
        for c in range(10):
            y = widened(parts[c], index_ref[pl.ds(FACES + side * PL, PL), :])
            far = FARFIELD[c] if c < 5 else 0.0
            v_ref[pl.ds((side * 10 + c) * PL, PL), :] = jnp.where(
                edge_ref[side] == 1, jnp.full_like(y, far), y
            )

    def spread(c, _):
        for g in range(3):
            low, high = (v_ref[rows8((side * 10 + c) * PL + g * 8), :] for side in range(2))
            for i in range(EDGE):
                gk_ref[rows8(c * ROWS + i * PL + g * 8), :] = spread_k(low, high, i)
        return 0

    lax.fori_loop(0, 10, spread, 0)

    def packed(load, out_ref, depth, first, step, g):
        planes = [[load(n) for n in range(depth)], [load(EDGE - 1 - n) for n in range(depth)]]
        for n, sides in enumerate((planes, compact_depths(load, depth))):
            for side in range(2):
                for at in range(depth):
                    row = (((n * 2 + side) * depth + at) * step + first) * PL + g * 8
                    out_ref[rows8(row), :] = sides[side][at]

    def pack(c, _):
        for g in range(3):

            def load_of(ref, first):
                return lambda i: ref[rows8((c + first) * ROWS + i * PL + g * 8), :]

            packed(load_of(prim_ref, 0), px_ref, 3, c, 10, g)
            packed(load_of(adj_ref, 0), px_ref, 3, c + 5, 10, g)
            packed(load_of(gk_ref, 0), pg_ref, 2, c, 10, g)
            packed(load_of(gk_ref, 5), pg_ref, 2, c + 5, 10, g)
        return 0

    lax.fori_loop(0, 5, pack, 0)
    for g in range(3):
        packed(lambda i: solid_ref[pl.ds(i * PL + g * 8, 8), :], ps_ref, 2, 0, 1, g)

    m = masks()
    inside = ~(m["j_first"] | m["j_last"])
    gone_j = m["j_first"] | m["j_last"] | m["j_penult"]
    for i in (0, EDGE - 1):
        acc_ref[pl.ds(i * PL, PL), :] = jnp.zeros((PL, LANES), jnp.float32)

    def column(g, _):
        g8 = g * 8
        start = state([jnp.full((8, LANES), y, jnp.float32) for y in (1.0, 0.0, 0.0, 0.0, 0.2)])
        for n in range(4):
            for q in range(7):
                pv_ref[pl.ds((n * 7 + q) * 8, 8), :] = start[q]
        aw_ref[...] = jnp.zeros_like(aw_ref)

        def plane(i, _):
            row = i * PL + g8

            def around(ref, c, first):
                at = c * ROWS + row
                return slopes_of(
                    ref[rows8(at - PL), :],
                    ref[rows8(at), :],
                    ref[rows8(at + PL), :],
                    None,
                    gk_ref[rows8((c + first) * ROWS + row), :],
                    m,
                )

            x = [prim_ref[rows8(c * ROWS + row), :] for c in range(5)]
            s = list(zip(*[around(prim_ref, c, 0) for c in range(5)]))
            ghost = [gk_ref[rows8(c * ROWS + row), :] for c in range(5)]
            solid = solid_ref[rows8(row), :]
            lower, upper = children(x, s)
            moments = Moments()
            within(moments, lower, upper, (0, 1, 2))

            before = [
                tuple(pv_ref[pl.ds((n * 7 + q) * 8, 8), :] for q in range(7)) for n in range(4)
            ]
            prior = row - PL
            wall_a = [pv_ref[pl.ds((28 + q) * 8, 8), :] for q in range(3)]
            wall_b = wall_sums(x[4], -s[0][4], s[1][4], s[2][4])
            sums = face_sums(before, lower[0], 0)
            sums = walled(sums, 0, solid_ref[rows8(prior), :], solid, wall_a, wall_b)
            used = jnp.where(i > 1, 1.0, 0.0)
            sums = [[used * y for y in part] for part in sums]
            moments.below(0, sums)
            old = [[aw_ref[pl.ds((q * 5 + c) * 8, 8), :] for c in range(5)] for q in range(3)]
            acc_ref[rows8(prior), :] = acc_ref[rows8(prior), :] + jnp.where(
                inside, weighed_sums(sums, *old), 0.0
            )
            for n in range(4):
                for q in range(7):
                    pv_ref[pl.ds((n * 7 + q) * 8, 8), :] = upper[0][n][q]
            for q, y in enumerate(wall_sums(x[4], s[0][4], s[1][4], s[2][4])):
                pv_ref[pl.ds((28 + q) * 8, 8), :] = y

            along(
                moments, 1, 1, lower, upper, x, s, solid,
                lambda y: next_j(y, m), lambda y: last_j(y, m), gone_j,
            )
            along(moments, 2, 2, lower, upper, x, s, solid, next_k, last_k, m["k_last"])
            ends(moments, 2, 2, x, s, ghost, m["k_first"], m["k_last"])

            a = [adj_ref[rows8(c * ROWS + row), :] for c in range(5)]
            t = list(zip(*[around(adj_ref, c, 5) for c in range(5)]))
            acc_ref[rows8(row), :] = jnp.where(inside, moments.weighed(a, t), 0.0)
            for c in range(5):
                aw_ref[pl.ds(c * 8, 8), :] = a[c] + t[0][c]
                aw_ref[pl.ds((5 + c) * 8, 8), :] = t[1][c]
                aw_ref[pl.ds((10 + c) * 8, 8), :] = t[2][c]
            return 0

        for q in range(3):
            pv_ref[pl.ds((28 + q) * 8, 8), :] = jnp.zeros((8, LANES), jnp.float32)
        lax.fori_loop(1, EDGE - 1, plane, 0, unroll=2)
        return 0

    lax.fori_loop(0, 3, column, 0)


def rim_kernel(
    index_ref, got_ref, px_ref, pg_ref, ps_ref, solid_ref, acc_ref, out_ref,
    gl_ref, tg_ref, pm_ref, total_ref,
):
    columns = one_hot(index_ref[pl.ds(144, FACES), :], 4 * PEERS)
    parts = fetched(
        columns,
        [
            jnp.concatenate(
                [got_ref[pl.ds(c * 4 + q, PEERS, stride=40), :] for q in range(4)], axis=0
            )
            for c in range(10)
        ],
    )
    for c in range(10):
        y = widened(parts[c], index_ref[pl.ds(0, FACES), :])
        for f in range(4):
            gl_ref[pl.ds((f * 10 + c) * PL, PL), :] = y[f * PL : (f + 1) * PL]

    for c in range(10):
        for g in range(3):
            low, high = (gl_ref[rows8((f * 10 + c) * PL + g * 8), :] for f in (2, 3))
            for at, i in enumerate((0, 1, EDGE - 1, EDGE - 2)):
                tg_ref[rows8((at * 10 + c) * PL + g * 8), :] = spread_j(low, high, i)
    m = masks()

    def boundary(n):
        axes = (n, 1 - n, 2)

        def one(at, _):
            side, g8 = at // 3, at % 3 * 8
            flip = jnp.where(side == 0, 1.0, -1.0)

            def load(ref, first):
                out = []
                for c in range(10):
                    y = ref[rows8((first + c) * PL + g8), :]
                    out.append(flip * y if c % 5 == n + 1 else y)
                return out

            place = n * 2 + side
            x = [load(px_ref, (place * 3 + depth) * 10) for depth in range(3)]
            outer = load(gl_ref, place * 10)
            gk = [load(pg_ref, (place * 2 + depth) * 10) for depth in range(2)]
            if n == 0:
                gt = [load(tg_ref, (side * 2 + depth) * 10) for depth in range(2)]
            else:
                gt = [[None] * 10] * 2
            solid = [ps_ref[rows8((place * 2 + depth) * PL + g8), :] for depth in range(2)]
            s0 = list(
                zip(*[slopes_of(outer[c], x[0][c], x[1][c], gt[0][c], gk[0][c], m) for c in range(10)])
            )
            s1 = list(
                zip(*[slopes_of(x[0][c], x[1][c], x[2][c], gt[1][c], gk[1][c], m) for c in range(10)])
            )
            flow, adj = x[0][:5], x[0][5:]
            s, t = [y[:5] for y in s0], [y[5:] for y in s0]
            lower, upper = children(flow, s)
            moments = Moments()
            within(moments, lower, upper, axes)
            moments.below(0, face_sums([state(outer[:5])] * 4, lower[0], n))

            flow1, adj1 = x[1][:5], x[1][5:]
            f1, t1 = [y[:5] for y in s1], [y[5:] for y in s1]
            sums = face_sums(
                upper[0], four([a - b for a, b in zip(flow1, f1[0])], f1[1], f1[2]), n
            )
            sums = walled(
                sums,
                n,
                solid[0],
                solid[1],
                wall_sums(flow[4], s[0][4], s[1][4], s[2][4]),
                wall_sums(flow1[4], -f1[0][4], f1[1][4], f1[2][4]),
            )
            moments.above(0, sums)
            next_total = -weighed_sums(
                sums, [a - b for a, b in zip(adj1, t1[0])], t1[1], t1[2]
            )

            gone = m["j_last"]
            if n == 1:
                gone = gone | m["j_first"] | m["j_penult"]
            along(
                moments, 1, axes[1], lower, upper, flow, s, solid[0],
                lambda y: next_j(y, m), lambda y: last_j(y, m), gone,
            )
            if n == 0:
                ends(moments, 1, axes[1], flow, s, gt[0][:5], m["j_first"], m["j_last"])
            along(moments, 2, 2, lower, upper, flow, s, solid[0], next_k, last_k, m["k_last"])
            ends(moments, 2, 2, flow, s, gk[0][:5], m["k_first"], m["k_last"])
            total = moments.weighed(adj, t)
            if n == 1:
                kept = ~(m["j_first"] | m["j_last"])
                total = jnp.where(kept, total, 0.0)
                next_total = jnp.where(kept, next_total, 0.0)
            pm_ref[rows8(place * 2 * PL + g8), :] = total
            pm_ref[rows8((place * 2 + 1) * PL + g8), :] = next_total
            return 0

        lax.fori_loop(0, 6, one, 0)

    boundary(0)
    boundary(1)

    low, even = lane() // EDGE, even_row()
    for g in range(3):
        planes = [[pm_ref[pl.ds((p * 2 + d) * PL + g * 8, 8), :] for d in range(2)] for p in range(4)]
        near = [planes[2], [rolled(y, -1, 0) for y in planes[2]]]
        far = [[rolled(y, 1, 0) for y in planes[3]], planes[3]]
        for i in range(EDGE):
            ih, il = i // 8, i % 8
            a, c = near[ih], far[ih]
            extra = jnp.where(
                even,
                jnp.where(
                    low == 0,
                    rolled(a[0], -16 * il),
                    jnp.where(low == 1, rolled(a[1], 16 - 16 * il), 0.0),
                ),
                jnp.where(
                    low == 7,
                    rolled(c[0], 112 - 16 * il),
                    jnp.where(low == 6, rolled(c[1], 96 - 16 * il), 0.0),
                ),
            )
            at = pl.ds(i * PL + g * 8, 8)
            total = acc_ref[at, :] + extra
            if i < 2:
                total = total + planes[0][i]
            elif i > EDGE - 3:
                total = total + planes[1][EDGE - 1 - i]
            total_ref[at, :] = jnp.where(solid_ref[at, :] > 0.5, 0.0, jnp.abs(total))
    for t in range(2 * EDGE):
        i, jh = divmod(t, 2)
        out_ref[:, pl.ds(t * LANES, LANES)] = total_ref[pl.ds(i * PL + jh, NB, stride=2), :]


def shape(*dims):
    return jax.ShapeDtypeStruct(dims, jnp.float32)


def scratch(*rows):
    return [pltpu.VMEM((r, LANES), jnp.float32) for r in rows]


SMEM = pl.BlockSpec(memory_space=pltpu.SMEM)
VMEM = pl.BlockSpec(memory_space=pltpu.VMEM)
PARAMS = pltpu.CompilerParams(vmem_limit_bytes=VMEM_LIMIT)


def prep(flow, adjoint, cut_flag, own, vertical):
    return pl.pallas_call(
        prep_kernel,
        out_shape=[
            shape(5 * ROWS, LANES),
            shape(5 * ROWS, LANES),
            shape(ROWS, LANES),
            shape(10 * FACES, LANES),
            shape(10 * PL, LANES),
            shape(10 * PL, LANES),
            jax.ShapeDtypeStruct((288, LANES), jnp.int32),
        ],
        in_specs=[VMEM] * 5,
        out_specs=[VMEM] * 7,
        cost_estimate=pl.CostEstimate(flops=10**8, bytes_accessed=3 * 10**7, transcendentals=0),
        compiler_params=PARAMS,
    )(flow.transpose(1, 0, 2), adjoint.transpose(1, 0, 2), cut_flag[None], own, vertical)


def reply(me, asked, layers):
    return pl.pallas_call(
        reply_kernel,
        out_shape=shape(40 * PEERS, LANES),
        in_specs=[SMEM, VMEM, VMEM],
        out_specs=VMEM,
        compiler_params=PARAMS,
    )(me, asked, layers)


def inner(edge, index, prim, adj, solid, low, high):
    return pl.pallas_call(
        inner_kernel,
        out_shape=[shape(n, LANES) for n in (ROWS, 120 * PL, 80 * PL, 8 * PL)],
        in_specs=[SMEM] + [VMEM] * 6,
        out_specs=[VMEM] * 4,
        scratch_shapes=scratch(20 * PL, 10 * ROWS, 31 * 8, 15 * 8),
        compiler_params=PARAMS,
    )(edge, index, prim, adj, solid, low, high)


def rim(index, got, planes, ghosts, walls, solid, acc):
    return pl.pallas_call(
        rim_kernel,
        out_shape=shape(NB, EDGE * EDGE * EDGE),
        in_specs=[VMEM] * 7,
        out_specs=VMEM,
        scratch_shapes=scratch(40 * PL, 40 * PL, 8 * PL, ROWS),
        compiler_params=PARAMS,
    )(index, got, planes, ghosts, walls, solid, acc)


def ask_kernel(owner_ref, link_ref, own_ref, out_ref):
    link = link_ref[...]
    slot = (link.astype(jnp.float32) * 0.2 + 0.05).astype(jnp.int32)
    far = lax.broadcasted_iota(jnp.int32, link.shape, 0) ^ 1
    own = (owner_ref[...] * 64 + slot * 4 + far) * 8 + (link - 5 * slot)
    own_ref[...] = own
    at = lax.broadcasted_iota(jnp.int32, (NB, LANES), 0)
    spot = lax.broadcasted_iota(jnp.int32, (NB, LANES), 1)
    row = jnp.full((1, LANES), -1.0, jnp.float32)
    for f in range(4):
        spread = jnp.dot(
            own[f : f + 1].astype(jnp.float32) + 1.0,
            jnp.where(spot == at + f * NB, 1.0, 0.0),
            precision=lax.Precision.HIGHEST,
            preferred_element_type=jnp.float32,
        )
        row = row + spread
    row = (row + jnp.where(row < 0.0, -0.25, 0.25)).astype(jnp.int32)
    out_ref[...] = jnp.broadcast_to(row, out_ref.shape)


def ask(lateral_owner, lateral_link):
    return pl.pallas_call(
        ask_kernel,
        out_shape=[
            jax.ShapeDtypeStruct((4, NB), jnp.int32),
            jax.ShapeDtypeStruct((PEERS, LANES), jnp.int32),
        ],
        in_specs=[VMEM] * 2,
        out_specs=[VMEM] * 2,
        compiler_params=PARAMS,
    )(lateral_owner[:, :, 0].T, lateral_link.T)


def exchange(block, axis):
    chunks = block.reshape(PEERS, -1, LANES)
    out = lax.all_to_all(chunks, axis, split_axis=0, concat_axis=0, tiled=True)
    return out.reshape(-1, LANES)


def local(flow, adjoint, cut_flag, lateral_owner, lateral_link, vertical_link):
    own, questions = ask(lateral_owner, lateral_link)
    asked = exchange(questions, "blk")
    prim, adj, solid, layers, low_face, high_face, index = prep(
        flow, adjoint, cut_flag, own, vertical_link.T
    )
    asked, low_face, high_face = lax.optimization_barrier((asked, low_face, high_face))
    regions = lax.axis_size("grp")
    region = lax.axis_index("grp")
    low = lax.ppermute(high_face, "grp", [(r, r + 1) for r in range(regions - 1)])
    high = lax.ppermute(low_face, "grp", [(r + 1, r) for r in range(regions - 1)])
    me = lax.axis_index("blk").astype(jnp.int32).reshape(1)
    replies = reply(me, asked, layers)
    replies, low, high = lax.optimization_barrier((replies, low, high))
    got = exchange(replies, "blk")
    edge = jnp.stack([region == 0, region == regions - 1]).astype(jnp.int32)
    acc, planes, ghosts, walls = inner(edge, index, prim, adj, solid, low, high)
    return rim(index, got, planes, ghosts, walls, solid, acc)


def solution(mesh):
    in_specs = (
        P(("blk", "grp"), None, None),
        P(("blk", "grp"), None, None),
        P(("blk", "grp"), None),
        P(("blk", "grp"), None, None),
        P(("blk", "grp"), None),
        P(("blk", "grp"), None),
    )
    out_specs = P(("blk", "grp"), None)
    return jax.shard_map(local, mesh=mesh, in_specs=in_specs, out_specs=out_specs, check_vma=False)
```

```python
import math

import jax
import jax.numpy as jnp
from jax import lax
from jax.experimental import pallas as pl
from jax.experimental.pallas import tpu as pltpu
from jax.sharding import PartitionSpec as P

EDGE = 16
NB = 12
PL = 2 * NB
ROWS = EDGE * PL
LANES = 128
PEERS = 64
REGIONS = 4
FACES = 4 * PL
PXR = (EDGE + 2) * PL
MR = (EDGE + 1) * PL

VEL = math.sqrt(0.2)
PRESS = 0.2
WEIGHTS = (1.0 / VEL, 5.0, 5.0, 5.0, 2.5 / VEL)
FARFIELD = (1.0, 0.0, 0.0, 0.3 * VEL, PRESS)
KNEE = 0.4 / math.sqrt(5.0)
START = 1.2 / math.sqrt(5.0)
CURVE = 1.25 * math.sqrt(5.0)

VMEM_LIMIT = 56 * 2**20


def lane():
    return lax.broadcasted_iota(jnp.int32, (8, LANES), 1)


def even_row():
    return lax.broadcasted_iota(jnp.int32, (8, LANES), 0) % 2 == 0


def rolled(x, amount, axis=1):
    size = x.shape[axis]
    amount = amount % size
    return x if amount == 0 else pltpu.roll(x, amount, axis)


def rows8(start):
    if isinstance(start, int):
        return pl.ds(start, 8)
    return pl.ds(pl.multiple_of(start, 8), 8)


def compact_k(load):
    depth = lane() % EDGE
    low = high = None
    for i in range(EDGE):
        x = rolled(load(i), i)
        low = x if low is None else jnp.where(depth == i, x, low)
        high = x if high is None else jnp.where(depth == (i + 15) % EDGE, x, high)
    return low, rolled(high, -15)


def compact_depths(load, count):
    low = lane() // EDGE
    spots = list(range(count)) + [7 - n for n in range(count)]
    halves = []
    for ih in range(2):
        totals = [None] * len(spots)
        for il in range(8):
            x = rolled(load(ih * 8 + il), 16 * il)
            for n, spot in enumerate(spots):
                t = totals[n]
                totals[n] = x if t is None else jnp.where(low == (spot + il) % 8, x, t)
        halves.append(totals)
    even = even_row()
    near = [jnp.where(even, a, rolled(c, 1, 0)) for a, c in zip(halves[0][:count], halves[1][:count])]
    far = [jnp.where(even, rolled(a, -1, 0), c) for a, c in zip(halves[0][count:], halves[1][count:])]
    out = [rolled(t, -16 * spot) for t, spot in zip(near + far, spots)]
    return out[:count], out[count:]


def spread_j(low, high, i):
    ih, il = i // 8, i % 8
    a = low if ih == 0 else rolled(low, -1, 0)
    c = rolled(high, 1, 0) if ih == 0 else high
    return jnp.where(even_row(), rolled(a, -16 * il), rolled(c, 16 * (7 - il)))


def spread_k(low, high, i):
    return jnp.where(lane() % EDGE == 0, rolled(low, -i), rolled(high, 15 - i))


def column_of(packed, rows, width):
    at = lax.broadcasted_iota(jnp.int32, (rows, width), 0) // 2
    spot = lax.broadcasted_iota(jnp.int32, (rows, width), 1)
    return jnp.sum(jnp.where(at == spot, packed, 0.0), axis=1, keepdims=True)


def index_tables(own, vertical, index_ref):
    spots = lax.broadcasted_iota(jnp.int32, (PL, LANES), 1)
    half = lax.broadcasted_iota(jnp.int32, (PL, LANES), 0) % 2
    low, depth = spots // EDGE, spots % EDGE
    wide = (4 * half + low // 2) * EDGE + depth // 2

    def store(f, code, row_part, col_part, base, step):
        full = code == 4
        index_ref[pl.ds(f * PL, PL), :] = jnp.where(full, spots, wide + 8 * col_part)
        index_ref[pl.ds(144 + f * PL, PL), :] = base + step * jnp.where(full, half, row_part)

    at = lax.broadcasted_iota(jnp.int32, (PL, NB), 0) // 2
    spot = lax.broadcasted_iota(jnp.int32, (PL, NB), 1)
    entries = [own[f : f + 1, :].astype(jnp.int32) for f in range(4)]
    holders = [e >> 9 for e in entries]
    for f in range(4):
        value = column_of(own[f : f + 1, :], PL, NB).astype(jnp.int32)
        owner, code = value >> 9, value & 7
        rank = jnp.zeros((PL, 1), jnp.float32)
        for other in range(f + 1):
            same = holders[other] == owner
            if other == f:
                same = same & (spot < at)
            rank = rank + jnp.sum(jnp.where(same, 1.0, 0.0), axis=1, keepdims=True)
        rank = rank.astype(jnp.int32)
        store(f, code, code >> 1, code & 1, rank * 2 * PEERS + owner, PEERS)
    for side in range(2):
        value = column_of(vertical[side : side + 1, :], PL, NB).astype(jnp.int32)
        slot = (value.astype(jnp.float32) * 0.2 + 0.05).astype(jnp.int32)
        code = value - 5 * slot
        store(4 + side, code, code & 1, code >> 1, slot * 2, 1)


def prep_kernel(
    flow_ref, adj_ref, flag_ref, own_ref, vertical_ref,
    prim_ref, adjl_ref, solid_ref, lat_ref, low_ref, high_ref, index_ref,
):
    def relaid(ref, c, out_ref):
        for t in range(2 * EDGE):
            i, jh = divmod(t, 2)
            part = ref[c, :, pl.ds(t * LANES, LANES)]
            out_ref[pl.ds(i * PL + jh + c * ROWS, NB, stride=2), :] = part.astype(jnp.float32)

    for c in range(5):
        relaid(flow_ref, c, prim_ref)
        relaid(adj_ref, c, adjl_ref)
    relaid(flag_ref, 0, solid_ref)
    index_tables(
        own_ref[...].astype(jnp.float32), vertical_ref[...].astype(jnp.float32), index_ref
    )

    def convert(n, _):
        at = [pl.ds(pl.multiple_of(c * ROWS + n * 64, 64), 64) for c in range(5)]
        rho = prim_ref[at[0]]
        inv = 1.0 / rho
        vel = [prim_ref[at[c]] * inv for c in (1, 2, 3)]
        square = vel[0] * vel[0] + vel[1] * vel[1] + vel[2] * vel[2]
        prim_ref[at[4]] = (0.4 * PRESS) * (prim_ref[at[4]] - 0.5 * rho * square)
        for c in range(3):
            prim_ref[at[c + 1]] = vel[c] * VEL
        return 0

    lax.fori_loop(0, ROWS // 64, convert, 0)

    def layers(ref, first):
        def one(c, _):
            for g in range(3):

                def load(i):
                    return ref[rows8(c * ROWS + i * PL + g * 8), :]

                out = (c + first) * FACES + g * 8
                lat_ref[rows8(out), :] = load(0)
                lat_ref[rows8(out + PL), :] = load(EDGE - 1)
                near, far = compact_depths(load, 1)
                lat_ref[rows8(out + 2 * PL), :] = near[0]
                lat_ref[rows8(out + 3 * PL), :] = far[0]
                low, high = compact_k(load)
                low_ref[rows8((c + first) * PL + g * 8), :] = low
                high_ref[rows8((c + first) * PL + g * 8), :] = high
            return 0

        lax.fori_loop(0, 5, one, 0)

    layers(prim_ref, 0)
    layers(adjl_ref, 5)


def reply_kernel(me_ref, asked_ref, lat_ref, out_ref):
    before = lax.broadcasted_iota(jnp.int32, (LANES, LANES), 0) < lax.broadcasted_iota(
        jnp.int32, (LANES, LANES), 1
    )
    asked = asked_ref[...]
    match = (asked >> 9) == me_ref[0]
    rank = jnp.dot(
        jnp.where(match, 1.0, 0.0),
        jnp.where(before, 1.0, 0.0),
        preferred_element_type=jnp.float32,
    )
    face = (asked >> 3) & 63
    target = (((face & 3) * PL) + ((face >> 2) * 2)).astype(jnp.float32) + 10.0
    column = lax.broadcasted_iota(jnp.int32, (PEERS, FACES), 1).astype(jnp.float32)
    picks = []
    for s in range(2):
        mine = match & (rank > s - 0.5) & (rank < s + 0.5)
        row = jnp.sum(jnp.where(mine, target, 0.0), axis=1, keepdims=True) - 10.0
        for h in range(2):
            picks.append(jnp.where(column == row + float(h), 1.0, 0.0))
    picks = jnp.concatenate(picks, axis=0)
    for c in range(10):
        out = jnp.dot(
            picks,
            lat_ref[pl.ds(c * FACES, FACES), :],
            precision=lax.Precision.HIGHEST,
            preferred_element_type=jnp.float32,
        )
        for q in range(4):
            out_ref[pl.ds(c * 4 + q, PEERS, stride=40), :] = out[q * PEERS : (q + 1) * PEERS]


def one_hot(columns, width):
    parts = []
    for start in range(0, width, LANES):
        parts.append(
            jnp.where(
                columns == lax.broadcasted_iota(jnp.int32, columns.shape, 1) + start, 1.0, 0.0
            )
        )
    return parts[0] if len(parts) == 1 else jnp.concatenate(parts, axis=1)


def widened(x, index):
    parts = [
        jnp.take_along_axis(
            x[n : n + 8], index[n : n + 8], axis=1, mode="promise_in_bounds"
        )
        for n in range(0, x.shape[0], 8)
    ]
    return jnp.concatenate(parts, axis=0)


def fetched(columns, parts):
    y = jnp.dot(
        columns,
        jnp.concatenate(parts, axis=1),
        precision=lax.Precision.HIGHEST,
        preferred_element_type=jnp.float32,
    )
    return [y[:, n * LANES : (n + 1) * LANES] for n in range(len(parts))]


def minmod(a, c):
    return jnp.maximum(jnp.minimum(a, jnp.maximum(c, 0.0)), jnp.minimum(c, 0.0))


def masks():
    low, depth, even = lane() // EDGE, lane() % EDGE, even_row()
    return dict(
        k_last=depth == EDGE - 1,
        k_first=depth == 0,
        j_wrap=low == 7,
        j_back=low == 0,
        j_last=(low == 7) & ~even,
        j_first=(low == 0) & even,
        j_penult=(low == 6) & ~even,
    )


def next_k(x):
    return rolled(x, -1)


def last_k(x):
    return rolled(x, 1)


def next_j(x, m):
    r = rolled(x, -16)
    return jnp.where(m["j_wrap"], rolled(r, -1, 0), r)


def last_j(x, m):
    r = rolled(x, 16)
    return jnp.where(m["j_back"], rolled(r, 1, 0), r)


def slopes_of(below, x, above, gt, gk, m):
    out = [0.25 * minmod(above - x, x - below)]
    gt = x if gt is None else gt
    up = jnp.where(m["j_last"], gt, next_j(x, m))
    down = jnp.where(m["j_first"], gt, last_j(x, m))
    out.append(0.25 * minmod(up - x, x - down))
    up = jnp.where(m["k_last"], gk, next_k(x))
    down = jnp.where(m["k_first"], gk, last_k(x))
    out.append(0.25 * minmod(up - x, x - down))
    return out


def state(q):
    rho, u, v, w, p = q
    rs = lax.rsqrt(rho)
    enth = 7.0 * p * (rs * rs) + (u * u + v * v + w * w)
    return (rho, u, v, w, p, rho * rs, enth)


def four(base, first, second):
    out = []
    for a in (-1, 1):
        half = [x + s if a > 0 else x - s for x, s in zip(base, first)]
        for e in (-1, 1):
            out.append(state([x + s if e > 0 else x - s for x, s in zip(half, second)]))
    return out


def roe(left, right, axis):
    n = 1 + axis
    weight = right[5] * pl.reciprocal(left[5] + right[5], approx=True)
    jump = right[n] - left[n]
    mean = [None] * 4
    for c in (1, 2, 3):
        d = jump if c == n else right[c] - left[c]
        mean[c] = left[c] + weight * d
    enth = left[6] + weight * (right[6] - left[6])
    c2 = enth - (mean[1] * mean[1] + mean[2] * mean[2] + mean[3] * mean[3])
    rc = lax.rsqrt(c2)
    un = mean[n]
    ahead = un > 0.0
    sign = jnp.where(ahead, VEL, -VEL)
    b = jnp.maximum(START - jnp.abs(un) * rc, 0.0)
    s = jnp.minimum(b, KNEE)
    speed = 2.5 * b - s * (2.5 - (2.5 * CURVE) * s)
    wave = speed * ((right[4] - left[4]) * rc - sign * (left[5] * right[5] * jump))
    sc = sign * (c2 * rc)
    up = [jnp.where(ahead, left[c], right[c]) for c in (0, 1, 2, 3, 4, 6)]
    mass = up[0] * up[n]
    t = un * sc
    flux = [mass - wave]
    for c in (1, 2, 3):
        if c == n:
            flux.append((mass * up[c] + up[4]) - wave * (mean[c] - sc))
        else:
            flux.append(mass * up[c] - wave * mean[c])
    flux.append(mass * up[5] - wave * (enth - t - t))
    return flux


def face_sums(lefts, rights, axis):
    f = [roe(a, c, axis) for a, c in zip(lefts, rights)]
    plain, first, second = [], [], []
    for c in range(5):
        lo, hi = f[0][c] + f[1][c], f[2][c] + f[3][c]
        dlo, dhi = f[1][c] - f[0][c], f[3][c] - f[2][c]
        plain.append(lo + hi)
        first.append(hi - lo)
        second.append(dlo + dhi)
    return plain, first, second


def plain_sum(lefts, rights, axis):
    f = [roe(a, c, axis) for a, c in zip(lefts, rights)]
    return [(f[0][c] + f[1][c]) + (f[2][c] + f[3][c]) for c in range(5)]


def walled(sums, axis, solid_a, solid_b, wall_a, wall_b, gone=None):
    from_a = (solid_b > 0.5) & (solid_a < 0.5)
    from_b = (solid_a > 0.5) & (solid_b < 0.5)
    dead = from_a | from_b
    if gone is not None:
        dead = dead | gone
    out = []
    for part, pa, pb in zip(sums, wall_a, wall_b):
        new = []
        for c in range(5):
            if c == axis + 1:
                value = jnp.where(from_a, pa, jnp.where(from_b, pb, part[c]))
                new.append(value if gone is None else jnp.where(gone, 0.0, value))
            else:
                new.append(jnp.where(dead, 0.0, part[c]))
        out.append(new)
    return out


def wall_sums(p, normal, first, second):
    return (4.0 * (p + normal), 4.0 * first, 4.0 * second)


TANGENTS = ((1, 2), (0, 2), (0, 1))


class Moments:
    def __init__(self):
        self.value = [[None] * 5 for _ in range(4)]

    def add(self, k, part, sign):
        for c in range(5):
            old = self.value[k][c]
            if old is None:
                self.value[k][c] = part[c] if sign > 0 else -part[c]
            else:
                self.value[k][c] = old + part[c] if sign > 0 else old - part[c]

    def below(self, d, sums):
        self.add(0, sums[0], -1)
        self.add(d + 1, sums[0], 1)
        for t, part in zip(TANGENTS[d], sums[1:]):
            self.add(t + 1, part, -1)

    def above(self, d, sums):
        self.add(0, sums[0], 1)
        self.add(d + 1, sums[0], 1)
        for t, part in zip(TANGENTS[d], sums[1:]):
            self.add(t + 1, part, 1)

    def weighed(self, adj, slopes):
        total = None
        for c in range(5):
            part = adj[c] * self.value[0][c]
            for d in range(3):
                part = part + slopes[d][c] * self.value[d + 1][c]
            total = WEIGHTS[c] * part if total is None else total + WEIGHTS[c] * part
        return total


def weighed_sums(sums, normal, first, second):
    total = None
    for c in range(5):
        part = WEIGHTS[c] * (normal[c] * sums[0][c] + first[c] * sums[1][c] + second[c] * sums[2][c])
        total = part if total is None else total + part
    return total


def children(x, s):
    child = [
        four([a + b if up else a - b for a, b in zip(x, s[0])], s[1], s[2]) for up in (False, True)
    ]
    lower = [
        child[0],
        [child[0][0], child[0][1], child[1][0], child[1][1]],
        [child[0][0], child[0][2], child[1][0], child[1][2]],
    ]
    upper = [
        child[1],
        [child[0][2], child[0][3], child[1][2], child[1][3]],
        [child[0][1], child[0][3], child[1][1], child[1][3]],
    ]
    return lower, upper


def within(moments, lower, upper, axes):
    for d in range(3):
        inner = plain_sum(lower[d], upper[d], axes[d])
        moments.add(d + 1, [y + y for y in inner], -1)


def along(moments, d, axis, lower, upper, x, s, solid, ahead, back, gone):
    sums = face_sums(upper[d], [tuple(ahead(y) for y in st) for st in lower[d]], axis)
    t0, t1 = TANGENTS[d]
    wall_a = wall_sums(x[4], s[d][4], s[t0][4], s[t1][4])
    wall_b = [ahead(y) for y in wall_sums(x[4], -s[d][4], s[t0][4], s[t1][4])]
    sums = walled(sums, axis, solid, ahead(solid), wall_a, wall_b, gone)
    moments.above(d, sums)
    moments.below(d, [[back(y) for y in part] for part in sums])


def ends(moments, d, axis, x, s, ghost, first, last):
    n = axis + 1
    flip = jnp.where(first, -1.0, 1.0)
    base = [a + flip * b for a, b in zip(x, s[d])]
    t0, t1 = TANGENTS[d]
    f0, f1, g = list(s[t0]), list(s[t1]), list(ghost)
    for part in (base, f0, f1, g):
        part[n] = flip * part[n]
    sums = face_sums(four(base, f0, f1), [state(g)] * 4, axis)
    shown = first | last
    sums = [
        [jnp.where(shown, flip * y if c == n else y, 0.0) for c, y in enumerate(part)] for part in sums
    ]
    moments.add(0, sums[0], 1)
    moments.add(d + 1, [flip * y for y in sums[0]], 1)
    moments.add(t0 + 1, sums[1], 1)
    moments.add(t1 + 1, sums[2], 1)


def inner_kernel(
    edge_ref, index_ref, prim_ref, adj_ref, solid_ref, low_ref, high_ref,
    acc_ref, px_ref, pg_ref, ps_ref,
    v_ref, gk_ref, pv_ref, aw_ref,
):
    for side in range(2):
        ref = (low_ref, high_ref)[side]
        columns = one_hot(index_ref[pl.ds(240 + side * PL, PL), :], LANES)[:, :PL]
        parts = fetched(columns, [ref[pl.ds(c * PL, PL), :] for c in range(10)])
        for c in range(10):
            y = widened(parts[c], index_ref[pl.ds(FACES + side * PL, PL), :])
            far = FARFIELD[c] if c < 5 else 0.0
            v_ref[pl.ds((side * 10 + c) * PL, PL), :] = jnp.where(
                edge_ref[0] == side * (REGIONS - 1), jnp.full_like(y, far), y
            )

    def spread(c, _):
        for g in range(3):
            low, high = (v_ref[rows8((side * 10 + c) * PL + g * 8), :] for side in range(2))
            for i in range(EDGE):
                gk_ref[rows8(c * ROWS + i * PL + g * 8), :] = spread_k(low, high, i)
        return 0

    lax.fori_loop(0, 10, spread, 0)

    def packed(load, out_ref, depth, first, step, g):
        planes = [[load(n) for n in range(depth)], [load(EDGE - 1 - n) for n in range(depth)]]
        for n, sides in enumerate((planes, compact_depths(load, depth))):
            for side in range(2):
                for at in range(depth):
                    row = (((n * 2 + side) * depth + at) * step + first) * PL + g * 8
                    out_ref[rows8(row), :] = sides[side][at]

    def pack(c, _):
        for g in range(3):

            def load_of(ref, first):
                return lambda i: ref[rows8((c + first) * ROWS + i * PL + g * 8), :]

            packed(load_of(prim_ref, 0), px_ref, 3, c, 10, g)
            packed(load_of(adj_ref, 0), px_ref, 3, c + 5, 10, g)
            packed(load_of(gk_ref, 0), pg_ref, 2, c, 10, g)
            packed(load_of(gk_ref, 5), pg_ref, 2, c + 5, 10, g)
        return 0

    lax.fori_loop(0, 5, pack, 0)
    for g in range(3):
        packed(lambda i: solid_ref[pl.ds(i * PL + g * 8, 8), :], ps_ref, 2, 0, 1, g)

    m = masks()
    inside = ~(m["j_first"] | m["j_last"])
    gone_j = m["j_first"] | m["j_last"] | m["j_penult"]
    for i in (0, EDGE - 1):
        acc_ref[pl.ds(i * PL, PL), :] = jnp.zeros((PL, LANES), jnp.float32)

    def column(g, _):
        g8 = g * 8
        start = state([jnp.full((8, LANES), y, jnp.float32) for y in (1.0, 0.0, 0.0, 0.0, 0.2)])
        for n in range(4):
            for q in range(7):
                pv_ref[pl.ds((n * 7 + q) * 8, 8), :] = start[q]
        aw_ref[...] = jnp.zeros_like(aw_ref)

        def plane(i, _):
            row = i * PL + g8

            def around(ref, c, first):
                at = c * ROWS + row
                return slopes_of(
                    ref[rows8(at - PL), :],
                    ref[rows8(at), :],
                    ref[rows8(at + PL), :],
                    None,
                    gk_ref[rows8((c + first) * ROWS + row), :],
                    m,
                )

            x = [prim_ref[rows8(c * ROWS + row), :] for c in range(5)]
            s = list(zip(*[around(prim_ref, c, 0) for c in range(5)]))
            ghost = [gk_ref[rows8(c * ROWS + row), :] for c in range(5)]
            solid = solid_ref[rows8(row), :]
            lower, upper = children(x, s)
            moments = Moments()
            within(moments, lower, upper, (0, 1, 2))

            before = [
                tuple(pv_ref[pl.ds((n * 7 + q) * 8, 8), :] for q in range(7)) for n in range(4)
            ]
            prior = row - PL
            wall_a = [pv_ref[pl.ds((28 + q) * 8, 8), :] for q in range(3)]
            wall_b = wall_sums(x[4], -s[0][4], s[1][4], s[2][4])
            sums = face_sums(before, lower[0], 0)
            sums = walled(sums, 0, solid_ref[rows8(prior), :], solid, wall_a, wall_b)
            used = jnp.where(i > 1, 1.0, 0.0)
            sums = [[used * y for y in part] for part in sums]
            moments.below(0, sums)
            old = [[aw_ref[pl.ds((q * 5 + c) * 8, 8), :] for c in range(5)] for q in range(3)]
            acc_ref[rows8(prior), :] = acc_ref[rows8(prior), :] + jnp.where(
                inside, weighed_sums(sums, *old), 0.0
            )
            for n in range(4):
                for q in range(7):
                    pv_ref[pl.ds((n * 7 + q) * 8, 8), :] = upper[0][n][q]
            for q, y in enumerate(wall_sums(x[4], s[0][4], s[1][4], s[2][4])):
                pv_ref[pl.ds((28 + q) * 8, 8), :] = y

            along(
                moments, 1, 1, lower, upper, x, s, solid,
                lambda y: next_j(y, m), lambda y: last_j(y, m), gone_j,
            )
            along(moments, 2, 2, lower, upper, x, s, solid, next_k, last_k, m["k_last"])
            ends(moments, 2, 2, x, s, ghost, m["k_first"], m["k_last"])

            a = [adj_ref[rows8(c * ROWS + row), :] for c in range(5)]
            t = list(zip(*[around(adj_ref, c, 5) for c in range(5)]))
            acc_ref[rows8(row), :] = jnp.where(inside, moments.weighed(a, t), 0.0)
            for c in range(5):
                aw_ref[pl.ds(c * 8, 8), :] = a[c] + t[0][c]
                aw_ref[pl.ds((5 + c) * 8, 8), :] = t[1][c]
                aw_ref[pl.ds((10 + c) * 8, 8), :] = t[2][c]
            return 0

        for q in range(3):
            pv_ref[pl.ds((28 + q) * 8, 8), :] = jnp.zeros((8, LANES), jnp.float32)
        lax.fori_loop(1, EDGE - 1, plane, 0, unroll=2)
        return 0

    lax.fori_loop(0, 3, column, 0)


def rim_kernel(
    index_ref, got_ref, px_ref, pg_ref, ps_ref, solid_ref, acc_ref, out_ref,
    gl_ref, tg_ref, pm_ref, total_ref,
):
    columns = one_hot(index_ref[pl.ds(144, FACES), :], 4 * PEERS)
    parts = fetched(
        columns,
        [
            jnp.concatenate(
                [got_ref[pl.ds(c * 4 + q, PEERS, stride=40), :] for q in range(4)], axis=0
            )
            for c in range(10)
        ],
    )
    for c in range(10):
        y = widened(parts[c], index_ref[pl.ds(0, FACES), :])
        for f in range(4):
            gl_ref[pl.ds((f * 10 + c) * PL, PL), :] = y[f * PL : (f + 1) * PL]

    for c in range(10):
        for g in range(3):
            low, high = (gl_ref[rows8((f * 10 + c) * PL + g * 8), :] for f in (2, 3))
            for at, i in enumerate((0, 1, EDGE - 1, EDGE - 2)):
                tg_ref[rows8((at * 10 + c) * PL + g * 8), :] = spread_j(low, high, i)
    m = masks()

    def boundary(n):
        axes = (n, 1 - n, 2)

        def one(at, _):
            side, g8 = at // 3, at % 3 * 8
            flip = jnp.where(side == 0, 1.0, -1.0)

            def load(ref, first):
                out = []
                for c in range(10):
                    y = ref[rows8((first + c) * PL + g8), :]
                    out.append(flip * y if c % 5 == n + 1 else y)
                return out

            place = n * 2 + side
            x = [load(px_ref, (place * 3 + depth) * 10) for depth in range(3)]
            outer = load(gl_ref, place * 10)
            gk = [load(pg_ref, (place * 2 + depth) * 10) for depth in range(2)]
            if n == 0:
                gt = [load(tg_ref, (side * 2 + depth) * 10) for depth in range(2)]
            else:
                gt = [[None] * 10] * 2
            solid = [ps_ref[rows8((place * 2 + depth) * PL + g8), :] for depth in range(2)]
            s0 = list(
                zip(*[slopes_of(outer[c], x[0][c], x[1][c], gt[0][c], gk[0][c], m) for c in range(10)])
            )
            s1 = list(
                zip(*[slopes_of(x[0][c], x[1][c], x[2][c], gt[1][c], gk[1][c], m) for c in range(10)])
            )
            flow, adj = x[0][:5], x[0][5:]
            s, t = [y[:5] for y in s0], [y[5:] for y in s0]
            lower, upper = children(flow, s)
            moments = Moments()
            within(moments, lower, upper, axes)
            moments.below(0, face_sums([state(outer[:5])] * 4, lower[0], n))

            flow1, adj1 = x[1][:5], x[1][5:]
            f1, t1 = [y[:5] for y in s1], [y[5:] for y in s1]
            sums = face_sums(
                upper[0], four([a - b for a, b in zip(flow1, f1[0])], f1[1], f1[2]), n
            )
            sums = walled(
                sums,
                n,
                solid[0],
                solid[1],
                wall_sums(flow[4], s[0][4], s[1][4], s[2][4]),
                wall_sums(flow1[4], -f1[0][4], f1[1][4], f1[2][4]),
            )
            moments.above(0, sums)
            next_total = -weighed_sums(
                sums, [a - b for a, b in zip(adj1, t1[0])], t1[1], t1[2]
            )

            gone = m["j_last"]
            if n == 1:
                gone = gone | m["j_first"] | m["j_penult"]
            along(
                moments, 1, axes[1], lower, upper, flow, s, solid[0],
                lambda y: next_j(y, m), lambda y: last_j(y, m), gone,
            )
            if n == 0:
                ends(moments, 1, axes[1], flow, s, gt[0][:5], m["j_first"], m["j_last"])
            along(moments, 2, 2, lower, upper, flow, s, solid[0], next_k, last_k, m["k_last"])
            ends(moments, 2, 2, flow, s, gk[0][:5], m["k_first"], m["k_last"])
            total = moments.weighed(adj, t)
            if n == 1:
                kept = ~(m["j_first"] | m["j_last"])
                total = jnp.where(kept, total, 0.0)
                next_total = jnp.where(kept, next_total, 0.0)
            pm_ref[rows8(place * 2 * PL + g8), :] = total
            pm_ref[rows8((place * 2 + 1) * PL + g8), :] = next_total
            return 0

        lax.fori_loop(0, 6, one, 0)

    boundary(0)
    boundary(1)

    low, even = lane() // EDGE, even_row()
    for g in range(3):
        planes = [[pm_ref[pl.ds((p * 2 + d) * PL + g * 8, 8), :] for d in range(2)] for p in range(4)]
        near = [planes[2], [rolled(y, -1, 0) for y in planes[2]]]
        far = [[rolled(y, 1, 0) for y in planes[3]], planes[3]]
        for i in range(EDGE):
            ih, il = i // 8, i % 8
            a, c = near[ih], far[ih]
            extra = jnp.where(
                even,
                jnp.where(
                    low == 0,
                    rolled(a[0], -16 * il),
                    jnp.where(low == 1, rolled(a[1], 16 - 16 * il), 0.0),
                ),
                jnp.where(
                    low == 7,
                    rolled(c[0], 112 - 16 * il),
                    jnp.where(low == 6, rolled(c[1], 96 - 16 * il), 0.0),
                ),
            )
            at = pl.ds(i * PL + g * 8, 8)
            total = acc_ref[at, :] + extra
            if i < 2:
                total = total + planes[0][i]
            elif i > EDGE - 3:
                total = total + planes[1][EDGE - 1 - i]
            total_ref[at, :] = jnp.where(solid_ref[at, :] > 0.5, 0.0, jnp.abs(total))
    for t in range(2 * EDGE):
        i, jh = divmod(t, 2)
        out_ref[:, pl.ds(t * LANES, LANES)] = total_ref[pl.ds(i * PL + jh, NB, stride=2), :]


def shape(*dims):
    return jax.ShapeDtypeStruct(dims, jnp.float32)


def scratch(*rows):
    return [pltpu.VMEM((r, LANES), jnp.float32) for r in rows]


SMEM = pl.BlockSpec(memory_space=pltpu.SMEM)
VMEM = pl.BlockSpec(memory_space=pltpu.VMEM)
PARAMS = pltpu.CompilerParams(vmem_limit_bytes=VMEM_LIMIT)


def prep(flow, adjoint, cut_flag, own, vertical):
    return pl.pallas_call(
        prep_kernel,
        out_shape=[
            shape(5 * ROWS, LANES),
            shape(5 * ROWS, LANES),
            shape(ROWS, LANES),
            shape(10 * FACES, LANES),
            shape(10 * PL, LANES),
            shape(10 * PL, LANES),
            jax.ShapeDtypeStruct((288, LANES), jnp.int32),
        ],
        in_specs=[VMEM] * 5,
        out_specs=[VMEM] * 7,
        cost_estimate=pl.CostEstimate(flops=10**8, bytes_accessed=3 * 10**7, transcendentals=0),
        compiler_params=PARAMS,
    )(flow.transpose(1, 0, 2), adjoint.transpose(1, 0, 2), cut_flag[None], own, vertical)


def reply(me, asked, layers):
    return pl.pallas_call(
        reply_kernel,
        out_shape=shape(40 * PEERS, LANES),
        in_specs=[SMEM, VMEM, VMEM],
        out_specs=VMEM,
        compiler_params=PARAMS,
    )(me, asked, layers)


def inner(edge, index, prim, adj, solid, low, high):
    return pl.pallas_call(
        inner_kernel,
        out_shape=[shape(n, LANES) for n in (ROWS, 120 * PL, 80 * PL, 8 * PL)],
        in_specs=[SMEM] + [VMEM] * 6,
        out_specs=[VMEM] * 4,
        scratch_shapes=scratch(20 * PL, 10 * ROWS, 31 * 8, 15 * 8),
        compiler_params=PARAMS,
    )(edge, index, prim, adj, solid, low, high)


def rim(index, got, planes, ghosts, walls, solid, acc):
    return pl.pallas_call(
        rim_kernel,
        out_shape=shape(NB, EDGE * EDGE * EDGE),
        in_specs=[VMEM] * 7,
        out_specs=VMEM,
        scratch_shapes=scratch(40 * PL, 40 * PL, 8 * PL, ROWS),
        compiler_params=PARAMS,
    )(index, got, planes, ghosts, walls, solid, acc)


def ask_kernel(owner_ref, link_ref, own_ref, out_ref):
    link = link_ref[...]
    slot = (link.astype(jnp.float32) * 0.2 + 0.05).astype(jnp.int32)
    far = lax.broadcasted_iota(jnp.int32, link.shape, 0) ^ 1
    own = (owner_ref[...] * 64 + slot * 4 + far) * 8 + (link - 5 * slot)
    own_ref[...] = own
    at = lax.broadcasted_iota(jnp.int32, (NB, LANES), 0)
    spot = lax.broadcasted_iota(jnp.int32, (NB, LANES), 1)
    row = jnp.full((1, LANES), -1.0, jnp.float32)
    for f in range(4):
        spread = jnp.dot(
            own[f : f + 1].astype(jnp.float32) + 1.0,
            jnp.where(spot == at + f * NB, 1.0, 0.0),
            precision=lax.Precision.HIGHEST,
            preferred_element_type=jnp.float32,
        )
        row = row + spread
    row = (row + jnp.where(row < 0.0, -0.25, 0.25)).astype(jnp.int32)
    out_ref[...] = jnp.broadcast_to(row, out_ref.shape)


def ask(lateral_owner, lateral_link):
    return pl.pallas_call(
        ask_kernel,
        out_shape=[
            jax.ShapeDtypeStruct((4, NB), jnp.int32),
            jax.ShapeDtypeStruct((PEERS, LANES), jnp.int32),
        ],
        in_specs=[VMEM] * 2,
        out_specs=[VMEM] * 2,
        compiler_params=PARAMS,
    )(lateral_owner[:, :, 0].T, lateral_link.T)


def exchange(block, axis):
    chunks = block.reshape(PEERS, -1, LANES)
    out = lax.all_to_all(chunks, axis, split_axis=0, concat_axis=0, tiled=True)
    return out.reshape(-1, LANES)


def local(flow, adjoint, cut_flag, lateral_owner, lateral_link, vertical_link):
    own, questions = ask(lateral_owner, lateral_link)
    asked = exchange(questions, "blk")
    prim, adj, solid, layers, low_face, high_face, index = prep(
        flow, adjoint, cut_flag, own, vertical_link.T
    )
    asked, low_face, high_face = lax.optimization_barrier((asked, low_face, high_face))
    regions = lax.axis_size("grp")
    region = lax.axis_index("grp")
    low = lax.ppermute(high_face, "grp", [(r, r + 1) for r in range(regions - 1)])
    high = lax.ppermute(low_face, "grp", [(r + 1, r) for r in range(regions - 1)])
    me = lax.axis_index("blk").astype(jnp.int32).reshape(1)
    replies = reply(me, asked, layers)
    got = exchange(replies, "blk")
    edge = region.astype(jnp.int32).reshape(1)
    acc, planes, ghosts, walls = inner(edge, index, prim, adj, solid, low, high)
    return rim(index, got, planes, ghosts, walls, solid, acc)


def solution(mesh):
    in_specs = (
        P(("blk", "grp"), None, None),
        P(("blk", "grp"), None, None),
        P(("blk", "grp"), None),
        P(("blk", "grp"), None, None),
        P(("blk", "grp"), None),
        P(("blk", "grp"), None),
    )
    out_specs = P(("blk", "grp"), None)
    return jax.shard_map(local, mesh=mesh, in_specs=in_specs, out_specs=out_specs, check_vma=False)
```

```python
import math

import jax
import jax.numpy as jnp
from jax import lax
from jax.experimental import pallas as pl
from jax.experimental.pallas import tpu as pltpu
from jax.sharding import PartitionSpec as P

EDGE = 16
NB = 12
PL = 2 * NB
ROWS = EDGE * PL
LANES = 128
PEERS = 64
REGIONS = 4
FACES = 4 * PL
PXR = (EDGE + 2) * PL
MR = (EDGE + 1) * PL

VEL = math.sqrt(0.2)
PRESS = 0.2
WEIGHTS = (1.0 / VEL, 5.0, 5.0, 5.0, 2.5 / VEL)
FARFIELD = (1.0, 0.0, 0.0, 0.3 * VEL, PRESS)
KNEE = 0.4 / math.sqrt(5.0)
START = 1.2 / math.sqrt(5.0)
CURVE = 1.25 * math.sqrt(5.0)

VMEM_LIMIT = 56 * 2**20


def lane():
    return lax.broadcasted_iota(jnp.int32, (8, LANES), 1)


def even_row():
    return lax.broadcasted_iota(jnp.int32, (8, LANES), 0) % 2 == 0


def rolled(x, amount, axis=1):
    size = x.shape[axis]
    amount = amount % size
    return x if amount == 0 else pltpu.roll(x, amount, axis)


def rows8(start):
    if isinstance(start, int):
        return pl.ds(start, 8)
    return pl.ds(pl.multiple_of(start, 8), 8)


def compact_k(load):
    depth = lane() % EDGE
    low = high = None
    for i in range(EDGE):
        x = rolled(load(i), i)
        low = x if low is None else jnp.where(depth == i, x, low)
        high = x if high is None else jnp.where(depth == (i + 15) % EDGE, x, high)
    return low, rolled(high, -15)


def compact_depths(load, count):
    low = lane() // EDGE
    spots = list(range(count)) + [7 - n for n in range(count)]
    halves = []
    for ih in range(2):
        totals = [None] * len(spots)
        for il in range(8):
            x = rolled(load(ih * 8 + il), 16 * il)
            for n, spot in enumerate(spots):
                t = totals[n]
                totals[n] = x if t is None else jnp.where(low == (spot + il) % 8, x, t)
        halves.append(totals)
    even = even_row()
    near = [jnp.where(even, a, rolled(c, 1, 0)) for a, c in zip(halves[0][:count], halves[1][:count])]
    far = [jnp.where(even, rolled(a, -1, 0), c) for a, c in zip(halves[0][count:], halves[1][count:])]
    out = [rolled(t, -16 * spot) for t, spot in zip(near + far, spots)]
    return out[:count], out[count:]


def spread_j(low, high, i):
    ih, il = i // 8, i % 8
    a = low if ih == 0 else rolled(low, -1, 0)
    c = rolled(high, 1, 0) if ih == 0 else high
    return jnp.where(even_row(), rolled(a, -16 * il), rolled(c, 16 * (7 - il)))


def spread_k(low, high, i):
    return jnp.where(lane() % EDGE == 0, rolled(low, -i), rolled(high, 15 - i))


def column_of(packed, rows, width):
    at = lax.broadcasted_iota(jnp.int32, (rows, width), 0) // 2
    spot = lax.broadcasted_iota(jnp.int32, (rows, width), 1)
    return jnp.sum(jnp.where(at == spot, packed, 0.0), axis=1, keepdims=True)


def index_tables(own, vertical, index_ref):
    spots = lax.broadcasted_iota(jnp.int32, (PL, LANES), 1)
    half = lax.broadcasted_iota(jnp.int32, (PL, LANES), 0) % 2
    low, depth = spots // EDGE, spots % EDGE
    wide = (4 * half + low // 2) * EDGE + depth // 2

    def store(f, code, row_part, col_part, base, step):
        full = code == 4
        index_ref[pl.ds(f * PL, PL), :] = jnp.where(full, spots, wide + 8 * col_part)
        index_ref[pl.ds(144 + f * PL, PL), :] = base + step * jnp.where(full, half, row_part)

    at = lax.broadcasted_iota(jnp.int32, (PL, NB), 0) // 2
    spot = lax.broadcasted_iota(jnp.int32, (PL, NB), 1)
    entries = [own[f : f + 1, :].astype(jnp.int32) for f in range(4)]
    holders = [e >> 9 for e in entries]
    for f in range(4):
        value = column_of(own[f : f + 1, :], PL, NB).astype(jnp.int32)
        owner, code = value >> 9, value & 7
        rank = jnp.zeros((PL, 1), jnp.float32)
        for other in range(f + 1):
            same = holders[other] == owner
            if other == f:
                same = same & (spot < at)
            rank = rank + jnp.sum(jnp.where(same, 1.0, 0.0), axis=1, keepdims=True)
        rank = rank.astype(jnp.int32)
        store(f, code, code >> 1, code & 1, rank * 2 * PEERS + owner, PEERS)
    for side in range(2):
        value = column_of(vertical[side : side + 1, :], PL, NB).astype(jnp.int32)
        slot = (value.astype(jnp.float32) * 0.2 + 0.05).astype(jnp.int32)
        code = value - 5 * slot
        store(4 + side, code, code & 1, code >> 1, slot * 2, 1)


def prep_kernel(
    flow_ref, adj_ref, flag_ref, own_ref, vertical_ref,
    prim_ref, adjl_ref, solid_ref, lat_ref, low_ref, high_ref, index_ref, px_ref, ps_ref,
):
    def relaid(ref, c, out_ref):
        for t in range(2 * EDGE):
            i, jh = divmod(t, 2)
            part = ref[c, :, pl.ds(t * LANES, LANES)]
            out_ref[pl.ds(i * PL + jh + c * ROWS, NB, stride=2), :] = part.astype(jnp.float32)

    for c in range(5):
        relaid(flow_ref, c, prim_ref)
        relaid(adj_ref, c, adjl_ref)
    relaid(flag_ref, 0, solid_ref)
    index_tables(
        own_ref[...].astype(jnp.float32), vertical_ref[...].astype(jnp.float32), index_ref
    )

    def convert(n, _):
        at = [pl.ds(pl.multiple_of(c * ROWS + n * 64, 64), 64) for c in range(5)]
        rho = prim_ref[at[0]]
        inv = 1.0 / rho
        vel = [prim_ref[at[c]] * inv for c in (1, 2, 3)]
        square = vel[0] * vel[0] + vel[1] * vel[1] + vel[2] * vel[2]
        prim_ref[at[4]] = (0.4 * PRESS) * (prim_ref[at[4]] - 0.5 * rho * square)
        for c in range(3):
            prim_ref[at[c + 1]] = vel[c] * VEL
        return 0

    lax.fori_loop(0, ROWS // 64, convert, 0)

    def layers(ref, first):
        def one(c, _):
            for g in range(3):

                def load(i):
                    return ref[rows8(c * ROWS + i * PL + g * 8), :]

                out = (c + first) * FACES + g * 8
                lat_ref[rows8(out), :] = load(0)
                lat_ref[rows8(out + PL), :] = load(EDGE - 1)
                near, far = packed(load, px_ref, 3, c + first, 10, g)
                lat_ref[rows8(out + 2 * PL), :] = near[0]
                lat_ref[rows8(out + 3 * PL), :] = far[0]
                low, high = compact_k(load)
                low_ref[rows8((c + first) * PL + g * 8), :] = low
                high_ref[rows8((c + first) * PL + g * 8), :] = high
            return 0

        lax.fori_loop(0, 5, one, 0)

    layers(prim_ref, 0)
    layers(adjl_ref, 5)
    for g in range(3):
        packed(lambda i: solid_ref[pl.ds(i * PL + g * 8, 8), :], ps_ref, 2, 0, 1, g)


def reply_kernel(me_ref, asked_ref, lat_ref, out_ref):
    before = lax.broadcasted_iota(jnp.int32, (LANES, LANES), 0) < lax.broadcasted_iota(
        jnp.int32, (LANES, LANES), 1
    )
    asked = asked_ref[...]
    match = (asked >> 9) == me_ref[0]
    rank = jnp.dot(
        jnp.where(match, 1.0, 0.0),
        jnp.where(before, 1.0, 0.0),
        preferred_element_type=jnp.float32,
    )
    face = (asked >> 3) & 63
    target = (((face & 3) * PL) + ((face >> 2) * 2)).astype(jnp.float32) + 10.0
    column = lax.broadcasted_iota(jnp.int32, (PEERS, FACES), 1).astype(jnp.float32)
    picks = []
    for s in range(2):
        mine = match & (rank > s - 0.5) & (rank < s + 0.5)
        row = jnp.sum(jnp.where(mine, target, 0.0), axis=1, keepdims=True) - 10.0
        for h in range(2):
            picks.append(jnp.where(column == row + float(h), 1.0, 0.0))
    picks = jnp.concatenate(picks, axis=0)
    for c in range(10):
        out = jnp.dot(
            picks,
            lat_ref[pl.ds(c * FACES, FACES), :],
            precision=lax.Precision.HIGHEST,
            preferred_element_type=jnp.float32,
        )
        for q in range(4):
            out_ref[pl.ds(c * 4 + q, PEERS, stride=40), :] = out[q * PEERS : (q + 1) * PEERS]


def one_hot(columns, width):
    parts = []
    for start in range(0, width, LANES):
        parts.append(
            jnp.where(
                columns == lax.broadcasted_iota(jnp.int32, columns.shape, 1) + start, 1.0, 0.0
            )
        )
    return parts[0] if len(parts) == 1 else jnp.concatenate(parts, axis=1)


def widened(x, index):
    parts = [
        jnp.take_along_axis(
            x[n : n + 8], index[n : n + 8], axis=1, mode="promise_in_bounds"
        )
        for n in range(0, x.shape[0], 8)
    ]
    return jnp.concatenate(parts, axis=0)


def fetched(columns, parts):
    y = jnp.dot(
        columns,
        jnp.concatenate(parts, axis=1),
        precision=lax.Precision.HIGHEST,
        preferred_element_type=jnp.float32,
    )
    return [y[:, n * LANES : (n + 1) * LANES] for n in range(len(parts))]


def packed(load, out_ref, depth, first, step, g):
    planes = [[load(n) for n in range(depth)], [load(EDGE - 1 - n) for n in range(depth)]]
    across = compact_depths(load, depth)
    for n, sides in enumerate((planes, across)):
        for side in range(2):
            for at in range(depth):
                row = (((n * 2 + side) * depth + at) * step + first) * PL + g * 8
                out_ref[rows8(row), :] = sides[side][at]
    return across


def minmod(a, c):
    return jnp.maximum(jnp.minimum(a, jnp.maximum(c, 0.0)), jnp.minimum(c, 0.0))


def masks():
    low, depth, even = lane() // EDGE, lane() % EDGE, even_row()
    return dict(
        k_last=depth == EDGE - 1,
        k_first=depth == 0,
        j_wrap=low == 7,
        j_back=low == 0,
        j_last=(low == 7) & ~even,
        j_first=(low == 0) & even,
        j_penult=(low == 6) & ~even,
    )


def next_k(x):
    return rolled(x, -1)


def last_k(x):
    return rolled(x, 1)


def next_j(x, m):
    r = rolled(x, -16)
    return jnp.where(m["j_wrap"], rolled(r, -1, 0), r)


def last_j(x, m):
    r = rolled(x, 16)
    return jnp.where(m["j_back"], rolled(r, 1, 0), r)


def slopes_of(below, x, above, gt, gk, m):
    out = [0.25 * minmod(above - x, x - below)]
    gt = x if gt is None else gt
    up = jnp.where(m["j_last"], gt, next_j(x, m))
    down = jnp.where(m["j_first"], gt, last_j(x, m))
    out.append(0.25 * minmod(up - x, x - down))
    up = jnp.where(m["k_last"], gk, next_k(x))
    down = jnp.where(m["k_first"], gk, last_k(x))
    out.append(0.25 * minmod(up - x, x - down))
    return out


def state(q):
    rho, u, v, w, p = q
    rs = lax.rsqrt(rho)
    enth = 7.0 * p * (rs * rs) + (u * u + v * v + w * w)
    return (rho, u, v, w, p, rho * rs, enth)


def four(base, first, second):
    out = []
    for a in (-1, 1):
        half = [x + s if a > 0 else x - s for x, s in zip(base, first)]
        for e in (-1, 1):
            out.append(state([x + s if e > 0 else x - s for x, s in zip(half, second)]))
    return out


def roe(left, right, axis):
    n = 1 + axis
    weight = right[5] * pl.reciprocal(left[5] + right[5], approx=True)
    jump = right[n] - left[n]
    mean = [None] * 4
    for c in (1, 2, 3):
        d = jump if c == n else right[c] - left[c]
        mean[c] = left[c] + weight * d
    enth = left[6] + weight * (right[6] - left[6])
    c2 = enth - (mean[1] * mean[1] + mean[2] * mean[2] + mean[3] * mean[3])
    rc = lax.rsqrt(c2)
    un = mean[n]
    ahead = un > 0.0
    sign = jnp.where(ahead, VEL, -VEL)
    b = jnp.maximum(START - jnp.abs(un) * rc, 0.0)
    s = jnp.minimum(b, KNEE)
    speed = 2.5 * b - s * (2.5 - (2.5 * CURVE) * s)
    wave = speed * ((right[4] - left[4]) * rc - sign * (left[5] * right[5] * jump))
    sc = sign * (c2 * rc)
    up = [jnp.where(ahead, left[c], right[c]) for c in (0, 1, 2, 3, 4, 6)]
    mass = up[0] * up[n]
    t = un * sc
    flux = [mass - wave]
    for c in (1, 2, 3):
        if c == n:
            flux.append((mass * up[c] + up[4]) - wave * (mean[c] - sc))
        else:
            flux.append(mass * up[c] - wave * mean[c])
    flux.append(mass * up[5] - wave * (enth - t - t))
    return flux


def face_sums(lefts, rights, axis):
    f = [roe(a, c, axis) for a, c in zip(lefts, rights)]
    plain, first, second = [], [], []
    for c in range(5):
        lo, hi = f[0][c] + f[1][c], f[2][c] + f[3][c]
        dlo, dhi = f[1][c] - f[0][c], f[3][c] - f[2][c]
        plain.append(lo + hi)
        first.append(hi - lo)
        second.append(dlo + dhi)
    return plain, first, second


def plain_sum(lefts, rights, axis):
    f = [roe(a, c, axis) for a, c in zip(lefts, rights)]
    return [(f[0][c] + f[1][c]) + (f[2][c] + f[3][c]) for c in range(5)]


def walled(sums, axis, solid_a, solid_b, wall_a, wall_b, gone=None):
    from_a = (solid_b > 0.5) & (solid_a < 0.5)
    from_b = (solid_a > 0.5) & (solid_b < 0.5)
    dead = from_a | from_b
    if gone is not None:
        dead = dead | gone
    out = []
    for part, pa, pb in zip(sums, wall_a, wall_b):
        new = []
        for c in range(5):
            if c == axis + 1:
                value = jnp.where(from_a, pa, jnp.where(from_b, pb, part[c]))
                new.append(value if gone is None else jnp.where(gone, 0.0, value))
            else:
                new.append(jnp.where(dead, 0.0, part[c]))
        out.append(new)
    return out


def wall_sums(p, normal, first, second):
    return (4.0 * (p + normal), 4.0 * first, 4.0 * second)


TANGENTS = ((1, 2), (0, 2), (0, 1))


class Moments:
    def __init__(self):
        self.value = [[None] * 5 for _ in range(4)]

    def add(self, k, part, sign):
        for c in range(5):
            old = self.value[k][c]
            if old is None:
                self.value[k][c] = part[c] if sign > 0 else -part[c]
            else:
                self.value[k][c] = old + part[c] if sign > 0 else old - part[c]

    def below(self, d, sums):
        self.add(0, sums[0], -1)
        self.add(d + 1, sums[0], 1)
        for t, part in zip(TANGENTS[d], sums[1:]):
            self.add(t + 1, part, -1)

    def above(self, d, sums):
        self.add(0, sums[0], 1)
        self.add(d + 1, sums[0], 1)
        for t, part in zip(TANGENTS[d], sums[1:]):
            self.add(t + 1, part, 1)

    def weighed(self, adj, slopes):
        total = None
        for c in range(5):
            part = adj[c] * self.value[0][c]
            for d in range(3):
                part = part + slopes[d][c] * self.value[d + 1][c]
            total = WEIGHTS[c] * part if total is None else total + WEIGHTS[c] * part
        return total


def weighed_sums(sums, normal, first, second):
    total = None
    for c in range(5):
        part = WEIGHTS[c] * (normal[c] * sums[0][c] + first[c] * sums[1][c] + second[c] * sums[2][c])
        total = part if total is None else total + part
    return total


def children(x, s):
    child = [
        four([a + b if up else a - b for a, b in zip(x, s[0])], s[1], s[2]) for up in (False, True)
    ]
    lower = [
        child[0],
        [child[0][0], child[0][1], child[1][0], child[1][1]],
        [child[0][0], child[0][2], child[1][0], child[1][2]],
    ]
    upper = [
        child[1],
        [child[0][2], child[0][3], child[1][2], child[1][3]],
        [child[0][1], child[0][3], child[1][1], child[1][3]],
    ]
    return lower, upper


def within(moments, lower, upper, axes):
    for d in range(3):
        inner = plain_sum(lower[d], upper[d], axes[d])
        moments.add(d + 1, [y + y for y in inner], -1)


def along(moments, d, axis, lower, upper, x, s, solid, ahead, back, gone):
    sums = face_sums(upper[d], [tuple(ahead(y) for y in st) for st in lower[d]], axis)
    t0, t1 = TANGENTS[d]
    wall_a = wall_sums(x[4], s[d][4], s[t0][4], s[t1][4])
    wall_b = [ahead(y) for y in wall_sums(x[4], -s[d][4], s[t0][4], s[t1][4])]
    sums = walled(sums, axis, solid, ahead(solid), wall_a, wall_b, gone)
    moments.above(d, sums)
    moments.below(d, [[back(y) for y in part] for part in sums])


def ends(moments, d, axis, x, s, ghost, first, last):
    n = axis + 1
    flip = jnp.where(first, -1.0, 1.0)
    base = [a + flip * b for a, b in zip(x, s[d])]
    t0, t1 = TANGENTS[d]
    f0, f1, g = list(s[t0]), list(s[t1]), list(ghost)
    for part in (base, f0, f1, g):
        part[n] = flip * part[n]
    sums = face_sums(four(base, f0, f1), [state(g)] * 4, axis)
    shown = first | last
    sums = [
        [jnp.where(shown, flip * y if c == n else y, 0.0) for c, y in enumerate(part)] for part in sums
    ]
    moments.add(0, sums[0], 1)
    moments.add(d + 1, [flip * y for y in sums[0]], 1)
    moments.add(t0 + 1, sums[1], 1)
    moments.add(t1 + 1, sums[2], 1)


def inner_kernel(
    edge_ref, index_ref, prim_ref, adj_ref, solid_ref, low_ref, high_ref,
    acc_ref, pg_ref,
    v_ref, gk_ref, pv_ref, aw_ref,
):
    for side in range(2):
        ref = (low_ref, high_ref)[side]
        columns = one_hot(index_ref[pl.ds(240 + side * PL, PL), :], LANES)[:, :PL]
        parts = fetched(columns, [ref[pl.ds(c * PL, PL), :] for c in range(10)])
        for c in range(10):
            y = widened(parts[c], index_ref[pl.ds(FACES + side * PL, PL), :])
            far = FARFIELD[c] if c < 5 else 0.0
            v_ref[pl.ds((side * 10 + c) * PL, PL), :] = jnp.where(
                edge_ref[0] == side * (REGIONS - 1), jnp.full_like(y, far), y
            )

    def spread(c, _):
        for g in range(3):
            low, high = (v_ref[rows8((side * 10 + c) * PL + g * 8), :] for side in range(2))
            for i in range(EDGE):
                gk_ref[rows8(c * ROWS + i * PL + g * 8), :] = spread_k(low, high, i)
        return 0

    lax.fori_loop(0, 10, spread, 0)

    def pack(c, _):
        for g in range(3):

            def load_of(ref, first):
                return lambda i: ref[rows8((c + first) * ROWS + i * PL + g * 8), :]

            packed(load_of(gk_ref, 0), pg_ref, 2, c, 10, g)
            packed(load_of(gk_ref, 5), pg_ref, 2, c + 5, 10, g)
        return 0

    lax.fori_loop(0, 5, pack, 0)
    m = masks()
    inside = ~(m["j_first"] | m["j_last"])
    gone_j = m["j_first"] | m["j_last"] | m["j_penult"]
    for i in (0, EDGE - 1):
        acc_ref[pl.ds(i * PL, PL), :] = jnp.zeros((PL, LANES), jnp.float32)

    def column(g, _):
        g8 = g * 8
        start = state([jnp.full((8, LANES), y, jnp.float32) for y in (1.0, 0.0, 0.0, 0.0, 0.2)])
        for n in range(4):
            for q in range(7):
                pv_ref[pl.ds((n * 7 + q) * 8, 8), :] = start[q]
        aw_ref[...] = jnp.zeros_like(aw_ref)

        def plane(i, _):
            row = i * PL + g8

            def around(ref, c, first):
                at = c * ROWS + row
                return slopes_of(
                    ref[rows8(at - PL), :],
                    ref[rows8(at), :],
                    ref[rows8(at + PL), :],
                    None,
                    gk_ref[rows8((c + first) * ROWS + row), :],
                    m,
                )

            x = [prim_ref[rows8(c * ROWS + row), :] for c in range(5)]
            s = list(zip(*[around(prim_ref, c, 0) for c in range(5)]))
            ghost = [gk_ref[rows8(c * ROWS + row), :] for c in range(5)]
            solid = solid_ref[rows8(row), :]
            lower, upper = children(x, s)
            moments = Moments()
            within(moments, lower, upper, (0, 1, 2))

            before = [
                tuple(pv_ref[pl.ds((n * 7 + q) * 8, 8), :] for q in range(7)) for n in range(4)
            ]
            prior = row - PL
            wall_a = [pv_ref[pl.ds((28 + q) * 8, 8), :] for q in range(3)]
            wall_b = wall_sums(x[4], -s[0][4], s[1][4], s[2][4])
            sums = face_sums(before, lower[0], 0)
            sums = walled(sums, 0, solid_ref[rows8(prior), :], solid, wall_a, wall_b)
            used = jnp.where(i > 1, 1.0, 0.0)
            sums = [[used * y for y in part] for part in sums]
            moments.below(0, sums)
            old = [[aw_ref[pl.ds((q * 5 + c) * 8, 8), :] for c in range(5)] for q in range(3)]
            acc_ref[rows8(prior), :] = acc_ref[rows8(prior), :] + jnp.where(
                inside, weighed_sums(sums, *old), 0.0
            )
            for n in range(4):
                for q in range(7):
                    pv_ref[pl.ds((n * 7 + q) * 8, 8), :] = upper[0][n][q]
            for q, y in enumerate(wall_sums(x[4], s[0][4], s[1][4], s[2][4])):
                pv_ref[pl.ds((28 + q) * 8, 8), :] = y

            along(
                moments, 1, 1, lower, upper, x, s, solid,
                lambda y: next_j(y, m), lambda y: last_j(y, m), gone_j,
            )
            along(moments, 2, 2, lower, upper, x, s, solid, next_k, last_k, m["k_last"])
            ends(moments, 2, 2, x, s, ghost, m["k_first"], m["k_last"])

            a = [adj_ref[rows8(c * ROWS + row), :] for c in range(5)]
            t = list(zip(*[around(adj_ref, c, 5) for c in range(5)]))
            acc_ref[rows8(row), :] = jnp.where(inside, moments.weighed(a, t), 0.0)
            for c in range(5):
                aw_ref[pl.ds(c * 8, 8), :] = a[c] + t[0][c]
                aw_ref[pl.ds((5 + c) * 8, 8), :] = t[1][c]
                aw_ref[pl.ds((10 + c) * 8, 8), :] = t[2][c]
            return 0

        for q in range(3):
            pv_ref[pl.ds((28 + q) * 8, 8), :] = jnp.zeros((8, LANES), jnp.float32)
        lax.fori_loop(1, EDGE - 1, plane, 0, unroll=2)
        return 0

    lax.fori_loop(0, 3, column, 0)


def rim_kernel(
    index_ref, got_ref, px_ref, pg_ref, ps_ref, solid_ref, acc_ref, out_ref,
    gl_ref, tg_ref, pm_ref, total_ref,
):
    columns = one_hot(index_ref[pl.ds(144, FACES), :], 4 * PEERS)
    parts = fetched(
        columns,
        [
            jnp.concatenate(
                [got_ref[pl.ds(c * 4 + q, PEERS, stride=40), :] for q in range(4)], axis=0
            )
            for c in range(10)
        ],
    )
    for c in range(10):
        y = widened(parts[c], index_ref[pl.ds(0, FACES), :])
        for f in range(4):
            gl_ref[pl.ds((f * 10 + c) * PL, PL), :] = y[f * PL : (f + 1) * PL]

    for c in range(10):
        for g in range(3):
            low, high = (gl_ref[rows8((f * 10 + c) * PL + g * 8), :] for f in (2, 3))
            for at, i in enumerate((0, 1, EDGE - 1, EDGE - 2)):
                tg_ref[rows8((at * 10 + c) * PL + g * 8), :] = spread_j(low, high, i)
    m = masks()

    def boundary(n):
        axes = (n, 1 - n, 2)

        def one(at, _):
            side, g8 = at // 3, at % 3 * 8
            flip = jnp.where(side == 0, 1.0, -1.0)

            def load(ref, first):
                out = []
                for c in range(10):
                    y = ref[rows8((first + c) * PL + g8), :]
                    out.append(flip * y if c % 5 == n + 1 else y)
                return out

            place = n * 2 + side
            x = [load(px_ref, (place * 3 + depth) * 10) for depth in range(3)]
            outer = load(gl_ref, place * 10)
            gk = [load(pg_ref, (place * 2 + depth) * 10) for depth in range(2)]
            if n == 0:
                gt = [load(tg_ref, (side * 2 + depth) * 10) for depth in range(2)]
            else:
                gt = [[None] * 10] * 2
            solid = [ps_ref[rows8((place * 2 + depth) * PL + g8), :] for depth in range(2)]
            s0 = list(
                zip(*[slopes_of(outer[c], x[0][c], x[1][c], gt[0][c], gk[0][c], m) for c in range(10)])
            )
            s1 = list(
                zip(*[slopes_of(x[0][c], x[1][c], x[2][c], gt[1][c], gk[1][c], m) for c in range(10)])
            )
            flow, adj = x[0][:5], x[0][5:]
            s, t = [y[:5] for y in s0], [y[5:] for y in s0]
            lower, upper = children(flow, s)
            moments = Moments()
            within(moments, lower, upper, axes)
            moments.below(0, face_sums([state(outer[:5])] * 4, lower[0], n))

            flow1, adj1 = x[1][:5], x[1][5:]
            f1, t1 = [y[:5] for y in s1], [y[5:] for y in s1]
            sums = face_sums(
                upper[0], four([a - b for a, b in zip(flow1, f1[0])], f1[1], f1[2]), n
            )
            sums = walled(
                sums,
                n,
                solid[0],
                solid[1],
                wall_sums(flow[4], s[0][4], s[1][4], s[2][4]),
                wall_sums(flow1[4], -f1[0][4], f1[1][4], f1[2][4]),
            )
            moments.above(0, sums)
            next_total = -weighed_sums(
                sums, [a - b for a, b in zip(adj1, t1[0])], t1[1], t1[2]
            )

            gone = m["j_last"]
            if n == 1:
                gone = gone | m["j_first"] | m["j_penult"]
            along(
                moments, 1, axes[1], lower, upper, flow, s, solid[0],
                lambda y: next_j(y, m), lambda y: last_j(y, m), gone,
            )
            if n == 0:
                ends(moments, 1, axes[1], flow, s, gt[0][:5], m["j_first"], m["j_last"])
            along(moments, 2, 2, lower, upper, flow, s, solid[0], next_k, last_k, m["k_last"])
            ends(moments, 2, 2, flow, s, gk[0][:5], m["k_first"], m["k_last"])
            total = moments.weighed(adj, t)
            if n == 1:
                kept = ~(m["j_first"] | m["j_last"])
                total = jnp.where(kept, total, 0.0)
                next_total = jnp.where(kept, next_total, 0.0)
            pm_ref[rows8(place * 2 * PL + g8), :] = total
            pm_ref[rows8((place * 2 + 1) * PL + g8), :] = next_total
            return 0

        lax.fori_loop(0, 6, one, 0, unroll=2)

    boundary(0)
    boundary(1)

    low, even = lane() // EDGE, even_row()
    for g in range(3):
        planes = [[pm_ref[pl.ds((p * 2 + d) * PL + g * 8, 8), :] for d in range(2)] for p in range(4)]
        near = [planes[2], [rolled(y, -1, 0) for y in planes[2]]]
        far = [[rolled(y, 1, 0) for y in planes[3]], planes[3]]
        for i in range(EDGE):
            ih, il = i // 8, i % 8
            a, c = near[ih], far[ih]
            extra = jnp.where(
                even,
                jnp.where(
                    low == 0,
                    rolled(a[0], -16 * il),
                    jnp.where(low == 1, rolled(a[1], 16 - 16 * il), 0.0),
                ),
                jnp.where(
                    low == 7,
                    rolled(c[0], 112 - 16 * il),
                    jnp.where(low == 6, rolled(c[1], 96 - 16 * il), 0.0),
                ),
            )
            at = pl.ds(i * PL + g * 8, 8)
            total = acc_ref[at, :] + extra
            if i < 2:
                total = total + planes[0][i]
            elif i > EDGE - 3:
                total = total + planes[1][EDGE - 1 - i]
            total_ref[at, :] = jnp.where(solid_ref[at, :] > 0.5, 0.0, jnp.abs(total))
    for t in range(2 * EDGE):
        i, jh = divmod(t, 2)
        out_ref[:, pl.ds(t * LANES, LANES)] = total_ref[pl.ds(i * PL + jh, NB, stride=2), :]


def shape(*dims):
    return jax.ShapeDtypeStruct(dims, jnp.float32)


def scratch(*rows):
    return [pltpu.VMEM((r, LANES), jnp.float32) for r in rows]


SMEM = pl.BlockSpec(memory_space=pltpu.SMEM)
VMEM = pl.BlockSpec(memory_space=pltpu.VMEM)
PARAMS = pltpu.CompilerParams(vmem_limit_bytes=VMEM_LIMIT)


def prep(flow, adjoint, cut_flag, own, vertical):
    return pl.pallas_call(
        prep_kernel,
        out_shape=[
            shape(5 * ROWS, LANES),
            shape(5 * ROWS, LANES),
            shape(ROWS, LANES),
            shape(10 * FACES, LANES),
            shape(10 * PL, LANES),
            shape(10 * PL, LANES),
            jax.ShapeDtypeStruct((288, LANES), jnp.int32),
            shape(120 * PL, LANES),
            shape(8 * PL, LANES),
        ],
        in_specs=[VMEM] * 5,
        out_specs=[VMEM] * 9,
        cost_estimate=pl.CostEstimate(flops=10**8, bytes_accessed=3 * 10**7, transcendentals=0),
        compiler_params=PARAMS,
    )(flow.transpose(1, 0, 2), adjoint.transpose(1, 0, 2), cut_flag[None], own, vertical)


def reply(me, asked, layers):
    return pl.pallas_call(
        reply_kernel,
        out_shape=shape(40 * PEERS, LANES),
        in_specs=[SMEM, VMEM, VMEM],
        out_specs=VMEM,
        compiler_params=PARAMS,
    )(me, asked, layers)


def inner(edge, index, prim, adj, solid, low, high):
    return pl.pallas_call(
        inner_kernel,
        out_shape=[shape(ROWS, LANES), shape(80 * PL, LANES)],
        in_specs=[SMEM] + [VMEM] * 6,
        out_specs=[VMEM] * 2,
        scratch_shapes=scratch(20 * PL, 10 * ROWS, 31 * 8, 15 * 8),
        compiler_params=PARAMS,
    )(edge, index, prim, adj, solid, low, high)


def rim(index, got, planes, ghosts, walls, solid, acc):
    return pl.pallas_call(
        rim_kernel,
        out_shape=shape(NB, EDGE * EDGE * EDGE),
        in_specs=[VMEM] * 7,
        out_specs=VMEM,
        scratch_shapes=scratch(40 * PL, 40 * PL, 8 * PL, ROWS),
        compiler_params=PARAMS,
    )(index, got, planes, ghosts, walls, solid, acc)


def ask_kernel(owner_ref, link_ref, own_ref, out_ref):
    link = link_ref[...]
    slot = (link.astype(jnp.float32) * 0.2 + 0.05).astype(jnp.int32)
    far = lax.broadcasted_iota(jnp.int32, link.shape, 0) ^ 1
    own = (owner_ref[...] * 64 + slot * 4 + far) * 8 + (link - 5 * slot)
    own_ref[...] = own
    at = lax.broadcasted_iota(jnp.int32, (NB, LANES), 0)
    spot = lax.broadcasted_iota(jnp.int32, (NB, LANES), 1)
    row = jnp.full((1, LANES), -1.0, jnp.float32)
    for f in range(4):
        spread = jnp.dot(
            own[f : f + 1].astype(jnp.float32) + 1.0,
            jnp.where(spot == at + f * NB, 1.0, 0.0),
            precision=lax.Precision.HIGHEST,
            preferred_element_type=jnp.float32,
        )
        row = row + spread
    row = (row + jnp.where(row < 0.0, -0.25, 0.25)).astype(jnp.int32)
    out_ref[...] = jnp.broadcast_to(row, out_ref.shape)


def ask(lateral_owner, lateral_link):
    return pl.pallas_call(
        ask_kernel,
        out_shape=[
            jax.ShapeDtypeStruct((4, NB), jnp.int32),
            jax.ShapeDtypeStruct((PEERS, LANES), jnp.int32),
        ],
        in_specs=[VMEM] * 2,
        out_specs=[VMEM] * 2,
        compiler_params=PARAMS,
    )(lateral_owner[:, :, 0].T, lateral_link.T)


def exchange(block, axis):
    chunks = block.reshape(PEERS, -1, LANES)
    out = lax.all_to_all(chunks, axis, split_axis=0, concat_axis=0, tiled=True)
    return out.reshape(-1, LANES)


def local(flow, adjoint, cut_flag, lateral_owner, lateral_link, vertical_link):
    own, questions = ask(lateral_owner, lateral_link)
    asked = exchange(questions, "blk")
    prim, adj, solid, layers, low_face, high_face, index, planes, walls = prep(
        flow, adjoint, cut_flag, own, vertical_link.T
    )
    asked, low_face, high_face = lax.optimization_barrier((asked, low_face, high_face))
    regions = lax.axis_size("grp")
    region = lax.axis_index("grp")
    low = lax.ppermute(high_face, "grp", [(r, r + 1) for r in range(regions - 1)])
    high = lax.ppermute(low_face, "grp", [(r + 1, r) for r in range(regions - 1)])
    me = lax.axis_index("blk").astype(jnp.int32).reshape(1)
    replies = reply(me, asked, layers)
    got = exchange(replies, "blk")
    edge = region.astype(jnp.int32).reshape(1)
    acc, ghosts = inner(edge, index, prim, adj, solid, low, high)
    return rim(index, got, planes, ghosts, walls, solid, acc)


def solution(mesh):
    in_specs = (
        P(("blk", "grp"), None, None),
        P(("blk", "grp"), None, None),
        P(("blk", "grp"), None),
        P(("blk", "grp"), None, None),
        P(("blk", "grp"), None),
        P(("blk", "grp"), None),
    )
    out_specs = P(("blk", "grp"), None)
    return jax.shard_map(local, mesh=mesh, in_specs=in_specs, out_specs=out_specs, check_vma=False)
```

```python
import math

import jax
import jax.numpy as jnp
from jax import lax
from jax.experimental import pallas as pl
from jax.experimental.pallas import tpu as pltpu
from jax.sharding import PartitionSpec as P

EDGE = 16
NB = 12
PL = 2 * NB
ROWS = EDGE * PL
LANES = 128
PEERS = 64
REGIONS = 4
FACES = 4 * PL
PXR = (EDGE + 2) * PL
MR = (EDGE + 1) * PL

VEL = math.sqrt(0.2)
PRESS = 0.2
WEIGHTS = (1.0 / VEL, 5.0, 5.0, 5.0, 2.5 / VEL)
FARFIELD = (1.0, 0.0, 0.0, 0.3 * VEL, PRESS)
KNEE = 0.4 / math.sqrt(5.0)
START = 1.2 / math.sqrt(5.0)
CURVE = 1.25 * math.sqrt(5.0)

VMEM_LIMIT = 56 * 2**20


def lane():
    return lax.broadcasted_iota(jnp.int32, (8, LANES), 1)


def even_row():
    return lax.broadcasted_iota(jnp.int32, (8, LANES), 0) % 2 == 0


def rolled(x, amount, axis=1):
    size = x.shape[axis]
    amount = amount % size
    return x if amount == 0 else pltpu.roll(x, amount, axis)


def rows8(start):
    if isinstance(start, int):
        return pl.ds(start, 8)
    return pl.ds(pl.multiple_of(start, 8), 8)


def compact_k(load):
    depth = lane() % EDGE
    low = high = None
    for i in range(EDGE):
        x = rolled(load(i), i)
        low = x if low is None else jnp.where(depth == i, x, low)
        high = x if high is None else jnp.where(depth == (i + 15) % EDGE, x, high)
    return low, rolled(high, -15)


def compact_depths(load, count):
    low = lane() // EDGE
    spots = list(range(count)) + [7 - n for n in range(count)]
    halves = []
    for ih in range(2):
        totals = [None] * len(spots)
        for il in range(8):
            x = rolled(load(ih * 8 + il), 16 * il)
            for n, spot in enumerate(spots):
                t = totals[n]
                totals[n] = x if t is None else jnp.where(low == (spot + il) % 8, x, t)
        halves.append(totals)
    even = even_row()
    near = [jnp.where(even, a, rolled(c, 1, 0)) for a, c in zip(halves[0][:count], halves[1][:count])]
    far = [jnp.where(even, rolled(a, -1, 0), c) for a, c in zip(halves[0][count:], halves[1][count:])]
    out = [rolled(t, -16 * spot) for t, spot in zip(near + far, spots)]
    return out[:count], out[count:]


def spread_j(low, high, i):
    ih, il = i // 8, i % 8
    a = low if ih == 0 else rolled(low, -1, 0)
    c = rolled(high, 1, 0) if ih == 0 else high
    return jnp.where(even_row(), rolled(a, -16 * il), rolled(c, 16 * (7 - il)))


def spread_k(low, high, i):
    return jnp.where(lane() % EDGE == 0, rolled(low, -i), rolled(high, 15 - i))


def column_of(packed, rows, width):
    at = lax.broadcasted_iota(jnp.int32, (rows, width), 0) // 2
    spot = lax.broadcasted_iota(jnp.int32, (rows, width), 1)
    return jnp.sum(jnp.where(at == spot, packed, 0.0), axis=1, keepdims=True)


def index_tables(own, vertical, index_ref):
    spots = lax.broadcasted_iota(jnp.int32, (PL, LANES), 1)
    half = lax.broadcasted_iota(jnp.int32, (PL, LANES), 0) % 2
    low, depth = spots // EDGE, spots % EDGE
    wide = (4 * half + low // 2) * EDGE + depth // 2

    def store(f, code, row_part, col_part, base, step):
        full = code == 4
        index_ref[pl.ds(f * PL, PL), :] = jnp.where(full, spots, wide + 8 * col_part)
        index_ref[pl.ds(144 + f * PL, PL), :] = base + step * jnp.where(full, half, row_part)

    at = lax.broadcasted_iota(jnp.int32, (PL, NB), 0) // 2
    spot = lax.broadcasted_iota(jnp.int32, (PL, NB), 1)
    entries = [own[f : f + 1, :].astype(jnp.int32) for f in range(4)]
    holders = [e >> 9 for e in entries]
    for f in range(4):
        value = column_of(own[f : f + 1, :], PL, NB).astype(jnp.int32)
        owner, code = value >> 9, value & 7
        rank = jnp.zeros((PL, 1), jnp.float32)
        for other in range(f + 1):
            same = holders[other] == owner
            if other == f:
                same = same & (spot < at)
            rank = rank + jnp.sum(jnp.where(same, 1.0, 0.0), axis=1, keepdims=True)
        rank = rank.astype(jnp.int32)
        store(f, code, code >> 1, code & 1, rank * 2 * PEERS + owner, PEERS)
    for side in range(2):
        value = column_of(vertical[side : side + 1, :], PL, NB).astype(jnp.int32)
        slot = (value.astype(jnp.float32) * 0.2 + 0.05).astype(jnp.int32)
        code = value - 5 * slot
        store(4 + side, code, code & 1, code >> 1, slot * 2, 1)


def prep_kernel(
    flow_ref, adj_ref, flag_ref, own_ref, vertical_ref,
    prim_ref, adjl_ref, solid_ref, lat_ref, low_ref, high_ref, index_ref, px_ref, ps_ref,
):
    def relaid(ref, c, out_ref):
        for t in range(2 * EDGE):
            i, jh = divmod(t, 2)
            part = ref[c, :, pl.ds(t * LANES, LANES)]
            out_ref[pl.ds(i * PL + jh + c * ROWS, NB, stride=2), :] = part.astype(jnp.float32)

    for c in range(5):
        relaid(flow_ref, c, prim_ref)
        relaid(adj_ref, c, adjl_ref)
    relaid(flag_ref, 0, solid_ref)
    index_tables(
        own_ref[...].astype(jnp.float32), vertical_ref[...].astype(jnp.float32), index_ref
    )

    def convert(n, _):
        at = [pl.ds(pl.multiple_of(c * ROWS + n * 64, 64), 64) for c in range(5)]
        rho = prim_ref[at[0]]
        inv = 1.0 / rho
        vel = [prim_ref[at[c]] * inv for c in (1, 2, 3)]
        square = vel[0] * vel[0] + vel[1] * vel[1] + vel[2] * vel[2]
        prim_ref[at[4]] = (0.4 * PRESS) * (prim_ref[at[4]] - 0.5 * rho * square)
        for c in range(3):
            prim_ref[at[c + 1]] = vel[c] * VEL
        return 0

    lax.fori_loop(0, ROWS // 64, convert, 0)

    def layers(ref, first):
        def one(c, _):
            for g in range(3):

                def load(i):
                    return ref[rows8(c * ROWS + i * PL + g * 8), :]

                out = (c + first) * FACES + g * 8
                lat_ref[rows8(out), :] = load(0)
                lat_ref[rows8(out + PL), :] = load(EDGE - 1)
                near, far = packed(load, px_ref, 3, c + first, 10, g)
                lat_ref[rows8(out + 2 * PL), :] = near[0]
                lat_ref[rows8(out + 3 * PL), :] = far[0]
                low, high = compact_k(load)
                low_ref[rows8((c + first) * PL + g * 8), :] = low
                high_ref[rows8((c + first) * PL + g * 8), :] = high
            return 0

        lax.fori_loop(0, 5, one, 0)

    layers(prim_ref, 0)
    layers(adjl_ref, 5)
    for g in range(3):
        packed(lambda i: solid_ref[pl.ds(i * PL + g * 8, 8), :], ps_ref, 2, 0, 1, g)


def reply_kernel(me_ref, asked_ref, lat_ref, out_ref):
    before = lax.broadcasted_iota(jnp.int32, (LANES, LANES), 0) < lax.broadcasted_iota(
        jnp.int32, (LANES, LANES), 1
    )
    asked = asked_ref[...]
    match = (asked >> 9) == me_ref[0]
    rank = jnp.dot(
        jnp.where(match, 1.0, 0.0),
        jnp.where(before, 1.0, 0.0),
        preferred_element_type=jnp.float32,
    )
    face = (asked >> 3) & 63
    target = (((face & 3) * PL) + ((face >> 2) * 2)).astype(jnp.float32) + 10.0
    column = lax.broadcasted_iota(jnp.int32, (PEERS, FACES), 1).astype(jnp.float32)
    picks = []
    for s in range(2):
        mine = match & (rank > s - 0.5) & (rank < s + 0.5)
        row = jnp.sum(jnp.where(mine, target, 0.0), axis=1, keepdims=True) - 10.0
        for h in range(2):
            picks.append(jnp.where(column == row + float(h), 1.0, 0.0))
    picks = jnp.concatenate(picks, axis=0)
    for c in range(10):
        out = jnp.dot(
            picks,
            lat_ref[pl.ds(c * FACES, FACES), :],
            precision=lax.Precision.HIGHEST,
            preferred_element_type=jnp.float32,
        )
        for q in range(4):
            out_ref[pl.ds(c * 4 + q, PEERS, stride=40), :] = out[q * PEERS : (q + 1) * PEERS]


def one_hot(columns, width):
    parts = []
    for start in range(0, width, LANES):
        parts.append(
            jnp.where(
                columns == lax.broadcasted_iota(jnp.int32, columns.shape, 1) + start, 1.0, 0.0
            )
        )
    return parts[0] if len(parts) == 1 else jnp.concatenate(parts, axis=1)


def widened(x, index):
    parts = [
        jnp.take_along_axis(
            x[n : n + 8], index[n : n + 8], axis=1, mode="promise_in_bounds"
        )
        for n in range(0, x.shape[0], 8)
    ]
    return jnp.concatenate(parts, axis=0)


def fetched(columns, parts):
    y = jnp.dot(
        columns,
        jnp.concatenate(parts, axis=1),
        precision=lax.Precision.HIGHEST,
        preferred_element_type=jnp.float32,
    )
    return [y[:, n * LANES : (n + 1) * LANES] for n in range(len(parts))]


def packed(load, out_ref, depth, first, step, g):
    planes = [[load(n) for n in range(depth)], [load(EDGE - 1 - n) for n in range(depth)]]
    across = compact_depths(load, depth)
    for n, sides in enumerate((planes, across)):
        for side in range(2):
            for at in range(depth):
                row = (((n * 2 + side) * depth + at) * step + first) * PL + g * 8
                out_ref[rows8(row), :] = sides[side][at]
    return across


def minmod(a, c):
    return jnp.maximum(jnp.minimum(a, jnp.maximum(c, 0.0)), jnp.minimum(c, 0.0))


def masks():
    low, depth, even = lane() // EDGE, lane() % EDGE, even_row()
    return dict(
        k_last=depth == EDGE - 1,
        k_first=depth == 0,
        j_wrap=low == 7,
        j_back=low == 0,
        j_last=(low == 7) & ~even,
        j_first=(low == 0) & even,
        j_penult=(low == 6) & ~even,
    )


def next_k(x):
    return rolled(x, -1)


def last_k(x):
    return rolled(x, 1)


def next_j(x, m):
    r = rolled(x, -16)
    return jnp.where(m["j_wrap"], rolled(r, -1, 0), r)


def last_j(x, m):
    r = rolled(x, 16)
    return jnp.where(m["j_back"], rolled(r, 1, 0), r)


def slopes_of(below, x, above, gt, gk, m):
    out = [0.25 * minmod(above - x, x - below)]
    gt = x if gt is None else gt
    up = jnp.where(m["j_last"], gt, next_j(x, m))
    down = jnp.where(m["j_first"], gt, last_j(x, m))
    out.append(0.25 * minmod(up - x, x - down))
    up = jnp.where(m["k_last"], gk, next_k(x))
    down = jnp.where(m["k_first"], gk, last_k(x))
    out.append(0.25 * minmod(up - x, x - down))
    return out


def state(q):
    rho, u, v, w, p = q
    rs = lax.rsqrt(rho)
    enth = 7.0 * p * (rs * rs) + (u * u + v * v + w * w)
    return (rho, u, v, w, p, rho * rs, enth)


def four(base, first, second):
    out = []
    for a in (-1, 1):
        half = [x + s if a > 0 else x - s for x, s in zip(base, first)]
        for e in (-1, 1):
            out.append(state([x + s if e > 0 else x - s for x, s in zip(half, second)]))
    return out


def roe(left, right, axis):
    n = 1 + axis
    weight = right[5] * pl.reciprocal(left[5] + right[5], approx=True)
    jump = right[n] - left[n]
    mean = [None] * 4
    for c in (1, 2, 3):
        d = jump if c == n else right[c] - left[c]
        mean[c] = left[c] + weight * d
    enth = left[6] + weight * (right[6] - left[6])
    c2 = enth - (mean[1] * mean[1] + mean[2] * mean[2] + mean[3] * mean[3])
    rc = lax.rsqrt(c2)
    un = mean[n]
    ahead = un > 0.0
    sign = jnp.where(ahead, VEL, -VEL)
    b = jnp.maximum(START - jnp.abs(un) * rc, 0.0)
    s = jnp.minimum(b, KNEE)
    speed = 2.5 * b - s * (2.5 - (2.5 * CURVE) * s)
    wave = speed * ((right[4] - left[4]) * rc - sign * (left[5] * right[5] * jump))
    sc = sign * (c2 * rc)
    up = [jnp.where(ahead, left[c], right[c]) for c in (0, 1, 2, 3, 4, 6)]
    mass = up[0] * up[n]
    t = un * sc
    flux = [mass - wave]
    for c in (1, 2, 3):
        if c == n:
            flux.append((mass * up[c] + up[4]) - wave * (mean[c] - sc))
        else:
            flux.append(mass * up[c] - wave * mean[c])
    flux.append(mass * up[5] - wave * (enth - t - t))
    return flux


def face_sums(lefts, rights, axis):
    f = [roe(a, c, axis) for a, c in zip(lefts, rights)]
    plain, first, second = [], [], []
    for c in range(5):
        lo, hi = f[0][c] + f[1][c], f[2][c] + f[3][c]
        dlo, dhi = f[1][c] - f[0][c], f[3][c] - f[2][c]
        plain.append(lo + hi)
        first.append(hi - lo)
        second.append(dlo + dhi)
    return plain, first, second


def plain_sum(lefts, rights, axis):
    f = [roe(a, c, axis) for a, c in zip(lefts, rights)]
    return [(f[0][c] + f[1][c]) + (f[2][c] + f[3][c]) for c in range(5)]


def walled(sums, axis, solid_a, solid_b, wall_a, wall_b, gone=None):
    from_a = (solid_b > 0.5) & (solid_a < 0.5)
    from_b = (solid_a > 0.5) & (solid_b < 0.5)
    dead = from_a | from_b
    if gone is not None:
        dead = dead | gone
    out = []
    for part, pa, pb in zip(sums, wall_a, wall_b):
        new = []
        for c in range(5):
            if c == axis + 1:
                value = jnp.where(from_a, pa, jnp.where(from_b, pb, part[c]))
                new.append(value if gone is None else jnp.where(gone, 0.0, value))
            else:
                new.append(jnp.where(dead, 0.0, part[c]))
        out.append(new)
    return out


def wall_sums(p, normal, first, second):
    return (4.0 * (p + normal), 4.0 * first, 4.0 * second)


TANGENTS = ((1, 2), (0, 2), (0, 1))


class Moments:
    def __init__(self):
        self.value = [[None] * 5 for _ in range(4)]

    def add(self, k, part, sign):
        for c in range(5):
            old = self.value[k][c]
            if old is None:
                self.value[k][c] = part[c] if sign > 0 else -part[c]
            else:
                self.value[k][c] = old + part[c] if sign > 0 else old - part[c]

    def below(self, d, sums):
        self.add(0, sums[0], -1)
        self.add(d + 1, sums[0], 1)
        for t, part in zip(TANGENTS[d], sums[1:]):
            self.add(t + 1, part, -1)

    def above(self, d, sums):
        self.add(0, sums[0], 1)
        self.add(d + 1, sums[0], 1)
        for t, part in zip(TANGENTS[d], sums[1:]):
            self.add(t + 1, part, 1)

    def weighed(self, adj, slopes):
        total = None
        for c in range(5):
            part = adj[c] * self.value[0][c]
            for d in range(3):
                part = part + slopes[d][c] * self.value[d + 1][c]
            total = WEIGHTS[c] * part if total is None else total + WEIGHTS[c] * part
        return total


def weighed_sums(sums, normal, first, second):
    total = None
    for c in range(5):
        part = WEIGHTS[c] * (normal[c] * sums[0][c] + first[c] * sums[1][c] + second[c] * sums[2][c])
        total = part if total is None else total + part
    return total


def children(x, s):
    child = [
        four([a + b if up else a - b for a, b in zip(x, s[0])], s[1], s[2]) for up in (False, True)
    ]
    lower = [
        child[0],
        [child[0][0], child[0][1], child[1][0], child[1][1]],
        [child[0][0], child[0][2], child[1][0], child[1][2]],
    ]
    upper = [
        child[1],
        [child[0][2], child[0][3], child[1][2], child[1][3]],
        [child[0][1], child[0][3], child[1][1], child[1][3]],
    ]
    return lower, upper


def within(moments, lower, upper, axes):
    for d in range(3):
        inner = plain_sum(lower[d], upper[d], axes[d])
        moments.add(d + 1, [y + y for y in inner], -1)


def along(moments, d, axis, lower, upper, x, s, solid, ahead, back, gone):
    sums = face_sums(upper[d], [tuple(ahead(y) for y in st) for st in lower[d]], axis)
    t0, t1 = TANGENTS[d]
    wall_a = wall_sums(x[4], s[d][4], s[t0][4], s[t1][4])
    wall_b = [ahead(y) for y in wall_sums(x[4], -s[d][4], s[t0][4], s[t1][4])]
    sums = walled(sums, axis, solid, ahead(solid), wall_a, wall_b, gone)
    moments.above(d, sums)
    moments.below(d, [[back(y) for y in part] for part in sums])


def ends(moments, d, axis, x, s, ghost, first, last):
    n = axis + 1
    flip = jnp.where(first, -1.0, 1.0)
    base = [a + flip * b for a, b in zip(x, s[d])]
    t0, t1 = TANGENTS[d]
    f0, f1, g = list(s[t0]), list(s[t1]), list(ghost)
    for part in (base, f0, f1, g):
        part[n] = flip * part[n]
    sums = face_sums(four(base, f0, f1), [state(g)] * 4, axis)
    shown = first | last
    sums = [
        [jnp.where(shown, flip * y if c == n else y, 0.0) for c, y in enumerate(part)] for part in sums
    ]
    moments.add(0, sums[0], 1)
    moments.add(d + 1, [flip * y for y in sums[0]], 1)
    moments.add(t0 + 1, sums[1], 1)
    moments.add(t1 + 1, sums[2], 1)


def inner_kernel(
    edge_ref, index_ref, prim_ref, adj_ref, solid_ref, low_ref, high_ref,
    acc_ref, pg_ref,
    v_ref, gk_ref, pv_ref, aw_ref,
):
    for side in range(2):
        ref = (low_ref, high_ref)[side]
        columns = one_hot(index_ref[pl.ds(240 + side * PL, PL), :], LANES)[:, :PL]
        parts = fetched(columns, [ref[pl.ds(c * PL, PL), :] for c in range(10)])
        for c in range(10):
            y = widened(parts[c], index_ref[pl.ds(FACES + side * PL, PL), :])
            far = FARFIELD[c] if c < 5 else 0.0
            v_ref[pl.ds((side * 10 + c) * PL, PL), :] = jnp.where(
                edge_ref[0] == side * (REGIONS - 1), jnp.full_like(y, far), y
            )

    def spread(c, _):
        for g in range(3):
            low, high = (v_ref[rows8((side * 10 + c) * PL + g * 8), :] for side in range(2))
            for i in range(EDGE):
                gk_ref[rows8(c * ROWS + i * PL + g * 8), :] = spread_k(low, high, i)
        return 0

    lax.fori_loop(0, 10, spread, 0)

    even, early = even_row(), lane() % EDGE < 8
    ahead = jnp.where(even, 0, 8) + lane() // EDGE
    picks = [[spot * EDGE + ahead for spot in spots] for spots in ((0, 1), (7, 6))]

    def pack(c, _):
        for g in range(3):
            ends_k = [v_ref[rows8((side * 10 + c) * PL + g * 8), :] for side in range(2)]
            near = [jnp.where(even, y, rolled(y, 1, 0)) for y in ends_k]
            far = [jnp.where(even, rolled(y, -1, 0), y) for y in ends_k]
            for side, pair in enumerate((near, far)):
                for at in range(2):
                    low, high = (
                        jnp.take_along_axis(y, picks[side][at], axis=1, mode="promise_in_bounds")
                        for y in pair
                    )
                    row = ((side * 2 + at) * 10 + c) * PL + g * 8
                    plane = at if side == 0 else EDGE - 1 - at
                    pg_ref[rows8(row), :] = gk_ref[rows8(c * ROWS + plane * PL + g * 8), :]
                    pg_ref[rows8(row + 40 * PL), :] = jnp.where(early, low, high)
        return 0

    lax.fori_loop(0, 10, pack, 0)
    m = masks()
    inside = ~(m["j_first"] | m["j_last"])
    gone_j = m["j_first"] | m["j_last"] | m["j_penult"]
    for i in (0, EDGE - 1):
        acc_ref[pl.ds(i * PL, PL), :] = jnp.zeros((PL, LANES), jnp.float32)

    def column(g, _):
        g8 = g * 8
        start = state([jnp.full((8, LANES), y, jnp.float32) for y in (1.0, 0.0, 0.0, 0.0, 0.2)])
        for n in range(4):
            for q in range(7):
                pv_ref[pl.ds((n * 7 + q) * 8, 8), :] = start[q]
        aw_ref[...] = jnp.zeros_like(aw_ref)

        def plane(i, _):
            row = i * PL + g8

            def around(ref, c, first):
                at = c * ROWS + row
                return slopes_of(
                    ref[rows8(at - PL), :],
                    ref[rows8(at), :],
                    ref[rows8(at + PL), :],
                    None,
                    gk_ref[rows8((c + first) * ROWS + row), :],
                    m,
                )

            x = [prim_ref[rows8(c * ROWS + row), :] for c in range(5)]
            s = list(zip(*[around(prim_ref, c, 0) for c in range(5)]))
            ghost = [gk_ref[rows8(c * ROWS + row), :] for c in range(5)]
            solid = solid_ref[rows8(row), :]
            lower, upper = children(x, s)
            moments = Moments()
            within(moments, lower, upper, (0, 1, 2))

            before = [
                tuple(pv_ref[pl.ds((n * 7 + q) * 8, 8), :] for q in range(7)) for n in range(4)
            ]
            prior = row - PL
            wall_a = [pv_ref[pl.ds((28 + q) * 8, 8), :] for q in range(3)]
            wall_b = wall_sums(x[4], -s[0][4], s[1][4], s[2][4])
            sums = face_sums(before, lower[0], 0)
            sums = walled(sums, 0, solid_ref[rows8(prior), :], solid, wall_a, wall_b)
            used = jnp.where(i > 1, 1.0, 0.0)
            sums = [[used * y for y in part] for part in sums]
            moments.below(0, sums)
            old = [[aw_ref[pl.ds((q * 5 + c) * 8, 8), :] for c in range(5)] for q in range(3)]
            acc_ref[rows8(prior), :] = acc_ref[rows8(prior), :] + jnp.where(
                inside, weighed_sums(sums, *old), 0.0
            )
            for n in range(4):
                for q in range(7):
                    pv_ref[pl.ds((n * 7 + q) * 8, 8), :] = upper[0][n][q]
            for q, y in enumerate(wall_sums(x[4], s[0][4], s[1][4], s[2][4])):
                pv_ref[pl.ds((28 + q) * 8, 8), :] = y

            along(
                moments, 1, 1, lower, upper, x, s, solid,
                lambda y: next_j(y, m), lambda y: last_j(y, m), gone_j,
            )
            along(moments, 2, 2, lower, upper, x, s, solid, next_k, last_k, m["k_last"])
            ends(moments, 2, 2, x, s, ghost, m["k_first"], m["k_last"])

            a = [adj_ref[rows8(c * ROWS + row), :] for c in range(5)]
            t = list(zip(*[around(adj_ref, c, 5) for c in range(5)]))
            acc_ref[rows8(row), :] = jnp.where(inside, moments.weighed(a, t), 0.0)
            for c in range(5):
                aw_ref[pl.ds(c * 8, 8), :] = a[c] + t[0][c]
                aw_ref[pl.ds((5 + c) * 8, 8), :] = t[1][c]
                aw_ref[pl.ds((10 + c) * 8, 8), :] = t[2][c]
            return 0

        for q in range(3):
            pv_ref[pl.ds((28 + q) * 8, 8), :] = jnp.zeros((8, LANES), jnp.float32)
        lax.fori_loop(1, EDGE - 1, plane, 0, unroll=2)
        return 0

    lax.fori_loop(0, 3, column, 0)


def rim_kernel(
    index_ref, got_ref, px_ref, pg_ref, ps_ref, solid_ref, acc_ref, out_ref,
    gl_ref, tg_ref, pm_ref, total_ref,
):
    columns = one_hot(index_ref[pl.ds(144, FACES), :], 4 * PEERS)
    parts = fetched(
        columns,
        [
            jnp.concatenate(
                [got_ref[pl.ds(c * 4 + q, PEERS, stride=40), :] for q in range(4)], axis=0
            )
            for c in range(10)
        ],
    )
    for c in range(10):
        y = widened(parts[c], index_ref[pl.ds(0, FACES), :])
        for f in range(4):
            gl_ref[pl.ds((f * 10 + c) * PL, PL), :] = y[f * PL : (f + 1) * PL]

    for c in range(10):
        for g in range(3):
            low, high = (gl_ref[rows8((f * 10 + c) * PL + g * 8), :] for f in (2, 3))
            for at, i in enumerate((0, 1, EDGE - 1, EDGE - 2)):
                tg_ref[rows8((at * 10 + c) * PL + g * 8), :] = spread_j(low, high, i)
    m = masks()

    def boundary(n):
        axes = (n, 1 - n, 2)

        def one(at, _):
            side, g8 = at // 3, at % 3 * 8
            flip = jnp.where(side == 0, 1.0, -1.0)

            def load(ref, first):
                out = []
                for c in range(10):
                    y = ref[rows8((first + c) * PL + g8), :]
                    out.append(flip * y if c % 5 == n + 1 else y)
                return out

            place = n * 2 + side
            x = [load(px_ref, (place * 3 + depth) * 10) for depth in range(3)]
            outer = load(gl_ref, place * 10)
            gk = [load(pg_ref, (place * 2 + depth) * 10) for depth in range(2)]
            if n == 0:
                gt = [load(tg_ref, (side * 2 + depth) * 10) for depth in range(2)]
            else:
                gt = [[None] * 10] * 2
            solid = [ps_ref[rows8((place * 2 + depth) * PL + g8), :] for depth in range(2)]
            s0 = list(
                zip(*[slopes_of(outer[c], x[0][c], x[1][c], gt[0][c], gk[0][c], m) for c in range(10)])
            )
            s1 = list(
                zip(*[slopes_of(x[0][c], x[1][c], x[2][c], gt[1][c], gk[1][c], m) for c in range(10)])
            )
            flow, adj = x[0][:5], x[0][5:]
            s, t = [y[:5] for y in s0], [y[5:] for y in s0]
            lower, upper = children(flow, s)
            moments = Moments()
            within(moments, lower, upper, axes)
            moments.below(0, face_sums([state(outer[:5])] * 4, lower[0], n))

            flow1, adj1 = x[1][:5], x[1][5:]
            f1, t1 = [y[:5] for y in s1], [y[5:] for y in s1]
            sums = face_sums(
                upper[0], four([a - b for a, b in zip(flow1, f1[0])], f1[1], f1[2]), n
            )
            sums = walled(
                sums,
                n,
                solid[0],
                solid[1],
                wall_sums(flow[4], s[0][4], s[1][4], s[2][4]),
                wall_sums(flow1[4], -f1[0][4], f1[1][4], f1[2][4]),
            )
            moments.above(0, sums)
            next_total = -weighed_sums(
                sums, [a - b for a, b in zip(adj1, t1[0])], t1[1], t1[2]
            )

            gone = m["j_last"]
            if n == 1:
                gone = gone | m["j_first"] | m["j_penult"]
            along(
                moments, 1, axes[1], lower, upper, flow, s, solid[0],
                lambda y: next_j(y, m), lambda y: last_j(y, m), gone,
            )
            if n == 0:
                ends(moments, 1, axes[1], flow, s, gt[0][:5], m["j_first"], m["j_last"])
            along(moments, 2, 2, lower, upper, flow, s, solid[0], next_k, last_k, m["k_last"])
            ends(moments, 2, 2, flow, s, gk[0][:5], m["k_first"], m["k_last"])
            total = moments.weighed(adj, t)
            if n == 1:
                kept = ~(m["j_first"] | m["j_last"])
                total = jnp.where(kept, total, 0.0)
                next_total = jnp.where(kept, next_total, 0.0)
            pm_ref[rows8(place * 2 * PL + g8), :] = total
            pm_ref[rows8((place * 2 + 1) * PL + g8), :] = next_total
            return 0

        lax.fori_loop(0, 6, one, 0, unroll=2)

    boundary(0)
    boundary(1)

    low, even = lane() // EDGE, even_row()
    for g in range(3):
        planes = [[pm_ref[pl.ds((p * 2 + d) * PL + g * 8, 8), :] for d in range(2)] for p in range(4)]
        near = [planes[2], [rolled(y, -1, 0) for y in planes[2]]]
        far = [[rolled(y, 1, 0) for y in planes[3]], planes[3]]
        for i in range(EDGE):
            ih, il = i // 8, i % 8
            a, c = near[ih], far[ih]
            extra = jnp.where(
                even,
                jnp.where(
                    low == 0,
                    rolled(a[0], -16 * il),
                    jnp.where(low == 1, rolled(a[1], 16 - 16 * il), 0.0),
                ),
                jnp.where(
                    low == 7,
                    rolled(c[0], 112 - 16 * il),
                    jnp.where(low == 6, rolled(c[1], 96 - 16 * il), 0.0),
                ),
            )
            at = pl.ds(i * PL + g * 8, 8)
            total = acc_ref[at, :] + extra
            if i < 2:
                total = total + planes[0][i]
            elif i > EDGE - 3:
                total = total + planes[1][EDGE - 1 - i]
            total_ref[at, :] = jnp.where(solid_ref[at, :] > 0.5, 0.0, jnp.abs(total))
    for t in range(2 * EDGE):
        i, jh = divmod(t, 2)
        out_ref[:, pl.ds(t * LANES, LANES)] = total_ref[pl.ds(i * PL + jh, NB, stride=2), :]


def shape(*dims):
    return jax.ShapeDtypeStruct(dims, jnp.float32)


def scratch(*rows):
    return [pltpu.VMEM((r, LANES), jnp.float32) for r in rows]


SMEM = pl.BlockSpec(memory_space=pltpu.SMEM)
VMEM = pl.BlockSpec(memory_space=pltpu.VMEM)
PARAMS = pltpu.CompilerParams(vmem_limit_bytes=VMEM_LIMIT)


def prep(flow, adjoint, cut_flag, own, vertical):
    return pl.pallas_call(
        prep_kernel,
        out_shape=[
            shape(5 * ROWS, LANES),
            shape(5 * ROWS, LANES),
            shape(ROWS, LANES),
            shape(10 * FACES, LANES),
            shape(10 * PL, LANES),
            shape(10 * PL, LANES),
            jax.ShapeDtypeStruct((288, LANES), jnp.int32),
            shape(120 * PL, LANES),
            shape(8 * PL, LANES),
        ],
        in_specs=[VMEM] * 5,
        out_specs=[VMEM] * 9,
        cost_estimate=pl.CostEstimate(flops=10**8, bytes_accessed=3 * 10**7, transcendentals=0),
        compiler_params=PARAMS,
    )(flow.transpose(1, 0, 2), adjoint.transpose(1, 0, 2), cut_flag[None], own, vertical)


def reply(me, asked, layers):
    return pl.pallas_call(
        reply_kernel,
        out_shape=shape(40 * PEERS, LANES),
        in_specs=[SMEM, VMEM, VMEM],
        out_specs=VMEM,
        compiler_params=PARAMS,
    )(me, asked, layers)


def inner(edge, index, prim, adj, solid, low, high):
    return pl.pallas_call(
        inner_kernel,
        out_shape=[shape(ROWS, LANES), shape(80 * PL, LANES)],
        in_specs=[SMEM] + [VMEM] * 6,
        out_specs=[VMEM] * 2,
        scratch_shapes=scratch(20 * PL, 10 * ROWS, 31 * 8, 15 * 8),
        compiler_params=PARAMS,
    )(edge, index, prim, adj, solid, low, high)


def rim(index, got, planes, ghosts, walls, solid, acc):
    return pl.pallas_call(
        rim_kernel,
        out_shape=shape(NB, EDGE * EDGE * EDGE),
        in_specs=[VMEM] * 7,
        out_specs=VMEM,
        scratch_shapes=scratch(40 * PL, 40 * PL, 8 * PL, ROWS),
        compiler_params=PARAMS,
    )(index, got, planes, ghosts, walls, solid, acc)


def ask_kernel(owner_ref, link_ref, own_ref, out_ref):
    link = link_ref[...]
    slot = (link.astype(jnp.float32) * 0.2 + 0.05).astype(jnp.int32)
    far = lax.broadcasted_iota(jnp.int32, link.shape, 0) ^ 1
    own = (owner_ref[...] * 64 + slot * 4 + far) * 8 + (link - 5 * slot)
    own_ref[...] = own
    at = lax.broadcasted_iota(jnp.int32, (NB, LANES), 0)
    spot = lax.broadcasted_iota(jnp.int32, (NB, LANES), 1)
    row = jnp.full((1, LANES), -1.0, jnp.float32)
    for f in range(4):
        spread = jnp.dot(
            own[f : f + 1].astype(jnp.float32) + 1.0,
            jnp.where(spot == at + f * NB, 1.0, 0.0),
            precision=lax.Precision.HIGHEST,
            preferred_element_type=jnp.float32,
        )
        row = row + spread
    row = (row + jnp.where(row < 0.0, -0.25, 0.25)).astype(jnp.int32)
    out_ref[...] = jnp.broadcast_to(row, out_ref.shape)


def ask(lateral_owner, lateral_link):
    return pl.pallas_call(
        ask_kernel,
        out_shape=[
            jax.ShapeDtypeStruct((4, NB), jnp.int32),
            jax.ShapeDtypeStruct((PEERS, LANES), jnp.int32),
        ],
        in_specs=[VMEM] * 2,
        out_specs=[VMEM] * 2,
        compiler_params=PARAMS,
    )(lateral_owner[:, :, 0].T, lateral_link.T)


def exchange(block, axis):
    chunks = block.reshape(PEERS, -1, LANES)
    out = lax.all_to_all(chunks, axis, split_axis=0, concat_axis=0, tiled=True)
    return out.reshape(-1, LANES)


def local(flow, adjoint, cut_flag, lateral_owner, lateral_link, vertical_link):
    own, questions = ask(lateral_owner, lateral_link)
    asked = exchange(questions, "blk")
    prim, adj, solid, layers, low_face, high_face, index, planes, walls = prep(
        flow, adjoint, cut_flag, own, vertical_link.T
    )
    asked, low_face, high_face = lax.optimization_barrier((asked, low_face, high_face))
    regions = lax.axis_size("grp")
    region = lax.axis_index("grp")
    low = lax.ppermute(high_face, "grp", [(r, r + 1) for r in range(regions - 1)])
    high = lax.ppermute(low_face, "grp", [(r + 1, r) for r in range(regions - 1)])
    me = lax.axis_index("blk").astype(jnp.int32).reshape(1)
    replies = reply(me, asked, layers)
    got = exchange(replies, "blk")
    edge = region.astype(jnp.int32).reshape(1)
    acc, ghosts = inner(edge, index, prim, adj, solid, low, high)
    return rim(index, got, planes, ghosts, walls, solid, acc)


def solution(mesh):
    in_specs = (
        P(("blk", "grp"), None, None),
        P(("blk", "grp"), None, None),
        P(("blk", "grp"), None),
        P(("blk", "grp"), None, None),
        P(("blk", "grp"), None),
        P(("blk", "grp"), None),
    )
    out_specs = P(("blk", "grp"), None)
    return jax.shard_map(local, mesh=mesh, in_specs=in_specs, out_specs=out_specs, check_vma=False)
```
